128 devices in a mesh: group: 4 (over z), dom: 32 (over x, y, core).
Axes of the slice: x: 4, y: 4, z: 4, core: 2. Of those that a mesh axis runs over, the one named last changes fastest.
Arguments:
- positions: float32 [4, 3, 262144], P('group', None, 'dom'), as said below
- velocity: float32 [4, 3, 262144], P('group', None, 'dom'), may hold values from -6 to 6
- mass: float32 [4, 262144], P('group', 'dom'), may hold values from 0.5 to 2
- stress: float32 [4, 3, 262144], P('group', None, 'dom'), may hold values from -6 to 6
- corner_block: int32 [4, 4, 2048], P('group', None, 'dom'), may hold values from 0 to 64, as said below
- corner_slot: int32 [4, 4, 262144], P('group', None, 'dom'), may hold values from 0 to 127, as said below
- halo_block: int32 [4, 32], P('group', 'dom'), may hold values from 0 to 63
- contact_owner: int32 [4, 2048], P('group', 'dom'), may hold values from -1 to 127, as said below
- contact_slot: int32 [4, 2048], P('group', 'dom'), may hold values from -1 to 31, as said below
- tile_pairs: int32 [4, 2, 768], P('group', None, 'dom'), may hold values from 0 to 31, as said below
- tile_active: int32 [4, 768], P('group', 'dom'), may hold values from 0 to 1
Outputs:
- velocity_next: float32 [4, 3, 262144], P('group', None, 'dom')
- stress_next: float32 [4, 3, 262144], P('group', None, 'dom')
The draws below stay inside these ranges and needn't reach their ends.
Inputs may be any that keep to these rules, and one draw needn't show every extreme that they name: `positions`: every element is a quadrilateral whose normal diag_a x diag_b has length 0.1 or more and whose vector diag_a - diag_b keeps a length of 0.5 or more off that normal. `corner_block`: in every element block corners 0 and 3 name one node block and corners 1 and 2 another; the value 64 names the shared block of the next partition (cyclic), given by halo_block. `corner_slot`: for each corner, the 128 elements of an element block name 128 different slots. `contact_owner`: -1 marks a node block without contact. Otherwise, for a block of the partition with dom index d, the owner's dom index (owner mod 32) is d - 1, d or d + 1, cyclic; at most 8 blocks of one partition go to one owner. `contact_slot`: -1 exactly where contact_owner is -1. Otherwise slot // 8 is the block's layer index, and no two blocks share an owner and a slot. `tile_pairs`: both slots of a tile with flag 1 hold a block at that owner.
All inputs are finite; a program needn't handle non-finite values.
Results may differ from the reference program's by a relative error of at most 0.0003.
Values sent between devices are 32-bit elements; how exact they have to be, the bound alone decides.
A program may use at most 64 MiB of HBM per device.

```python
import math
import jax
import jax.numpy as jnp
from jax import lax

BLOCKS_DEV = 64
CYCLE = 128
MOST = 8
GROUPS = 4
DOMS = 32
SLOTS = 32
TILES_OWN = 24
BLOCKS = 2048
NODES = 262144
ELEMS = 262144
TILES = 768


def layout(key):
    columns = DOMS * BLOCKS_DEV
    key_list = jax.random.split(key, 12)
    column_store = jax.vmap(lambda subkey: jax.random.permutation(subkey, BLOCKS_DEV))(jax.random.split(key_list[0], GROUPS * DOMS))
    column_store = column_store.astype(jnp.int32)
    top_row = jax.random.randint(key_list[11], (), 0, GROUPS * DOMS)
    low_row = (top_row + 1) % (GROUPS * DOMS)
    store_pos = jnp.arange(BLOCKS_DEV)[None, :]
    row_ids = jnp.arange(GROUPS * DOMS)[:, None]
    wanted = jnp.where(row_ids == top_row, BLOCKS_DEV - 1, 0)
    where_wanted = jnp.sum(jnp.where(column_store == wanted, store_pos, 0), 1, keepdims=True)
    first_value = column_store[:, :1]
    swapped = jnp.where(store_pos == 0, wanted, jnp.where(store_pos == where_wanted, first_value, column_store))
    pick_rows = (row_ids == top_row) | (row_ids == low_row)
    column_store = jnp.where(pick_rows, swapped, column_store)
    column_store = column_store.reshape(GROUPS, DOMS, BLOCKS_DEV).astype(jnp.int32)
    cycle_rows = jax.vmap(lambda subkey: jax.random.permutation(subkey, CYCLE))(jax.random.split(key_list[1], GROUPS * columns))
    cycle_rows = cycle_rows.reshape(GROUPS, columns, CYCLE).astype(jnp.int32)
    layer_turns = 4 * jax.random.randint(key_list[2], (GROUPS,), 0, MOST)
    layer_turns = jnp.where(jnp.arange(GROUPS) == 0, columns - 8, layer_turns)
    run_pick = jax.random.randint(key_list[3], (columns // 8,), 0, 8)
    shifts = 8 * jax.random.randint(key_list[4], (DOMS,), 0, MOST // 3 + 1)
    forced_dom = jax.random.randint(key_list[5], (), 0, DOMS)
    forced_box = jax.random.randint(key_list[6], (), 0, GROUPS)
    shifts = jnp.where((jnp.arange(DOMS) == forced_dom) | (jnp.arange(DOMS) == 0), 0, shifts)
    slab_cuts = jnp.arange(DOMS) * BLOCKS_DEV + shifts
    cut_ends = jnp.concatenate([slab_cuts[1:], slab_cuts[:1] + columns])
    remain = 3 * ((cut_ends - slab_cuts) // 8)
    forced = (jnp.arange(DOMS)[:, None] == forced_dom) & (jnp.arange(GROUPS)[None, :] == forced_box)
    corner_cell = (jnp.arange(DOMS)[:, None] == DOMS - 1) & (jnp.arange(GROUPS)[None, :] == GROUPS - 1)
    needed = jnp.where(forced, MOST, jnp.where(corner_cell, 1, 0))
    part_keys = jax.random.split(key_list[7], GROUPS)
    lengths = []
    for box_index in range(GROUPS):
        after_count = GROUPS - 1 - box_index
        needed_after = jnp.sum(needed[:, box_index + 1:], 1)
        lower_bound = jnp.maximum(needed[:, box_index], remain - after_count * MOST)
        upper_bound = jnp.minimum(MOST, remain - needed_after)
        raw_draw = jax.random.randint(part_keys[box_index], (DOMS,), 0, 1 << 20)
        picked = lower_bound + raw_draw % (upper_bound - lower_bound + 1)
        lengths.append(picked)
        remain = remain - picked
    lengths = jnp.stack(lengths, 1)
    box_end = jnp.cumsum(lengths, 1)
    box_start = box_end - lengths
    places = jnp.arange(columns)
    run_rank = (places % 8 - jnp.repeat(run_pick, 8)) % 8
    in_contact = run_rank < 3
    unrolled = jnp.where(places < slab_cuts[0], places + columns, places)
    slab_index = jnp.sum((slab_cuts[None, :] <= unrolled[:, None]).astype(jnp.int32), 1) - 1
    within = (unrolled - slab_cuts[slab_index]) // 8 * 3 + jnp.minimum(run_rank, 2)
    box_at = jnp.sum((box_end[slab_index] <= within[:, None]).astype(jnp.int32), 1)
    box_at = jnp.minimum(box_at, GROUPS - 1)
    offset_at = within - jnp.take_along_axis(box_start[slab_index], box_at[:, None], 1)[:, 0]
    owner_at = jnp.where(in_contact, box_at * DOMS + slab_index, -1)
    offset_at = jnp.where(in_contact, offset_at, -1)
    store_to_column = jnp.argsort(column_store, axis=-1).astype(jnp.int32)
    block_column = (jnp.arange(DOMS)[None, :, None] * BLOCKS_DEV + store_to_column).reshape(GROUPS, BLOCKS)
    block_phase = (block_column + layer_turns[:, None]) % columns
    block_owner = owner_at[block_phase].astype(jnp.int32)
    block_slot = jnp.where(block_owner >= 0, jnp.arange(GROUPS)[:, None] * MOST + offset_at[block_phase], -1).astype(jnp.int32)
    row_index = jnp.arange(TILES_OWN)
    layer_index = row_index // MOST
    spot_index = row_index % MOST
    live_length = jnp.transpose(lengths)
    is_live = spot_index[None, None, :] < live_length[:, :, None]
    near_slot = layer_index * MOST + spot_index
    filler = jax.random.randint(key_list[8], (2, GROUPS, DOMS, TILES_OWN), 0, SLOTS)
    first_slot = jnp.where(is_live, near_slot[None, None, :], filler[0])
    second_slot = jnp.where(is_live, near_slot[None, None, :] + MOST, filler[1])
    flag_draw = jax.random.randint(key_list[9], (GROUPS, DOMS, TILES_OWN), 0, 4)
    tile_flags = jnp.where(is_live & ((flag_draw > 0) | (layer_index[None, None, :] == 0)), 1, 0)
    row_order = jax.vmap(lambda subkey: jax.random.permutation(subkey, TILES_OWN))(jax.random.split(key_list[10], GROUPS * DOMS))
    row_order = row_order.reshape(GROUPS, DOMS, TILES_OWN)
    first_slot = jnp.take_along_axis(first_slot, row_order, 2)
    second_slot = jnp.take_along_axis(second_slot, row_order, 2)
    tile_flags = jnp.take_along_axis(tile_flags, row_order, 2)
    pair_table = jnp.stack([first_slot, second_slot], 1).reshape(GROUPS, 2, TILES).astype(jnp.int32)
    return {'column_store': column_store, 'cycle_rows': cycle_rows, 'block_column': block_column, 'block_phase': block_phase, 'block_owner': block_owner, 'block_slot': block_slot, 'pair_table': pair_table, 'tile_flags': tile_flags.reshape(GROUPS, TILES).astype(jnp.int32)}


def draw_positions(key, part):
    layout_plan = layout(key)
    key = jax.random.fold_in(key, 11)
    columns = DOMS * BLOCKS_DEV
    layer_ids = jnp.arange(GROUPS)[:, None]
    cycle_row = layout_plan['cycle_rows'][layer_ids, layout_plan['block_column']]
    phase_index = layout_plan['block_phase'].astype(jnp.float32)
    beside_all = 2.0 * math.pi / columns * phase_index[:, :, None]
    circle = 2.0 * math.pi / CYCLE * cycle_row.astype(jnp.float32)
    tube_radius = CYCLE / (2.0 * math.pi) + 0.6 * jnp.arange(GROUPS, dtype=jnp.float32)[:, None, None]
    major_radius = (columns + 2.0 * CYCLE) / (2.0 * math.pi)
    radial = major_radius + tube_radius * jnp.cos(circle)
    coords = jnp.stack([radial * jnp.cos(beside_all), radial * jnp.sin(beside_all), tube_radius * jnp.sin(circle)], 1)
    jitter = jax.random.uniform(key, coords.shape, jnp.float32, minval=-0.12, maxval=0.12)
    return (coords + jitter).reshape(GROUPS, 3, NODES).astype(jnp.float32)


def draw_corner_block(key, part):
    layout_plan = layout(key)
    column_store = layout_plan['column_store']
    shifted = jnp.concatenate([column_store[:, :, 1:], jnp.full((GROUPS, DOMS, 1), BLOCKS_DEV, jnp.int32)], 2)
    return jnp.stack([column_store, shifted, shifted, column_store], 1).reshape(GROUPS, 4, BLOCKS).astype(jnp.int32)


def draw_corner_slot(key, part):
    layout_plan = layout(key)
    columns = DOMS * BLOCKS_DEV
    cycle_slot = jnp.argsort(layout_plan['cycle_rows'], axis=-1).astype(jnp.int32)
    next_row = jnp.roll(cycle_slot, -1, axis=2)
    layer_ids = jnp.arange(GROUPS)[:, None]
    column_here = jnp.arange(columns)[None, :]
    column_after = (column_here + 1) % columns
    corner_zero = cycle_slot[layer_ids, column_here]
    corner_one = cycle_slot[layer_ids, column_after]
    corner_two = next_row[layer_ids, column_after]
    corner_three = next_row[layer_ids, column_here]
    return jnp.stack([corner_zero, corner_one, corner_two, corner_three], 1).reshape(GROUPS, 4, ELEMS).astype(jnp.int32)


def draw_halo_block(key, part):
    layout_plan = layout(key)
    return layout_plan['column_store'][:, :, 0].astype(jnp.int32)


def draw_contact_owner(key, part):
    layout_plan = layout(key)
    return layout_plan['block_owner']


def draw_contact_slot(key, part):
    layout_plan = layout(key)
    return layout_plan['block_slot']


def draw_tile_pairs(key, part):
    layout_plan = layout(key)
    return layout_plan['pair_table']


def draw_tile_active(key, part):
    layout_plan = layout(key)
    return layout_plan['tile_flags']


def levels(rng, shape, cuts, low, top_value):
    gain = 1.0
    for position, shards_of in cuts:
        steps = jax.random.uniform(jax.random.fold_in(jax.random.fold_in(rng, 6), position), (shards_of,), jnp.float32, low / len(cuts), top_value / len(cuts))
        gain = gain * jnp.repeat(jnp.exp(steps), shape[position] // shards_of).reshape((-1,) + (1,) * (len(shape) - 1 - position))
    return gain


def normal_values(stream_key, shape, width, reach, cuts=(), kind=jnp.bfloat16):
    drawn = width * jax.random.normal(stream_key, shape, jnp.float32)
    if cuts:
        drawn = drawn * levels(stream_key, shape, cuts, -0.22, 0.18)
    return jnp.clip(drawn, -reach, reach).astype(kind)


def setup_inputs(seed: int = 0) -> dict:
    arg_keys = jax.random.split(jax.random.key(seed), 12)
    positions = draw_positions(jax.random.fold_in(arg_keys[11], 71), 0)
    velocity = normal_values(arg_keys[1], (GROUPS, 3, NODES), 1.0, 6.0, ((0, 4), (2, 32)), jnp.float32)
    mass = jnp.clip(jnp.exp(math.log(2.0) - 1.3862944 * jax.random.uniform(arg_keys[2], (GROUPS, NODES), jnp.float32) ** levels(arg_keys[2], (GROUPS, NODES), ((0, 4), (1, 32)), -0.2, 0.2)), 0.5, 2.0)
    stress = normal_values(arg_keys[3], (GROUPS, 3, ELEMS), 1.0, 6.0, ((0, 4), (2, 32)), jnp.float32)
    corner_block = draw_corner_block(jax.random.fold_in(arg_keys[11], 71), 0)
    corner_slot = draw_corner_slot(jax.random.fold_in(arg_keys[11], 71), 0)
    halo_block = draw_halo_block(jax.random.fold_in(arg_keys[11], 71), 0)
    contact_owner = draw_contact_owner(jax.random.fold_in(arg_keys[11], 71), 0)
    contact_slot = draw_contact_slot(jax.random.fold_in(arg_keys[11], 71), 0)
    tile_pairs = draw_tile_pairs(jax.random.fold_in(arg_keys[11], 71), 0)
    tile_active = draw_tile_active(jax.random.fold_in(arg_keys[11], 71), 0)
    return {"positions": positions, "velocity": velocity, "mass": mass, "stress": stress, "corner_block": corner_block, "corner_slot": corner_slot, "halo_block": halo_block, "contact_owner": contact_owner, "contact_slot": contact_slot, "tile_pairs": tile_pairs, "tile_active": tile_active}


DT = 0.5
STIFF = 2.0
POISSON = 0.3
HOURGLASS = 0.1
PENALTY = 4.0
REACH = 1.0

def inner_rows(first_vec, second_vec):
    return first_vec[0] * second_vec[0] + first_vec[1] * second_vec[1] + first_vec[2] * second_vec[2]

def cross_rows(first_vec, second_vec):
    return jnp.stack([first_vec[1] * second_vec[2] - first_vec[2] * second_vec[1], first_vec[2] * second_vec[0] - first_vec[0] * second_vec[2], first_vec[0] * second_vec[1] - first_vec[1] * second_vec[0]])

def shell_forces(corner_pos, corner_vel, stress_old):
    diag_a = corner_pos[2] - corner_pos[0]
    diag_b = corner_pos[3] - corner_pos[1]
    normal = cross_rows(diag_a, diag_b)
    jacobian = jnp.sqrt(inner_rows(normal, normal))
    axis_three = normal / jacobian
    tangent = diag_a - diag_b
    tangent = tangent - inner_rows(tangent, axis_three) * axis_three
    axis_one = tangent / jnp.sqrt(inner_rows(tangent, tangent))
    axis_two = cross_rows(axis_three, axis_one)
    along_a = inner_rows(diag_a, axis_one)
    across_a = inner_rows(diag_a, axis_two)
    along_b = inner_rows(diag_b, axis_one)
    across_b = inner_rows(diag_b, axis_two)
    speed_a = corner_vel[2] - corner_vel[0]
    speed_b = corner_vel[3] - corner_vel[1]
    slide_a = inner_rows(speed_a, axis_one)
    lift_a = inner_rows(speed_a, axis_two)
    slide_b = inner_rows(speed_b, axis_one)
    lift_b = inner_rows(speed_b, axis_two)
    rate_xx = (across_b * slide_a - across_a * slide_b) / jacobian
    rate_yy = (along_a * lift_b - along_b * lift_a) / jacobian
    rate_xy = (across_b * lift_a - across_a * lift_b + along_a * slide_b - along_b * slide_a) / jacobian
    stress_xx = stress_old[0] + DT * STIFF * (rate_xx + POISSON * rate_yy)
    stress_yy = stress_old[1] + DT * STIFF * (POISSON * rate_xx + rate_yy)
    stress_xy = stress_old[2] + DT * STIFF * (0.5 * (1.0 - POISSON)) * rate_xy
    grad_x = (-across_b, across_a, across_b, -across_a)
    grad_y = (along_b, -along_a, -along_b, along_a)
    mode_signs = (1.0, -1.0, 1.0, -1.0)
    twist_mode = corner_vel[0] - corner_vel[1] + corner_vel[2] - corner_vel[3]
    results = []
    for corner_index in range(4):
        force_x = 0.5 * (grad_x[corner_index] * stress_xx + grad_y[corner_index] * stress_xy)
        force_y = 0.5 * (grad_x[corner_index] * stress_xy + grad_y[corner_index] * stress_yy)
        results.append(force_x * axis_one + force_y * axis_two + HOURGLASS * mode_signs[corner_index] * twist_mode)
    return (jnp.stack(results), jnp.stack([stress_xx, stress_yy, stress_xy]))

def owner_tiles(owner_args):
    slots_here, pair_rows, flag_rows = owner_args

    def one_tile(totals, tile_args):
        near_index, far_index, flag_value = tile_args
        near_side = slots_here[near_index]
        far_side = slots_here[far_index]
        offsets = near_side[:, :, None] - far_side[:, None, :]
        distance = lax.optimization_barrier(jnp.sum(offsets * offsets, 0))
        weight = PENALTY * flag_value.astype(jnp.float32) * jnp.maximum(REACH - distance, 0.0)
        push_force = weight[None] * offsets
        totals = totals.at[near_index].add(lax.optimization_barrier(jnp.sum(push_force, 2)))
        totals = totals.at[far_index].add(-lax.optimization_barrier(jnp.sum(push_force, 1)))
        return (totals, None)
    totals, unused = lax.scan(one_tile, jnp.zeros_like(slots_here), (pair_rows[0], pair_rows[1], flag_rows))
    return totals

def reference(positions, velocity, mass, stress, corner_block, corner_slot, halo_block, contact_owner, contact_slot, tile_pairs, tile_active):
    partition = jnp.arange(BLOCKS, dtype=jnp.int32) // BLOCKS_DEV
    following = (partition + 1) % DOMS

    def one_layer(layer_args):
        layer_pos, layer_vel, layer_stress, layer_blocks, layer_slots, layer_halo = layer_args
        node_block = jnp.where(layer_blocks < BLOCKS_DEV, partition * BLOCKS_DEV + layer_blocks, following * BLOCKS_DEV + layer_halo[following])
        corner_node = jnp.repeat(node_block, CYCLE, axis=1) * CYCLE + layer_slots
        node_state = jnp.concatenate([layer_pos, layer_vel], 0)
        corner = jnp.transpose(node_state[:, corner_node], (1, 0, 2))
        forces, stress_new = shell_forces(corner[:, :3], corner[:, 3:], layer_stress)
        internal = jnp.zeros_like(layer_pos)
        for corner_index in range(4):
            internal = internal.at[:, corner_node[corner_index]].add(forces[corner_index])
        return (internal, stress_new)
    internal, stress_next = lax.map(one_layer, (positions, velocity, stress, corner_block, corner_slot, halo_block))
    owners_all = GROUPS * DOMS
    block_pos = jnp.transpose(positions.reshape(GROUPS, 3, BLOCKS, CYCLE), (0, 2, 1, 3)).reshape(GROUPS * BLOCKS, 3, CYCLE)
    owner_flat = contact_owner.reshape(-1)
    slot_flat = contact_slot.reshape(-1)
    is_live = owner_flat >= 0
    target = jnp.where(is_live, owner_flat * SLOTS + slot_flat, owners_all * SLOTS)
    canonical = jnp.zeros((owners_all * SLOTS, 3, CYCLE), jnp.float32).at[target].set(block_pos, mode='drop')
    pair_rows = jnp.transpose(tile_pairs.reshape(GROUPS, 2, DOMS, TILES_OWN), (0, 2, 1, 3)).reshape(owners_all, 2, TILES_OWN)
    flag_rows = tile_active.reshape(owners_all, TILES_OWN)
    owner_force = lax.map(owner_tiles, (canonical.reshape(owners_all, SLOTS, 3, CYCLE), pair_rows, flag_rows))
    gathered = owner_force.reshape(owners_all * SLOTS, 3, CYCLE)[jnp.minimum(target, owners_all * SLOTS - 1)]
    gathered = jnp.where(is_live[:, None, None], gathered, 0.0)
    contact = jnp.transpose(gathered.reshape(GROUPS, BLOCKS, 3, CYCLE), (0, 2, 1, 3)).reshape(GROUPS, 3, NODES)
    velocity_next = velocity + DT * (contact - internal) / mass[:, None, :]
    return (velocity_next, stress_next)
```

```python
import functools

import jax
import jax.numpy as jnp
from jax import lax
from jax.experimental import pallas as pl
from jax.experimental.pallas import tpu as pltpu
from jax.sharding import PartitionSpec as P

LANES = 128
ROWS = 8
DT = 0.5
STIFF = 2.0
POISSON = 0.3
HOURGLASS = 0.1
PENALTY = 4.0
REACH = 1.0
MESH = pl.DeviceIdType.MESH
HIGHEST = lax.Precision.HIGHEST


def inner_rows(a, b):
    return a[0] * b[0] + a[1] * b[1] + a[2] * b[2]


def cross_rows(a, b):
    return (
        a[1] * b[2] - a[2] * b[1],
        a[2] * b[0] - a[0] * b[2],
        a[0] * b[1] - a[1] * b[0],
    )


def minus(a, b):
    return tuple(x - y for x, y in zip(a, b))


def scaled(a, s):
    return tuple(x * s for x in a)


def shell_forces(pos, vel, stress_old):
    diag_a = minus(pos[2], pos[0])
    diag_b = minus(pos[3], pos[1])
    normal = cross_rows(diag_a, diag_b)
    inv_j = lax.rsqrt(inner_rows(normal, normal))
    axis_three = scaled(normal, inv_j)
    tangent = minus(diag_a, diag_b)
    tangent = minus(tangent, scaled(axis_three, inner_rows(tangent, axis_three)))
    axis_one = scaled(tangent, lax.rsqrt(inner_rows(tangent, tangent)))
    axis_two = cross_rows(axis_three, axis_one)
    along_a = inner_rows(diag_a, axis_one)
    across_a = inner_rows(diag_a, axis_two)
    along_b = inner_rows(diag_b, axis_one)
    across_b = inner_rows(diag_b, axis_two)
    speed_a = minus(vel[2], vel[0])
    speed_b = minus(vel[3], vel[1])
    slide_a = inner_rows(speed_a, axis_one)
    lift_a = inner_rows(speed_a, axis_two)
    slide_b = inner_rows(speed_b, axis_one)
    lift_b = inner_rows(speed_b, axis_two)
    rate_xx = (across_b * slide_a - across_a * slide_b) * inv_j
    rate_yy = (along_a * lift_b - along_b * lift_a) * inv_j
    rate_xy = (
        across_b * lift_a - across_a * lift_b + along_a * slide_b - along_b * slide_a
    ) * inv_j
    s_xx = stress_old[0] + (DT * STIFF) * (rate_xx + POISSON * rate_yy)
    s_yy = stress_old[1] + (DT * STIFF) * (POISSON * rate_xx + rate_yy)
    s_xy = stress_old[2] + (DT * STIFF * 0.5 * (1.0 - POISSON)) * rate_xy
    half_xx, half_yy, half_xy = 0.5 * s_xx, 0.5 * s_yy, 0.5 * s_xy
    fx0 = along_b * half_xy - across_b * half_xx
    fy0 = along_b * half_yy - across_b * half_xy
    fx1 = across_a * half_xx - along_a * half_xy
    fy1 = across_a * half_xy - along_a * half_yy
    forces = [[], [], [], []]
    for c in range(3):
        mode = HOURGLASS * (vel[0][c] - vel[1][c] + vel[2][c] - vel[3][c])
        first = fx0 * axis_one[c] + fy0 * axis_two[c]
        second = fx1 * axis_one[c] + fy1 * axis_two[c]
        forces[0].append(mode + first)
        forces[1].append(second - mode)
        forces[2].append(mode - first)
        forces[3].append(-mode - second)
    return forces, (s_xx, s_yy, s_xy)


def kernel(
    groups,
    doms,
    pos_ref,
    vel_ref,
    mass_ref,
    stress_ref,
    slot_ref,
    cb_ref,
    owner_ref,
    spot_ref,
    pair_ref,
    cb_smem,
    halo_smem,
    pair_smem,
    active_smem,
    vel_out,
    stress_out,
    state,
    rim,
    ghost_in,
    out_buf,
    in_buf,
    ans,
    ret,
    canon,
    tile_out,
    inverse,
    corner_buf,
    force_buf,
    spread,
    push_out,
    push_in,
    fwd_send,
    fwd_recv,
    back_send,
    back_recv,
    rim_sems,
    push_sems,
):
    g = lax.axis_index("group")
    d = lax.axis_index("dom")
    blocks = mass_ref.shape[0]
    tiles = pair_ref.shape[1]
    slots = groups * ROWS
    left = lax.rem(d + doms - 1, doms)
    right = lax.rem(d + 1, doms)
    partners = []
    for turn in range(groups):
        k = lax.rem(g + turn, groups)
        for step, dd in ((0, left), (1, d), (2, right)):
            if turn == 0 and step == 1:
                continue
            partners.append((turn, k, step, dd))

    barrier = pltpu.get_barrier_semaphore()
    for turn, k, step, dd in partners:
        pl.semaphore_signal(barrier, inc=1, device_id=(k, dd), device_id_type=MESH)

    halo = halo_smem[0, 0]
    state_rows = state.reshape((blocks + 1) * ROWS, LANES)
    for c in range(3):
        state_rows[pl.ds(c, blocks, stride=ROWS), :] = pos_ref[c]
        state_rows[pl.ds(3 + c, blocks, stride=ROWS), :] = vel_ref[c]
    rim[...] = state[halo]

    owner = owner_ref[...]
    step_of = lax.rem(lax.rem(owner, doms) - d + 1 + doms, doms)
    goal = (lax.div(owner, doms) * 3 + step_of) * ROWS + lax.rem(spot_ref[...], ROWS)
    goal = jnp.where(owner >= 0, goal, -1)
    places = groups * 3 * ROWS
    chosen = (
        lax.broadcasted_iota(jnp.int32, (places, blocks), 0) == goal
    ).astype(jnp.float32)
    for c in range(3):
        column = pos_ref[c]
        packed = jnp.dot(chosen, column, precision=HIGHEST, preferred_element_type=jnp.float32)
        out_buf[:, :, c, :, :] = packed.reshape(groups, 3, ROWS, LANES)

    pl.semaphore_wait(barrier, len(partners))

    rim_copy = pltpu.make_async_remote_copy(
        src_ref=rim,
        dst_ref=ghost_in,
        send_sem=rim_sems.at[0],
        recv_sem=rim_sems.at[1],
        device_id=(g, left),
        device_id_type=MESH,
    )
    rim_copy.start()
    forward = []
    for turn, k, step, dd in partners:
        copy = pltpu.make_async_remote_copy(
            src_ref=out_buf.at[k, step],
            dst_ref=in_buf.at[step, g],
            send_sem=fwd_send.at[turn, step],
            recv_sem=fwd_recv.at[turn, step],
            device_id=(k, dd),
            device_id_type=MESH,
        )
        copy.start()
        forward.append(copy)
    in_buf[1, g] = out_buf[g, 1]

    lane16 = lax.broadcasted_iota(jnp.int32, (16, 2 * LANES), 1)
    row16 = lax.broadcasted_iota(jnp.int32, (16, 2 * LANES), 0)
    half = lax.div(lane16, LANES)
    weights = jnp.where(lax.rem(lax.div(row16, 4), 2) == half, lax.rem(lane16, LANES), 0)
    weights = weights.astype(jnp.float32).astype(jnp.bfloat16)
    rows_of = lax.broadcasted_iota(jnp.int32, (16, LANES), 0)
    one = jnp.ones((16, LANES), jnp.bfloat16)
    zero = jnp.zeros((16, LANES), jnp.bfloat16)

    def invert(k, carry):
        ids = slot_ref[:, pl.ds(pl.multiple_of(k * LANES, LANES), LANES)].astype(jnp.float32)
        level = [
            (rows_of + 16 * j).astype(jnp.float32).astype(jnp.bfloat16) for j in range(ROWS)
        ]
        marks = []
        for c in range(4):
            here = jnp.broadcast_to(ids[c : c + 1, :], (16, LANES)).astype(jnp.bfloat16)
            marks.append(
                jnp.concatenate([jnp.where(here == lv, one, zero) for lv in level], 0)
            )
        for side, (first, second) in enumerate(((0, 3), (1, 2))):
            both = jnp.concatenate([marks[first], marks[second]], 1)
            found = lax.dot_general(
                weights, both, (((1,), (1,)), ((), ())), preferred_element_type=jnp.float32
            )
            inverse[side, k] = found[0:ROWS, :].astype(jnp.int32)
        return carry

    lax.fori_loop(0, blocks, invert, 0, unroll=2)

    for copy in forward:
        copy.wait_recv()
    canon_rows = canon.reshape(slots * ROWS, LANES)
    for c in range(3):
        for layer in range(groups):
            canon_rows[pl.ds(layer * ROWS * ROWS + c, ROWS, stride=ROWS), :] = (
                in_buf[0, layer, c] + in_buf[1, layer, c] + in_buf[2, layer, c]
            )
    sub_iota = lax.broadcasted_iota(jnp.int32, (ROWS, LANES), 0)
    lane_iota = lax.broadcasted_iota(jnp.int32, (ROWS, LANES), 1)

    def one_tile(t, carry):
        i = pair_smem[0, t]
        j = pair_smem[1, t]
        gain = PENALTY * active_smem[0, t].astype(jnp.float32)
        near_block = canon[i]
        far_block = canon[j]
        near = [jnp.broadcast_to(near_block[c : c + 1, :], (ROWS, LANES)) for c in range(3)]
        far = [jnp.broadcast_to(far_block[c : c + 1, :], (ROWS, LANES)) for c in range(3)]
        near_sum = [jnp.zeros((ROWS, LANES), jnp.float32) for _ in range(3)]
        far_sum = [jnp.zeros((ROWS, LANES), jnp.float32) for _ in range(3)]
        for r in range(LANES // ROWS):
            at = sub_iota + ROWS * r
            diff = [
                jnp.take_along_axis(near[c], at, axis=1, mode="promise_in_bounds") - far[c]
                for c in range(3)
            ]
            weight = gain * jnp.maximum(REACH - inner_rows(diff, diff), 0.0)
            for c in range(3):
                push = weight * diff[c]
                far_sum[c] = far_sum[c] + push
                total = jnp.sum(push, 1, keepdims=True)
                near_sum[c] = jnp.where(lane_iota == at, total, near_sum[c])
        for c in range(3):
            tile_out[c, pl.ds(t, 1), :] = jnp.sum(
                jnp.where(lax.rem(lane_iota, ROWS) == sub_iota, near_sum[c], 0.0),
                0,
                keepdims=True,
            )
            tile_out[c, pl.ds(tiles + t, 1), :] = jnp.sum(far_sum[c], 0, keepdims=True)
        return carry

    lax.fori_loop(0, tiles, one_tile, 0)
    slot_iota = lax.broadcasted_iota(jnp.int32, (slots, tiles), 0)
    take_near = (slot_iota == pair_ref[0:1, :]).astype(jnp.float32)
    take_far = (slot_iota == pair_ref[1:2, :]).astype(jnp.float32)
    for c in range(3):
        total = jnp.dot(
            take_near, tile_out[c, 0:tiles, :], precision=HIGHEST, preferred_element_type=jnp.float32
        ) - jnp.dot(
            take_far,
            tile_out[c, tiles : 2 * tiles, :],
            precision=HIGHEST,
            preferred_element_type=jnp.float32,
        )
        ans[:, c, :, :] = total.reshape(groups, ROWS, LANES)
    backward = []
    for turn, k, step, dd in partners:
        copy = pltpu.make_async_remote_copy(
            src_ref=ans.at[k],
            dst_ref=ret.at[g, 2 - step],
            send_sem=back_send.at[turn, step],
            recv_sem=back_recv.at[turn, step],
            device_id=(k, dd),
            device_id_type=MESH,
        )
        copy.start()
        backward.append(copy)
    ret[g, 1] = ans[g]

    rim_copy.wait_recv()
    state[blocks] = ghost_in[...]

    def elements(part, carry):
        for kk in range(ROWS):
            k = part * ROWS + kk
            at = pl.ds(pl.multiple_of(k * LANES, LANES), LANES)
            ids = slot_ref[:, at]
            for side, pair in enumerate(((0, 3), (1, 2))):
                b = cb_smem[side, k]
                block = state[b]
                for c in pair:
                    index = jnp.broadcast_to(ids[c : c + 1, :], (ROWS, LANES))
                    corner_buf[c, pl.ds(kk * ROWS, ROWS), :] = jnp.take_along_axis(
                        block, index, axis=1, mode="promise_in_bounds"
                    )
        pos = [[corner_buf[c, pl.ds(x, ROWS, stride=ROWS), :] for x in range(3)] for c in range(4)]
        vel = [
            [corner_buf[c, pl.ds(3 + x, ROWS, stride=ROWS), :] for x in range(3)] for c in range(4)
        ]
        here = pl.ds(pl.multiple_of(part * ROWS, ROWS), ROWS)
        old = [stress_ref[x, here, :] for x in range(3)]
        forces, new = shell_forces(pos, vel, old)
        for x in range(3):
            stress_out[x, here, :] = new[x]
            force_buf[0, pl.ds(x, ROWS, stride=ROWS), :] = forces[0][x]
            force_buf[0, pl.ds(4 + x, ROWS, stride=ROWS), :] = forces[3][x]
            force_buf[1, pl.ds(x, ROWS, stride=ROWS), :] = forces[1][x]
            force_buf[1, pl.ds(4 + x, ROWS, stride=ROWS), :] = forces[2][x]
        for kk in range(ROWS):
            k = part * ROWS + kk
            for side in range(2):
                spread[side, pl.ds(pl.multiple_of(k * ROWS, ROWS), ROWS), :] = jnp.take_along_axis(
                    force_buf[side, pl.ds(kk * ROWS, ROWS), :],
                    inverse[side, k],
                    axis=1,
                    mode="promise_in_bounds",
                )
        return carry

    lax.fori_loop(0, blocks // ROWS, elements, 0)

    block_iota = lax.broadcasted_iota(jnp.int32, (blocks + ROWS, blocks), 0)
    hits = [(block_iota == cb_ref[side : side + 1, :]).astype(jnp.float32) for side in range(2)]
    internal = []
    for c in range(3):
        total = None
        for side in range(2):
            part = (
                spread[side, pl.ds(c, blocks, stride=ROWS), :]
                + spread[side, pl.ds(4 + c, blocks, stride=ROWS), :]
            )
            value = jnp.dot(
                hits[side], part, precision=HIGHEST, preferred_element_type=jnp.float32
            )
            total = value if total is None else total + value
        internal.append(total)
        push_out[pl.ds(c, 1), :] = total[blocks : blocks + 1, :]
    push_copy = pltpu.make_async_remote_copy(
        src_ref=push_out,
        dst_ref=push_in,
        send_sem=push_sems.at[0],
        recv_sem=push_sems.at[1],
        device_id=(g, right),
        device_id_type=MESH,
    )
    push_copy.start()

    for copy in backward:
        copy.wait_recv()
    contact = []
    for c in range(3):
        answers = ret[:, :, c, :, :].reshape(places, LANES)
        contact.append(
            lax.dot_general(
                chosen,
                answers,
                (((0,), (0,)), ((), ())),
                precision=HIGHEST,
                preferred_element_type=jnp.float32,
            )
        )
    push_copy.wait_recv()
    is_rim = lax.broadcasted_iota(jnp.int32, (blocks, LANES), 0) == halo
    factor = DT / mass_ref[...]
    for c in range(3):
        extra = jnp.where(is_rim, push_in[pl.ds(c, 1), :], 0.0)
        force = contact[c] - internal[c][0:blocks, :] - extra
        vel_out[c] = vel_ref[c] + factor * force
    rim_copy.wait_send()
    push_copy.wait_send()
    for copy in forward:
        copy.wait_send()
    for copy in backward:
        copy.wait_send()


def local(
    positions,
    velocity,
    mass,
    stress,
    corner_block,
    corner_slot,
    halo_block,
    contact_owner,
    contact_slot,
    tile_pairs,
    tile_active,
):
    groups = lax.axis_size("group")
    doms = lax.axis_size("dom")
    blocks = corner_block.shape[2]
    nodes = positions.shape[2]
    tiles = tile_pairs.shape[2]
    slots = groups * ROWS
    vmem = pl.BlockSpec(memory_space=pltpu.VMEM)
    smem = pl.BlockSpec(memory_space=pltpu.SMEM)
    f32 = jnp.float32
    out = pl.pallas_call(
        functools.partial(kernel, groups, doms),
        out_shape=[jax.ShapeDtypeStruct((3, blocks, LANES), f32)] * 2,
        in_specs=[vmem] * 9 + [smem] * 4,
        out_specs=[vmem] * 2,
        scratch_shapes=[
            pltpu.VMEM((blocks + 1, ROWS, LANES), f32),
            pltpu.VMEM((ROWS, LANES), f32),
            pltpu.VMEM((ROWS, LANES), f32),
            pltpu.VMEM((groups, 3, 3, ROWS, LANES), f32),
            pltpu.VMEM((3, groups, 3, ROWS, LANES), f32),
            pltpu.VMEM((groups, 3, ROWS, LANES), f32),
            pltpu.VMEM((groups, 3, 3, ROWS, LANES), f32),
            pltpu.VMEM((slots, ROWS, LANES), f32),
            pltpu.VMEM((3, 2 * tiles, LANES), f32),
            pltpu.VMEM((2, blocks, ROWS, LANES), jnp.int32),
            pltpu.VMEM((4, ROWS * ROWS, LANES), f32),
            pltpu.VMEM((2, ROWS * ROWS, LANES), f32),
            pltpu.VMEM((2, blocks * ROWS, LANES), f32),
            pltpu.VMEM((ROWS, LANES), f32),
            pltpu.VMEM((ROWS, LANES), f32),
            pltpu.SemaphoreType.DMA((groups, 3)),
            pltpu.SemaphoreType.DMA((groups, 3)),
            pltpu.SemaphoreType.DMA((groups, 3)),
            pltpu.SemaphoreType.DMA((groups, 3)),
            pltpu.SemaphoreType.DMA((2,)),
            pltpu.SemaphoreType.DMA((2,)),
        ],
        compiler_params=pltpu.CompilerParams(
            collective_id=0, has_side_effects=True, vmem_limit_bytes=32 * 1024 * 1024
        ),
        name="shell_step",
    )(
        positions.reshape(3, blocks, LANES),
        velocity.reshape(3, blocks, LANES),
        mass.reshape(blocks, LANES),
        stress.reshape(3, blocks, LANES),
        corner_slot.reshape(4, nodes),
        corner_block.reshape(4, blocks),
        contact_owner,
        contact_slot,
        tile_pairs.reshape(2, tiles),
        corner_block.reshape(4, blocks),
        halo_block,
        tile_pairs.reshape(2, tiles),
        tile_active,
    )
    return out[0].reshape(1, 3, nodes), out[1].reshape(1, 3, nodes)


def solution(mesh):
    in_specs = (
        P("group", None, "dom"),
        P("group", None, "dom"),
        P("group", "dom"),
        P("group", None, "dom"),
        P("group", None, "dom"),
        P("group", None, "dom"),
        P("group", "dom"),
        P("group", "dom"),
        P("group", "dom"),
        P("group", None, "dom"),
        P("group", "dom"),
    )
    out_specs = (P("group", None, "dom"), P("group", None, "dom"))
    return jax.shard_map(local, mesh=mesh, in_specs=in_specs, out_specs=out_specs, check_vma=False)
```

```python
import functools

import jax
import jax.numpy as jnp
from jax import lax
from jax.experimental import pallas as pl
from jax.experimental.pallas import tpu as pltpu
from jax.sharding import PartitionSpec as P

LANES = 128
ROWS = 8
DT = 0.5
STIFF = 2.0
POISSON = 0.3
HOURGLASS = 0.1
PENALTY = 4.0
REACH = 1.0
MESH = pl.DeviceIdType.MESH
HIGHEST = lax.Precision.HIGHEST
CHUNKS = 2


def inner_rows(a, b):
    return a[0] * b[0] + a[1] * b[1] + a[2] * b[2]


def cross_rows(a, b):
    return (
        a[1] * b[2] - a[2] * b[1],
        a[2] * b[0] - a[0] * b[2],
        a[0] * b[1] - a[1] * b[0],
    )


def minus(a, b):
    return tuple(x - y for x, y in zip(a, b))


def scaled(a, s):
    return tuple(x * s for x in a)


def gather_lanes(value, index):
    return jnp.take_along_axis(value, index, axis=1, mode="promise_in_bounds")


def shell_forces(pos, vel, stress_old):
    diag_a = minus(pos[2], pos[0])
    diag_b = minus(pos[3], pos[1])
    normal = cross_rows(diag_a, diag_b)
    inv_j = lax.rsqrt(inner_rows(normal, normal))
    axis_three = scaled(normal, inv_j)
    tangent = minus(diag_a, diag_b)
    tangent = minus(tangent, scaled(axis_three, inner_rows(tangent, axis_three)))
    axis_one = scaled(tangent, lax.rsqrt(inner_rows(tangent, tangent)))
    axis_two = cross_rows(axis_three, axis_one)
    along_a = inner_rows(diag_a, axis_one)
    across_a = inner_rows(diag_a, axis_two)
    along_b = inner_rows(diag_b, axis_one)
    across_b = inner_rows(diag_b, axis_two)
    speed_a = minus(vel[2], vel[0])
    speed_b = minus(vel[3], vel[1])
    slide_a = inner_rows(speed_a, axis_one)
    lift_a = inner_rows(speed_a, axis_two)
    slide_b = inner_rows(speed_b, axis_one)
    lift_b = inner_rows(speed_b, axis_two)
    rate_xx = (across_b * slide_a - across_a * slide_b) * inv_j
    rate_yy = (along_a * lift_b - along_b * lift_a) * inv_j
    rate_xy = (
        across_b * lift_a - across_a * lift_b + along_a * slide_b - along_b * slide_a
    ) * inv_j
    s_xx = stress_old[0] + (DT * STIFF) * (rate_xx + POISSON * rate_yy)
    s_yy = stress_old[1] + (DT * STIFF) * (POISSON * rate_xx + rate_yy)
    s_xy = stress_old[2] + (DT * STIFF * 0.5 * (1.0 - POISSON)) * rate_xy
    half_xx, half_yy, half_xy = 0.5 * s_xx, 0.5 * s_yy, 0.5 * s_xy
    fx0 = along_b * half_xy - across_b * half_xx
    fy0 = along_b * half_yy - across_b * half_xy
    fx1 = across_a * half_xx - along_a * half_xy
    fy1 = across_a * half_xy - along_a * half_yy
    forces = [[], [], [], []]
    for c in range(3):
        mode = HOURGLASS * (vel[0][c] - vel[1][c] + vel[2][c] - vel[3][c])
        first = fx0 * axis_one[c] + fy0 * axis_two[c]
        second = fx1 * axis_one[c] + fy1 * axis_two[c]
        forces[0].append(mode + first)
        forces[1].append(second - mode)
        forces[2].append(mode - first)
        forces[3].append(-mode - second)
    return forces, (s_xx, s_yy, s_xy)


def kernel(
    groups,
    doms,
    pos_ref,
    vel_ref,
    mass_ref,
    stress_ref,
    slot_ref,
    cb_ref,
    owner_ref,
    spot_ref,
    pair_ref,
    cb_smem,
    halo_smem,
    pair_smem,
    active_smem,
    vel_out,
    stress_out,
    state,
    rim,
    ghost_in,
    out_buf,
    in_buf,
    ans,
    ret,
    canon,
    tile_out,
    inverse,
    corner_buf,
    spread,
    push_out,
    push_in,
    fwd_send,
    fwd_recv,
    back_send,
    back_recv,
    rim_sems,
    push_sems,
):
    g = lax.axis_index("group")
    d = lax.axis_index("dom")
    blocks = mass_ref.shape[0]
    tiles = pair_ref.shape[1]
    slots = groups * ROWS
    left = lax.rem(d + doms - 1, doms)
    right = lax.rem(d + 1, doms)
    partners = []
    for turn in range(groups):
        k = lax.rem(g + turn, groups)
        for step, dd in ((0, left), (1, d), (2, right)):
            if turn == 0 and step == 1:
                continue
            partners.append((turn, k, step, dd))

    barrier = pltpu.get_barrier_semaphore()
    for turn, k, step, dd in partners:
        pl.semaphore_signal(barrier, inc=1, device_id=(k, dd), device_id_type=MESH)

    halo = halo_smem[0, 0]
    state_rows = state.reshape((blocks + 1) * ROWS, LANES)
    for c in range(3):
        state_rows[pl.ds(c, blocks, stride=ROWS), :] = pos_ref[c]
        state_rows[pl.ds(3 + c, blocks, stride=ROWS), :] = vel_ref[c]
    rim[...] = state[halo]

    owner = owner_ref[...]
    step_of = lax.rem(lax.rem(owner, doms) - d + 1 + doms, doms)
    goal = (lax.div(owner, doms) * 3 + step_of) * ROWS + lax.rem(spot_ref[...], ROWS)
    goal = jnp.where(owner >= 0, goal, -1)
    places = groups * 3 * ROWS
    chosen = (
        lax.broadcasted_iota(jnp.int32, (places, blocks), 0) == goal
    ).astype(jnp.float32)
    for c in range(3):
        column = pos_ref[c]
        packed = jnp.dot(chosen, column, precision=HIGHEST, preferred_element_type=jnp.float32)
        out_buf[:, :, c, :, :] = packed.reshape(groups, 3, ROWS, LANES)

    pl.semaphore_wait(barrier, len(partners))

    rim_copy = pltpu.make_async_remote_copy(
        src_ref=rim,
        dst_ref=ghost_in,
        send_sem=rim_sems.at[0],
        recv_sem=rim_sems.at[1],
        device_id=(g, left),
        device_id_type=MESH,
    )
    rim_copy.start()
    forward = []
    for turn, k, step, dd in partners:
        copy = pltpu.make_async_remote_copy(
            src_ref=out_buf.at[k, step],
            dst_ref=in_buf.at[step, g],
            send_sem=fwd_send.at[turn, step],
            recv_sem=fwd_recv.at[turn, step],
            device_id=(k, dd),
            device_id_type=MESH,
        )
        copy.start()
        forward.append(copy)
    in_buf[1, g] = out_buf[g, 1]

    sub_iota = lax.broadcasted_iota(jnp.int32, (ROWS, LANES), 0)
    lane_iota = lax.broadcasted_iota(jnp.int32, (ROWS, LANES), 1)
    together = blocks // ROWS // CHUNKS

    def invert(chunk, carry):
        keys = []
        for part in range(together):
            for c in range(4):
                row = (chunk * together + part) * ROWS * 4 + c
                ids = slot_ref[pl.ds(row, ROWS, stride=4), :]
                keys.append((ids * LANES + lane_iota).astype(jnp.float32))
        size = 2
        while size <= LANES:
            gap = size // 2
            while gap >= 1:
                other = lane_iota ^ gap
                low = ((lane_iota & gap) == 0) == ((lane_iota & size) == 0)
                swapped = [gather_lanes(key, other) for key in keys]
                keys = [
                    jnp.where(low, jnp.minimum(key, swap), jnp.maximum(key, swap))
                    for key, swap in zip(keys, swapped)
                ]
                gap //= 2
            size *= 2
        for part in range(together):
            here = pl.ds(pl.multiple_of((chunk * together + part) * ROWS, ROWS), ROWS)
            for c in range(4):
                inverse[c, here, :] = keys[part * 4 + c].astype(jnp.int32) - lane_iota * LANES
        return carry

    lax.fori_loop(0, CHUNKS, invert, 0)

    for copy in forward:
        copy.wait_recv()
    canon_rows = canon.reshape(slots * ROWS, LANES)
    for c in range(3):
        for layer in range(groups):
            canon_rows[pl.ds(layer * ROWS * ROWS + c, ROWS, stride=ROWS), :] = (
                in_buf[0, layer, c] + in_buf[1, layer, c] + in_buf[2, layer, c]
            )
    ahead = (lane_iota + sub_iota) & (LANES - 1)
    back = (lane_iota - sub_iota) & (LANES - 1)

    def one_tile(t, carry):
        i = pair_smem[0, t]
        j = pair_smem[1, t]
        gain = PENALTY * active_smem[0, t].astype(jnp.float32)
        near_block = canon[i]
        far_block = canon[j]
        near = [jnp.broadcast_to(near_block[c : c + 1, :], (ROWS, LANES)) for c in range(3)]
        far = [
            gather_lanes(jnp.broadcast_to(far_block[c : c + 1, :], (ROWS, LANES)), ahead)
            for c in range(3)
        ]
        near_sum = [None] * 3
        far_sum = [None] * 3
        for r in range(LANES // ROWS):
            turn = ROWS * r
            if r:
                turned = [pltpu.roll(far[c], LANES - turn, 1) for c in range(3)]
            else:
                turned = far
            diff = [near[c] - turned[c] for c in range(3)]
            weight = jnp.maximum(REACH - inner_rows(diff, diff), 0.0)
            for c in range(3):
                push = weight * diff[c]
                home = pltpu.roll(push, turn, 1) if r else push
                near_sum[c] = near_sum[c] + push if r else push
                far_sum[c] = far_sum[c] + home if r else home
        for c in range(3):
            tile_out[c, pl.ds(t, 1), :] = gain * jnp.sum(near_sum[c], 0, keepdims=True)
            tile_out[c, pl.ds(tiles + t, 1), :] = gain * jnp.sum(
                gather_lanes(far_sum[c], back), 0, keepdims=True
            )
        return carry

    lax.fori_loop(0, tiles, one_tile, 0)
    slot_iota = lax.broadcasted_iota(jnp.int32, (slots, tiles), 0)
    take_near = (slot_iota == pair_ref[0:1, :]).astype(jnp.float32)
    take_far = (slot_iota == pair_ref[1:2, :]).astype(jnp.float32)
    for c in range(3):
        total = jnp.dot(
            take_near, tile_out[c, 0:tiles, :], precision=HIGHEST, preferred_element_type=jnp.float32
        ) - jnp.dot(
            take_far,
            tile_out[c, tiles : 2 * tiles, :],
            precision=HIGHEST,
            preferred_element_type=jnp.float32,
        )
        ans[:, c, :, :] = total.reshape(groups, ROWS, LANES)
    backward = []
    for turn, k, step, dd in partners:
        copy = pltpu.make_async_remote_copy(
            src_ref=ans.at[k],
            dst_ref=ret.at[g, 2 - step],
            send_sem=back_send.at[turn, step],
            recv_sem=back_recv.at[turn, step],
            device_id=(k, dd),
            device_id_type=MESH,
        )
        copy.start()
        backward.append(copy)
    ret[g, 1] = ans[g]

    rim_copy.wait_recv()
    state[blocks] = ghost_in[...]

    def elements(part, carry):
        here = pl.ds(pl.multiple_of(part * ROWS, ROWS), ROWS)
        for side in range(2):
            for kk in range(ROWS):
                b = cb_smem[side, part * ROWS + kk]
                corner_buf[side, pl.ds(kk * ROWS, ROWS), :] = state[b]
        pos = [None] * 4
        vel = [None] * 4
        for side, pair in enumerate(((0, 3), (1, 2))):
            column = [corner_buf[side, pl.ds(x, ROWS, stride=ROWS), :] for x in range(6)]
            for c in pair:
                ids = slot_ref[pl.ds(part * ROWS * 4 + c, ROWS, stride=4), :]
                picked = [gather_lanes(value, ids) for value in column]
                pos[c] = picked[:3]
                vel[c] = picked[3:]
        old = [stress_ref[x, here, :] for x in range(3)]
        forces, new = shell_forces(pos, vel, old)
        for x in range(3):
            stress_out[x, here, :] = new[x]
            for side, pair in enumerate(((0, 3), (1, 2))):
                spread[side, x, here, :] = sum(
                    gather_lanes(forces[c][x], inverse[c, here, :]) for c in pair
                )
        return carry

    lax.fori_loop(0, blocks // ROWS, elements, 0)

    block_iota = lax.broadcasted_iota(jnp.int32, (blocks + ROWS, blocks), 0)
    hits = [(block_iota == cb_ref[side : side + 1, :]).astype(jnp.float32) for side in range(2)]
    internal = []
    for c in range(3):
        total = None
        for side in range(2):
            value = jnp.dot(
                hits[side], spread[side, c], precision=HIGHEST, preferred_element_type=jnp.float32
            )
            total = value if total is None else total + value
        internal.append(total)
        push_out[pl.ds(c, 1), :] = total[blocks : blocks + 1, :]
    push_copy = pltpu.make_async_remote_copy(
        src_ref=push_out,
        dst_ref=push_in,
        send_sem=push_sems.at[0],
        recv_sem=push_sems.at[1],
        device_id=(g, right),
        device_id_type=MESH,
    )
    push_copy.start()

    for copy in backward:
        copy.wait_recv()
    contact = []
    for c in range(3):
        answers = ret[:, :, c, :, :].reshape(places, LANES)
        contact.append(
            lax.dot_general(
                chosen,
                answers,
                (((0,), (0,)), ((), ())),
                precision=HIGHEST,
                preferred_element_type=jnp.float32,
            )
        )
    push_copy.wait_recv()
    is_rim = lax.broadcasted_iota(jnp.int32, (blocks, LANES), 0) == halo
    factor = DT / mass_ref[...]
    for c in range(3):
        extra = jnp.where(is_rim, push_in[pl.ds(c, 1), :], 0.0)
        force = contact[c] - internal[c][0:blocks, :] - extra
        vel_out[c] = vel_ref[c] + factor * force
    rim_copy.wait_send()
    push_copy.wait_send()
    for copy in forward:
        copy.wait_send()
    for copy in backward:
        copy.wait_send()


def local(
    positions,
    velocity,
    mass,
    stress,
    corner_block,
    corner_slot,
    halo_block,
    contact_owner,
    contact_slot,
    tile_pairs,
    tile_active,
):
    groups = lax.axis_size("group")
    doms = lax.axis_size("dom")
    blocks = corner_block.shape[2]
    nodes = positions.shape[2]
    tiles = tile_pairs.shape[2]
    slots = groups * ROWS
    vmem = pl.BlockSpec(memory_space=pltpu.VMEM)
    smem = pl.BlockSpec(memory_space=pltpu.SMEM)
    f32 = jnp.float32
    out = pl.pallas_call(
        functools.partial(kernel, groups, doms),
        out_shape=[jax.ShapeDtypeStruct((3, blocks, LANES), f32)] * 2,
        in_specs=[vmem] * 9 + [smem] * 4,
        out_specs=[vmem] * 2,
        scratch_shapes=[
            pltpu.VMEM((blocks + 1, ROWS, LANES), f32),
            pltpu.VMEM((ROWS, LANES), f32),
            pltpu.VMEM((ROWS, LANES), f32),
            pltpu.VMEM((groups, 3, 3, ROWS, LANES), f32),
            pltpu.VMEM((3, groups, 3, ROWS, LANES), f32),
            pltpu.VMEM((groups, 3, ROWS, LANES), f32),
            pltpu.VMEM((groups, 3, 3, ROWS, LANES), f32),
            pltpu.VMEM((slots, ROWS, LANES), f32),
            pltpu.VMEM((3, 2 * tiles, LANES), f32),
            pltpu.VMEM((4, blocks, LANES), jnp.int32),
            pltpu.VMEM((2, ROWS * ROWS, LANES), f32),
            pltpu.VMEM((2, 3, blocks, LANES), f32),
            pltpu.VMEM((ROWS, LANES), f32),
            pltpu.VMEM((ROWS, LANES), f32),
            pltpu.SemaphoreType.DMA((groups, 3)),
            pltpu.SemaphoreType.DMA((groups, 3)),
            pltpu.SemaphoreType.DMA((groups, 3)),
            pltpu.SemaphoreType.DMA((groups, 3)),
            pltpu.SemaphoreType.DMA((2,)),
            pltpu.SemaphoreType.DMA((2,)),
        ],
        compiler_params=pltpu.CompilerParams(
            collective_id=0, has_side_effects=True, vmem_limit_bytes=32 * 1024 * 1024
        ),
        name="shell_step",
    )(
        positions.reshape(3, blocks, LANES),
        velocity.reshape(3, blocks, LANES),
        mass.reshape(blocks, LANES),
        stress.reshape(3, blocks, LANES),
        corner_slot.reshape(4, blocks, LANES).transpose(1, 0, 2).reshape(4 * blocks, LANES),
        corner_block.reshape(4, blocks),
        contact_owner,
        contact_slot,
        tile_pairs.reshape(2, tiles),
        corner_block.reshape(4, blocks),
        halo_block,
        tile_pairs.reshape(2, tiles),
        tile_active,
    )
    return out[0].reshape(1, 3, nodes), out[1].reshape(1, 3, nodes)


def solution(mesh):
    in_specs = (
        P("group", None, "dom"),
        P("group", None, "dom"),
        P("group", "dom"),
        P("group", None, "dom"),
        P("group", None, "dom"),
        P("group", None, "dom"),
        P("group", "dom"),
        P("group", "dom"),
        P("group", "dom"),
        P("group", None, "dom"),
        P("group", "dom"),
    )
    out_specs = (P("group", None, "dom"), P("group", None, "dom"))
    return jax.shard_map(local, mesh=mesh, in_specs=in_specs, out_specs=out_specs, check_vma=False)
```

```python
import functools

import jax
import jax.numpy as jnp
from jax import lax
from jax.experimental import pallas as pl
from jax.experimental.pallas import tpu as pltpu
from jax.sharding import PartitionSpec as P

LANES = 128
ROWS = 8
DT = 0.5
STIFF = 2.0
POISSON = 0.3
HOURGLASS = 0.1
PENALTY = 4.0
REACH = 1.0
MESH = pl.DeviceIdType.MESH
HIGHEST = lax.Precision.HIGHEST
BF16 = jnp.bfloat16


def inner_rows(a, b):
    return a[0] * b[0] + a[1] * b[1] + a[2] * b[2]


def cross_rows(a, b):
    return (
        a[1] * b[2] - a[2] * b[1],
        a[2] * b[0] - a[0] * b[2],
        a[0] * b[1] - a[1] * b[0],
    )


def minus(a, b):
    return tuple(x - y for x, y in zip(a, b))


def scaled(a, s):
    return tuple(x * s for x in a)


def gather_lanes(value, index):
    return jnp.take_along_axis(value, index, axis=1, mode="promise_in_bounds")


def pieces(value, count):
    parts = []
    for _ in range(count - 1):
        top = value.astype(BF16).astype(jnp.float32)
        parts.append(top)
        value = value - top
    parts.append(value)
    return jnp.concatenate(parts, 0).astype(BF16)


def pick_rows(chosen, value, count):
    lhs = jnp.concatenate([chosen] * count, 1).astype(BF16)
    return jnp.dot(lhs, pieces(value, count), preferred_element_type=jnp.float32)


def sort_rows(rows, sub):
    rows = list(rows)
    for k in range(1, 8):
        up = None if k < 4 or k == 7 else (sub & (1 << (k - 4))) == 0
        for j in range(k - 1, -1, -1):
            if j >= 4:
                gap = 1 << (j - 4)
                keep = (sub & gap) == 0
                if up is not None:
                    keep = keep == up
                for r in range(16):
                    other = jnp.take_along_axis(
                        rows[r], sub ^ gap, axis=0, mode="promise_in_bounds"
                    )
                    rows[r] = jnp.where(
                        keep, jnp.minimum(rows[r], other), jnp.maximum(rows[r], other)
                    )
                continue
            for r in range(16):
                far = r | (1 << j)
                if far == r:
                    continue
                low = jnp.minimum(rows[r], rows[far])
                high = jnp.maximum(rows[r], rows[far])
                if up is not None:
                    low, high = jnp.where(up, low, high), jnp.where(up, high, low)
                elif k < 4 and r & (1 << k):
                    low, high = high, low
                rows[r], rows[far] = low, high
    return rows


def shell_forces(pos, vel, stress_old):
    diag_a = minus(pos[2], pos[0])
    diag_b = minus(pos[3], pos[1])
    normal = cross_rows(diag_a, diag_b)
    inv_j = lax.rsqrt(inner_rows(normal, normal))
    axis_three = scaled(normal, inv_j)
    tangent = minus(diag_a, diag_b)
    tangent = minus(tangent, scaled(axis_three, inner_rows(tangent, axis_three)))
    axis_one = scaled(tangent, lax.rsqrt(inner_rows(tangent, tangent)))
    axis_two = cross_rows(axis_three, axis_one)
    along_a = inner_rows(diag_a, axis_one)
    across_a = inner_rows(diag_a, axis_two)
    along_b = inner_rows(diag_b, axis_one)
    across_b = inner_rows(diag_b, axis_two)
    speed_a = minus(vel[2], vel[0])
    speed_b = minus(vel[3], vel[1])
    slide_a = inner_rows(speed_a, axis_one)
    lift_a = inner_rows(speed_a, axis_two)
    slide_b = inner_rows(speed_b, axis_one)
    lift_b = inner_rows(speed_b, axis_two)
    rate_xx = (across_b * slide_a - across_a * slide_b) * inv_j
    rate_yy = (along_a * lift_b - along_b * lift_a) * inv_j
    rate_xy = (
        across_b * lift_a - across_a * lift_b + along_a * slide_b - along_b * slide_a
    ) * inv_j
    s_xx = stress_old[0] + (DT * STIFF) * (rate_xx + POISSON * rate_yy)
    s_yy = stress_old[1] + (DT * STIFF) * (POISSON * rate_xx + rate_yy)
    s_xy = stress_old[2] + (DT * STIFF * 0.5 * (1.0 - POISSON)) * rate_xy
    half_xx, half_yy, half_xy = 0.5 * s_xx, 0.5 * s_yy, 0.5 * s_xy
    fx0 = along_b * half_xy - across_b * half_xx
    fy0 = along_b * half_yy - across_b * half_xy
    fx1 = across_a * half_xx - along_a * half_xy
    fy1 = across_a * half_xy - along_a * half_yy
    forces = [[], [], [], []]
    for c in range(3):
        mode = HOURGLASS * (vel[0][c] - vel[1][c] + vel[2][c] - vel[3][c])
        first = fx0 * axis_one[c] + fy0 * axis_two[c]
        second = fx1 * axis_one[c] + fy1 * axis_two[c]
        forces[0].append(mode + first)
        forces[1].append(second - mode)
        forces[2].append(mode - first)
        forces[3].append(-mode - second)
    return forces, (s_xx, s_yy, s_xy)


def kernel(
    groups,
    doms,
    pos_hbm,
    vel_hbm,
    mass_hbm,
    stress_hbm,
    slot_hbm,
    cb_hbm,
    owner_hbm,
    spot_hbm,
    pair_hbm,
    active_hbm,
    halo_hbm,
    vel_out,
    stress_out,
    pos_ref,
    vel_ref,
    mass_ref,
    stress_ref,
    slot_ref,
    cb_ref,
    owner_ref,
    spot_ref,
    pair_ref,
    active_ref,
    cb_smem,
    pair_smem,
    halo_smem,
    in_sems,
    state,
    rim,
    ghost_in,
    out_buf,
    in_buf,
    ans,
    ret,
    canon,
    tile_out,
    inverse,
    sort_buf,
    corner_buf,
    spread,
    push_out,
    push_in,
    fwd_send,
    fwd_recv,
    back_send,
    back_recv,
    rim_sems,
    push_sems,
):
    g = lax.axis_index("group")
    d = lax.axis_index("dom")
    blocks = mass_ref.shape[0]
    tiles = pair_ref.shape[1]
    slots = groups * ROWS
    left = lax.rem(d + doms - 1, doms)
    right = lax.rem(d + 1, doms)
    partners = []
    for turn in range(groups):
        k = lax.rem(g + turn, groups)
        for step, dd in ((0, left), (1, d), (2, right)):
            if turn == 0 and step == 1:
                continue
            partners.append((turn, k, step, dd))

    barrier = pltpu.get_barrier_semaphore()
    for turn, k, step, dd in partners:
        pl.semaphore_signal(barrier, inc=1, device_id=(k, dd), device_id_type=MESH)

    sources = (
        (pos_hbm, pos_ref),
        (owner_hbm, owner_ref),
        (spot_hbm, spot_ref),
        (vel_hbm, vel_ref),
        (halo_hbm, halo_smem),
        (slot_hbm, slot_ref),
        (pair_hbm, pair_ref),
        (pair_hbm, pair_smem),
        (active_hbm, active_ref),
        (cb_hbm, cb_ref),
        (cb_hbm, cb_smem),
        (stress_hbm, stress_ref),
        (mass_hbm, mass_ref),
    )
    loads = []
    for n, (source, target) in enumerate(sources):
        copy = pltpu.make_async_copy(source, target, in_sems.at[n])
        copy.start()
        loads.append(copy)
    for copy in loads[:3]:
        copy.wait()
    sub_iota = lax.broadcasted_iota(jnp.int32, (ROWS, LANES), 0)
    lane_iota = lax.broadcasted_iota(jnp.int32, (ROWS, LANES), 1)
    owner = owner_ref[...]
    step_of = lax.rem(lax.rem(owner, doms) - d + 1 + doms, doms)
    goal = (lax.div(owner, doms) * 3 + step_of) * ROWS + lax.rem(spot_ref[...], ROWS)
    goal = jnp.where(owner >= 0, goal, -1)
    places = groups * 3 * ROWS
    chosen = (
        lax.broadcasted_iota(jnp.int32, (places, blocks), 0) == goal
    ).astype(jnp.float32)
    everywhere = jnp.concatenate([pos_ref[c] for c in range(3)], 1)
    packed = pick_rows(chosen, everywhere, 3)
    for c in range(3):
        out_buf[:, :, c, :, :] = packed[:, c * LANES : (c + 1) * LANES].reshape(
            groups, 3, ROWS, LANES
        )
    pl.semaphore_wait(barrier, len(partners))

    forward = []
    for turn, k, step, dd in partners:
        copy = pltpu.make_async_remote_copy(
            src_ref=out_buf.at[k, step],
            dst_ref=in_buf.at[step, g],
            send_sem=fwd_send.at[turn, step],
            recv_sem=fwd_recv.at[turn, step],
            device_id=(k, dd),
            device_id_type=MESH,
        )
        copy.start()
        forward.append(copy)
    in_buf[1, g] = out_buf[g, 1]

    for copy in loads[3:5]:
        copy.wait()
    halo = halo_smem[0, 0]
    state_rows = state.reshape((blocks + 1) * ROWS, LANES)
    for c in range(3):
        state_rows[pl.ds(c, blocks, stride=ROWS), :] = pos_ref[c]
        state_rows[pl.ds(3 + c, blocks, stride=ROWS), :] = vel_ref[c]
    rim[...] = state[halo]
    rim_copy = pltpu.make_async_remote_copy(
        src_ref=rim,
        dst_ref=ghost_in,
        send_sem=rim_sems.at[0],
        recv_sem=rim_sems.at[1],
        device_id=(g, left),
        device_id_type=MESH,
    )
    rim_copy.start()
    for copy in loads[5:]:
        copy.wait()
    goers = jnp.transpose(jnp.concatenate([chosen, jnp.zeros((LANES - places, blocks), jnp.float32)], 0))

    wide_iota = lax.broadcasted_iota(jnp.int32, (LANES, LANES), 1)
    for half in range(4 * blocks // LANES):
        rows = pl.ds(half * LANES, LANES)
        keys = jnp.transpose((slot_ref[rows, :] * LANES + wide_iota).astype(jnp.float32))
        keys = sort_rows([keys[r * ROWS : (r + 1) * ROWS, :] for r in range(16)], sub_iota)
        for r in range(16):
            sort_buf[half, pl.ds(r, ROWS, stride=16), :] = keys[r]
        inverse[rows, :] = jnp.transpose(sort_buf[half]).astype(jnp.int32) - wide_iota * LANES

    for copy in forward:
        copy.wait_recv()
    ahead = (lane_iota + sub_iota) & (LANES - 1)
    back = (lane_iota - sub_iota) & (LANES - 1)
    for layer in range(groups):
        for c in range(3):
            rows = in_buf[0, layer, c] + in_buf[1, layer, c] + in_buf[2, layer, c]
            for spot in range(ROWS):
                slot = layer * ROWS + spot
                row = jnp.broadcast_to(rows[spot : spot + 1, :], (ROWS, LANES))
                canon[slot, c] = row
                canon[slot, 3 + c] = gather_lanes(row, ahead)

    def one_tile(t, carry):
        near_block = canon[pair_smem[0, t]]
        far_block = canon[pair_smem[1, t]]
        near = [near_block[c] for c in range(3)]
        far = [far_block[3 + c] for c in range(3)]
        near_sum = [None] * 3
        far_sum = [None] * 3
        for r in range(LANES // ROWS):
            turn = ROWS * r
            if r:
                turned = [pltpu.roll(far[c], LANES - turn, 1) for c in range(3)]
            else:
                turned = far
            diff = [near[c] - turned[c] for c in range(3)]
            weight = jnp.maximum(REACH - inner_rows(diff, diff), 0.0)
            for c in range(3):
                push = weight * diff[c]
                home = pltpu.roll(push, turn, 1) if r else push
                near_sum[c] = near_sum[c] + push if r else push
                far_sum[c] = far_sum[c] + home if r else home
        for c in range(3):
            tile_out[t, c] = near_sum[c]
            tile_out[t, 3 + c] = far_sum[c]
        return carry

    lax.fori_loop(0, tiles, one_tile, 0, unroll=2)
    near_rows = []
    far_rows = []
    for t in range(tiles):
        near_rows.append(
            jnp.concatenate(
                [jnp.sum(tile_out[t, c], 0, keepdims=True) for c in range(3)], 1
            )
        )
        far_rows.append(
            jnp.concatenate(
                [
                    jnp.sum(gather_lanes(tile_out[t, 3 + c], back), 0, keepdims=True)
                    for c in range(3)
                ],
                1,
            )
        )
    slot_iota = lax.broadcasted_iota(jnp.int32, (slots, tiles), 0)
    gain = PENALTY * active_ref[...].astype(jnp.float32)
    take_near = jnp.where(slot_iota == pair_ref[0:1, :], gain, 0.0)
    take_far = jnp.where(slot_iota == pair_ref[1:2, :], -gain, 0.0)
    total = pick_rows(
        jnp.concatenate([take_near, take_far], 1), jnp.concatenate(near_rows + far_rows, 0), 2
    )
    for c in range(3):
        ans[:, c, :, :] = total[:, c * LANES : (c + 1) * LANES].reshape(groups, ROWS, LANES)
    backward = []
    for turn, k, step, dd in partners:
        copy = pltpu.make_async_remote_copy(
            src_ref=ans.at[k],
            dst_ref=ret.at[g, 2 - step],
            send_sem=back_send.at[turn, step],
            recv_sem=back_recv.at[turn, step],
            device_id=(k, dd),
            device_id_type=MESH,
        )
        copy.start()
        backward.append(copy)
    ret[g, 1] = ans[g]

    rim_copy.wait_recv()
    state[blocks] = ghost_in[...]

    def elements(part, carry):
        here = pl.ds(pl.multiple_of(part * ROWS, ROWS), ROWS)
        for side in range(2):
            for kk in range(ROWS):
                b = cb_smem[side, part * ROWS + kk]
                corner_buf[side, pl.ds(kk * ROWS, ROWS), :] = state[b]
        pos = [None] * 4
        vel = [None] * 4
        for side, pair in enumerate(((0, 3), (1, 2))):
            column = [corner_buf[side, pl.ds(x, ROWS, stride=ROWS), :] for x in range(6)]
            for c in pair:
                ids = slot_ref[pl.ds(part * ROWS * 4 + c, ROWS, stride=4), :]
                picked = [gather_lanes(value, ids) for value in column]
                pos[c] = picked[:3]
                vel[c] = picked[3:]
        old = [stress_ref[x, here, :] for x in range(3)]
        forces, new = shell_forces(pos, vel, old)
        for x in range(3):
            stress_out[x, here, :] = new[x]
            for side, pair in enumerate(((0, 3), (1, 2))):
                spread[side, x, here, :] = sum(
                    gather_lanes(forces[c][x], inverse[pl.ds(part * ROWS * 4 + c, ROWS, stride=4), :]) for c in pair
                )
        return carry

    lax.fori_loop(0, blocks // ROWS, elements, 0)

    block_iota = lax.broadcasted_iota(jnp.int32, (blocks + ROWS, blocks), 0)
    hits = jnp.concatenate(
        [(block_iota == cb_ref[side : side + 1, :]).astype(jnp.float32) for side in range(2)], 1
    )
    both = jnp.concatenate(
        [
            jnp.concatenate([spread[side, c] for c in range(3)], 1)
            for side in range(2)
        ],
        0,
    )
    internal = pick_rows(hits, both, 2)
    for c in range(3):
        push_out[pl.ds(c, 1), :] = internal[blocks : blocks + 1, c * LANES : (c + 1) * LANES]
    push_copy = pltpu.make_async_remote_copy(
        src_ref=push_out,
        dst_ref=push_in,
        send_sem=push_sems.at[0],
        recv_sem=push_sems.at[1],
        device_id=(g, right),
        device_id_type=MESH,
    )
    push_copy.start()

    for copy in backward:
        copy.wait_recv()
    answers = jnp.concatenate(
        [ret[:, :, c, :, :].reshape(places, LANES) for c in range(3)], 1
    )
    answers = jnp.concatenate([answers, jnp.zeros((LANES - places, 3 * LANES), jnp.float32)], 0)
    contact = pick_rows(goers, answers, 2)
    push_copy.wait_recv()
    is_rim = lax.broadcasted_iota(jnp.int32, (blocks, LANES), 0) == halo
    factor = DT / mass_ref[...]
    for c in range(3):
        extra = jnp.where(is_rim, push_in[pl.ds(c, 1), :], 0.0)
        cols = slice(c * LANES, (c + 1) * LANES)
        force = contact[:, cols] - internal[0:blocks, cols] - extra
        vel_out[c] = vel_ref[c] + factor * force
    rim_copy.wait_send()
    push_copy.wait_send()
    for copy in forward:
        copy.wait_send()
    for copy in backward:
        copy.wait_send()


def local(
    positions,
    velocity,
    mass,
    stress,
    corner_block,
    corner_slot,
    halo_block,
    contact_owner,
    contact_slot,
    tile_pairs,
    tile_active,
):
    groups = lax.axis_size("group")
    doms = lax.axis_size("dom")
    blocks = corner_block.shape[2]
    nodes = positions.shape[2]
    tiles = tile_pairs.shape[2]
    slots = groups * ROWS
    vmem = pl.BlockSpec(memory_space=pltpu.VMEM)
    i32 = jnp.int32
    f32 = jnp.float32
    out = pl.pallas_call(
        functools.partial(kernel, groups, doms),
        out_shape=[jax.ShapeDtypeStruct((3, blocks, LANES), f32)] * 2,
        in_specs=[pl.BlockSpec(memory_space=pltpu.HBM)] * 11,
        out_specs=[vmem] * 2,
        scratch_shapes=[
            pltpu.VMEM((3, blocks, LANES), f32),
            pltpu.VMEM((3, blocks, LANES), f32),
            pltpu.VMEM((blocks, LANES), f32),
            pltpu.VMEM((3, blocks, LANES), f32),
            pltpu.VMEM((4 * blocks, LANES), i32),
            pltpu.VMEM((4, blocks), i32),
            pltpu.VMEM((1, blocks), i32),
            pltpu.VMEM((1, blocks), i32),
            pltpu.VMEM((2, tiles), i32),
            pltpu.VMEM((1, tiles), i32),
            pltpu.SMEM((4, blocks), i32),
            pltpu.SMEM((2, tiles), i32),
            pltpu.SMEM((1, 1), i32),
            pltpu.SemaphoreType.DMA((13,)),
            pltpu.VMEM((blocks + 1, ROWS, LANES), f32),
            pltpu.VMEM((ROWS, LANES), f32),
            pltpu.VMEM((ROWS, LANES), f32),
            pltpu.VMEM((groups, 3, 3, ROWS, LANES), f32),
            pltpu.VMEM((3, groups, 3, ROWS, LANES), f32),
            pltpu.VMEM((groups, 3, ROWS, LANES), f32),
            pltpu.VMEM((groups, 3, 3, ROWS, LANES), f32),
            pltpu.VMEM((slots, 6, ROWS, LANES), f32),
            pltpu.VMEM((tiles, 6, ROWS, LANES), f32),
            pltpu.VMEM((4 * blocks, LANES), jnp.int32),
            pltpu.VMEM((4 * blocks // LANES, LANES, LANES), f32),
            pltpu.VMEM((2, ROWS * ROWS, LANES), f32),
            pltpu.VMEM((2, 3, blocks, LANES), f32),
            pltpu.VMEM((ROWS, LANES), f32),
            pltpu.VMEM((ROWS, LANES), f32),
            pltpu.SemaphoreType.DMA((groups, 3)),
            pltpu.SemaphoreType.DMA((groups, 3)),
            pltpu.SemaphoreType.DMA((groups, 3)),
            pltpu.SemaphoreType.DMA((groups, 3)),
            pltpu.SemaphoreType.DMA((2,)),
            pltpu.SemaphoreType.DMA((2,)),
        ],
        compiler_params=pltpu.CompilerParams(
            collective_id=0, has_side_effects=True, vmem_limit_bytes=60 * 1024 * 1024
        ),
        name="shell_step",
    )(
        positions.reshape(3, blocks, LANES),
        velocity.reshape(3, blocks, LANES),
        mass.reshape(blocks, LANES),
        stress.reshape(3, blocks, LANES),
        corner_slot.reshape(4, blocks, LANES).transpose(1, 0, 2).reshape(4 * blocks, LANES),
        corner_block.reshape(4, blocks),
        contact_owner,
        contact_slot,
        tile_pairs.reshape(2, tiles),
        tile_active,
        halo_block,
    )
    return out[0].reshape(1, 3, nodes), out[1].reshape(1, 3, nodes)


def solution(mesh):
    in_specs = (
        P("group", None, "dom"),
        P("group", None, "dom"),
        P("group", "dom"),
        P("group", None, "dom"),
        P("group", None, "dom"),
        P("group", None, "dom"),
        P("group", "dom"),
        P("group", "dom"),
        P("group", "dom"),
        P("group", None, "dom"),
        P("group", "dom"),
    )
    out_specs = (P("group", None, "dom"), P("group", None, "dom"))
    return jax.shard_map(local, mesh=mesh, in_specs=in_specs, out_specs=out_specs, check_vma=False)
```

```python
import functools

import jax
import jax.numpy as jnp
from jax import lax
from jax.experimental import pallas as pl
from jax.experimental.pallas import tpu as pltpu
from jax.sharding import PartitionSpec as P

LANES = 128
ROWS = 8
DT = 0.5
STIFF = 2.0
POISSON = 0.3
HOURGLASS = 0.1
PENALTY = 4.0
REACH = 1.0
MESH = pl.DeviceIdType.MESH
HIGHEST = lax.Precision.HIGHEST
BF16 = jnp.bfloat16
UNROLL = 2


def inner_rows(a, b):
    return a[0] * b[0] + a[1] * b[1] + a[2] * b[2]


def cross_rows(a, b):
    return (
        a[1] * b[2] - a[2] * b[1],
        a[2] * b[0] - a[0] * b[2],
        a[0] * b[1] - a[1] * b[0],
    )


def minus(a, b):
    return tuple(x - y for x, y in zip(a, b))


def scaled(a, s):
    return tuple(x * s for x in a)


def gather_lanes(value, index):
    return jnp.take_along_axis(value, index, axis=1, mode="promise_in_bounds")


def pieces(value, count):
    parts = []
    for _ in range(count - 1):
        top = value.astype(BF16).astype(jnp.float32)
        parts.append(top)
        value = value - top
    parts.append(value)
    return jnp.concatenate(parts, 0).astype(BF16)


def pick_rows(chosen, value, count):
    lhs = jnp.concatenate([chosen] * count, 1).astype(BF16)
    return jnp.dot(lhs, pieces(value, count), preferred_element_type=jnp.float32)


def sort_rows(rows, sub):
    rows = list(rows)
    for k in range(1, 8):
        up = None if k < 4 or k == 7 else (sub & (1 << (k - 4))) == 0
        for j in range(k - 1, -1, -1):
            if j >= 4:
                gap = 1 << (j - 4)
                keep = (sub & gap) == 0
                if up is not None:
                    keep = keep == up
                for r in range(16):
                    other = jnp.take_along_axis(
                        rows[r], sub ^ gap, axis=0, mode="promise_in_bounds"
                    )
                    rows[r] = jnp.where(
                        keep, jnp.minimum(rows[r], other), jnp.maximum(rows[r], other)
                    )
                continue
            for r in range(16):
                far = r | (1 << j)
                if far == r:
                    continue
                low = jnp.minimum(rows[r], rows[far])
                high = jnp.maximum(rows[r], rows[far])
                if up is not None:
                    low, high = jnp.where(up, low, high), jnp.where(up, high, low)
                elif k < 4 and r & (1 << k):
                    low, high = high, low
                rows[r], rows[far] = low, high
    return rows


def shell_forces(pos, vel, stress_old):
    diag_a = minus(pos[2], pos[0])
    diag_b = minus(pos[3], pos[1])
    normal = cross_rows(diag_a, diag_b)
    inv_j = lax.rsqrt(inner_rows(normal, normal))
    axis_three = scaled(normal, inv_j)
    tangent = minus(diag_a, diag_b)
    tangent = minus(tangent, scaled(axis_three, inner_rows(tangent, axis_three)))
    axis_one = scaled(tangent, lax.rsqrt(inner_rows(tangent, tangent)))
    axis_two = cross_rows(axis_three, axis_one)
    along_a = inner_rows(diag_a, axis_one)
    across_a = inner_rows(diag_a, axis_two)
    along_b = inner_rows(diag_b, axis_one)
    across_b = inner_rows(diag_b, axis_two)
    speed_a = minus(vel[2], vel[0])
    speed_b = minus(vel[3], vel[1])
    slide_a = inner_rows(speed_a, axis_one)
    lift_a = inner_rows(speed_a, axis_two)
    slide_b = inner_rows(speed_b, axis_one)
    lift_b = inner_rows(speed_b, axis_two)
    rate_xx = (across_b * slide_a - across_a * slide_b) * inv_j
    rate_yy = (along_a * lift_b - along_b * lift_a) * inv_j
    rate_xy = (
        across_b * lift_a - across_a * lift_b + along_a * slide_b - along_b * slide_a
    ) * inv_j
    s_xx = stress_old[0] + (DT * STIFF) * (rate_xx + POISSON * rate_yy)
    s_yy = stress_old[1] + (DT * STIFF) * (POISSON * rate_xx + rate_yy)
    s_xy = stress_old[2] + (DT * STIFF * 0.5 * (1.0 - POISSON)) * rate_xy
    half_xx, half_yy, half_xy = 0.5 * s_xx, 0.5 * s_yy, 0.5 * s_xy
    fx0 = along_b * half_xy - across_b * half_xx
    fy0 = along_b * half_yy - across_b * half_xy
    fx1 = across_a * half_xx - along_a * half_xy
    fy1 = across_a * half_xy - along_a * half_yy
    forces = [[], [], [], []]
    for c in range(3):
        mode = HOURGLASS * (vel[0][c] - vel[1][c] + vel[2][c] - vel[3][c])
        first = fx0 * axis_one[c] + fy0 * axis_two[c]
        second = fx1 * axis_one[c] + fy1 * axis_two[c]
        forces[0].append(mode + first)
        forces[1].append(second - mode)
        forces[2].append(mode - first)
        forces[3].append(-mode - second)
    return forces, (s_xx, s_yy, s_xy)


def kernel(
    groups,
    doms,
    pos_hbm,
    vel_hbm,
    mass_hbm,
    stress_hbm,
    slot_hbm,
    cb_hbm,
    owner_hbm,
    spot_hbm,
    pair_hbm,
    active_hbm,
    halo_hbm,
    vel_out,
    stress_out,
    pos_ref,
    vel_ref,
    mass_ref,
    stress_ref,
    slot_ref,
    cb_ref,
    owner_ref,
    spot_ref,
    pair_ref,
    active_ref,
    cb_smem,
    pair_smem,
    halo_smem,
    in_sems,
    state,
    rim,
    ghost_in,
    out_buf,
    in_buf,
    ans,
    ret,
    canon,
    near_pick,
    cols_even,
    cols_odd,
    held_even,
    held_odd,
    near_sums,
    far_sums,
    inverse,
    sort_buf,
    corner_buf,
    spread,
    push_out,
    push_in,
    fwd_send,
    fwd_recv,
    back_send,
    back_recv,
    rim_sems,
    push_sems,
):
    g = lax.axis_index("group")
    d = lax.axis_index("dom")
    blocks = mass_ref.shape[0]
    tiles = pair_ref.shape[1]
    slots = groups * ROWS
    left = lax.rem(d + doms - 1, doms)
    right = lax.rem(d + 1, doms)
    partners = []
    for turn in (2, 1, 3, 0):
        k = lax.rem(g + turn, groups)
        for step, dd in ((0, left), (1, d), (2, right)):
            if turn == 0 and step == 1:
                continue
            partners.append((turn, k, step, dd))

    barrier = pltpu.get_barrier_semaphore()
    for turn, k, step, dd in partners:
        pl.semaphore_signal(barrier, inc=1, device_id=(k, dd), device_id_type=MESH)

    sources = (
        (pos_hbm, pos_ref),
        (owner_hbm, owner_ref),
        (spot_hbm, spot_ref),
        (vel_hbm, vel_ref),
        (halo_hbm, halo_smem),
        (slot_hbm, slot_ref),
        (pair_hbm, pair_ref),
        (pair_hbm, pair_smem),
        (active_hbm, active_ref),
        (cb_hbm, cb_ref),
        (cb_hbm, cb_smem),
        (stress_hbm, stress_ref),
        (mass_hbm, mass_ref),
    )
    loads = []
    for n, (source, target) in enumerate(sources):
        copy = pltpu.make_async_copy(source, target, in_sems.at[n])
        copy.start()
        loads.append(copy)
    for copy in loads[:3]:
        copy.wait()
    sub_iota = lax.broadcasted_iota(jnp.int32, (ROWS, LANES), 0)
    lane_iota = lax.broadcasted_iota(jnp.int32, (ROWS, LANES), 1)
    owner = owner_ref[...]
    step_of = lax.rem(lax.rem(owner, doms) - d + 1 + doms, doms)
    goal = (lax.div(owner, doms) * 3 + step_of) * ROWS + lax.rem(spot_ref[...], ROWS)
    goal = jnp.where(owner >= 0, goal, -1)
    places = groups * 3 * ROWS
    chosen = (
        lax.broadcasted_iota(jnp.int32, (places, blocks), 0) == goal
    ).astype(jnp.float32)
    everywhere = jnp.concatenate([pos_ref[c] for c in range(3)], 1)
    packed = pick_rows(chosen, everywhere, 3)
    for c in range(3):
        out_buf[:, :, c, :, :] = packed[:, c * LANES : (c + 1) * LANES].reshape(
            groups, 3, ROWS, LANES
        )
    pl.semaphore_wait(barrier, len(partners))

    forward = []
    for turn, k, step, dd in partners:
        copy = pltpu.make_async_remote_copy(
            src_ref=out_buf.at[k, step],
            dst_ref=in_buf.at[step, g],
            send_sem=fwd_send.at[turn, step],
            recv_sem=fwd_recv.at[turn, step],
            device_id=(k, dd),
            device_id_type=MESH,
        )
        copy.start()
        forward.append(copy)
    in_buf[1, g] = out_buf[g, 1]

    for copy in loads[3:5]:
        copy.wait()
    halo = halo_smem[0, 0]
    state_rows = state.reshape((blocks + 1) * ROWS, LANES)
    for c in range(3):
        state_rows[pl.ds(c, blocks, stride=ROWS), :] = pos_ref[c]
        state_rows[pl.ds(3 + c, blocks, stride=ROWS), :] = vel_ref[c]
    rim[...] = state[halo]
    rim_copy = pltpu.make_async_remote_copy(
        src_ref=rim,
        dst_ref=ghost_in,
        send_sem=rim_sems.at[0],
        recv_sem=rim_sems.at[1],
        device_id=(g, left),
        device_id_type=MESH,
    )
    rim_copy.start()
    for copy in loads[5:]:
        copy.wait()
    goers = jnp.transpose(jnp.concatenate([chosen, jnp.zeros((LANES - places, blocks), jnp.float32)], 0))

    wide_iota = lax.broadcasted_iota(jnp.int32, (LANES, LANES), 1)
    for half in range(4 * blocks // LANES):
        rows = pl.ds(half * LANES, LANES)
        keys = jnp.transpose((slot_ref[rows, :] * LANES + wide_iota).astype(jnp.float32))
        keys = sort_rows([keys[r * ROWS : (r + 1) * ROWS, :] for r in range(16)], sub_iota)
        for r in range(16):
            sort_buf[half, pl.ds(r, ROWS, stride=16), :] = keys[r]
        inverse[rows, :] = jnp.transpose(sort_buf[half]).astype(jnp.int32) - wide_iota * LANES

    slot_iota = lax.broadcasted_iota(jnp.int32, (slots, tiles), 0)
    gain = PENALTY * active_ref[...].astype(jnp.float32)
    take_near = jnp.where(slot_iota == pair_ref[0:1, :], gain, 0.0).astype(BF16)
    take_far = jnp.where(slot_iota == pair_ref[1:2, :], -gain, 0.0).astype(BF16)
    tile_iota = lax.broadcasted_iota(jnp.int32, (tiles, 2 * LANES), 0)
    column = lax.broadcasted_iota(jnp.int32, (tiles, 2 * LANES), 1)
    same = ((column & (LANES - 1)) == tile_iota).astype(BF16)
    take_near = jnp.dot(take_near, same, preferred_element_type=jnp.float32).astype(BF16)
    tile_iota = lax.broadcasted_iota(jnp.int32, (tiles, tiles * ROWS), 0)
    column = lax.broadcasted_iota(jnp.int32, (tiles, tiles * ROWS), 1)
    same = (lax.div(column, ROWS) == tile_iota).astype(BF16)
    take_far = jnp.dot(take_far, same, preferred_element_type=jnp.float32)
    near_sums[...] = jnp.zeros_like(near_sums)
    depth = lax.broadcasted_iota(jnp.int32, (LANES, LANES), 0)
    depth = jnp.where(depth < 3 * slots, lax.rem(depth, slots), -1)

    def pick(t, carry):
        near_pick[t] = (depth == pair_smem[0, t]).astype(jnp.float32).astype(BF16)
        return carry

    lax.fori_loop(0, tiles, pick, 0)

    for copy in forward:
        copy.wait_recv()
    cols = (cols_even, cols_odd)
    held = (held_even, held_odd)
    canon_rows = canon.reshape(slots * ROWS, LANES)
    split = []
    for c in range(3):
        layers = []
        for layer in range(groups):
            rows = in_buf[0, layer, c] + in_buf[1, layer, c] + in_buf[2, layer, c]
            canon_rows[pl.ds(layer * ROWS * ROWS + c, ROWS, stride=ROWS), :] = rows
            layers.append(rows)
        value = jnp.concatenate(layers, 0)
        top = value.astype(BF16).astype(jnp.float32)
        rest = value - top
        middle = rest.astype(BF16).astype(jnp.float32)
        stack = jnp.concatenate([top, middle, rest - middle, jnp.zeros_like(value)], 0)
        split.append(jnp.transpose(stack).astype(BF16))
    split = jnp.concatenate(split, 0)

    def broadcasts(step, cols):
        for u in range(UNROLL):
            cols[u] = jnp.dot(
                split, near_pick[step * UNROLL + u], preferred_element_type=jnp.float32
            )

    def lane_sums(step, held):
        for c in range(3):
            for r in range(LANES // ROWS):
                rows = pl.ds(c * LANES + r * ROWS, ROWS)
                value = near_sums[rows, :]
                for u in range(UNROLL):
                    total = jnp.sum(held[u, rows, :], 1, keepdims=True)
                    value = jnp.where(lane_iota == step * UNROLL + u, total, value)
                near_sums[rows, :] = value

    def pushes(step, cols, held):
        for u in range(UNROLL):
            t = step * UNROLL + u
            far_block = canon[pair_smem[1, t]]
            far = [jnp.broadcast_to(far_block[c : c + 1, :], (ROWS, LANES)) for c in range(3)]
            far_sum = [None] * 3
            for r in range(LANES // ROWS):
                rows = [pl.ds(c * LANES + r * ROWS, ROWS) for c in range(3)]
                diff = [cols[u, rows[c], :] - far[c] for c in range(3)]
                weight = jnp.maximum(REACH - inner_rows(diff, diff), 0.0)
                for c in range(3):
                    push = weight * diff[c]
                    held[u, rows[c], :] = push
                    far_sum[c] = far_sum[c] + push if r else push
            place = pl.ds(pl.multiple_of(t * ROWS, ROWS), ROWS)
            for c in range(3):
                far_sums[place, c * LANES : (c + 1) * LANES] = far_sum[c]

    def tile_steps(half, carry):
        for phase in range(2):
            step = half * 2 + phase
            lane_sums(step - 1, held[1 - phase])
            pushes(step, cols[phase], held[phase])
            broadcasts(step + 1, cols[1 - phase])
        return carry

    steps = tiles // UNROLL
    broadcasts(0, cols[0])
    lax.fori_loop(0, steps // 2, tile_steps, 0)
    lane_sums(steps - 1, held[1])
    total = pick_rows(take_far, far_sums[...], 2)
    near_total = []
    for c in range(3):
        value = near_sums[pl.ds(c * LANES, LANES), :]
        top = value.astype(BF16)
        low = (value - top.astype(jnp.float32)).astype(BF16)
        near_total.append(
            lax.dot_general(
                take_near,
                jnp.concatenate([top, low], 1),
                (((1,), (1,)), ((), ())),
                preferred_element_type=jnp.float32,
            )
        )
    total = total + jnp.concatenate(near_total, 1)
    for c in range(3):
        ans[:, c, :, :] = total[:, c * LANES : (c + 1) * LANES].reshape(groups, ROWS, LANES)
    backward = []
    for turn, k, step, dd in partners:
        copy = pltpu.make_async_remote_copy(
            src_ref=ans.at[k],
            dst_ref=ret.at[g, 2 - step],
            send_sem=back_send.at[turn, step],
            recv_sem=back_recv.at[turn, step],
            device_id=(k, dd),
            device_id_type=MESH,
        )
        copy.start()
        backward.append(copy)
    ret[g, 1] = ans[g]

    rim_copy.wait_recv()
    state[blocks] = ghost_in[...]

    def elements(part, carry):
        here = pl.ds(pl.multiple_of(part * ROWS, ROWS), ROWS)
        for side in range(2):
            for kk in range(ROWS):
                b = cb_smem[side, part * ROWS + kk]
                corner_buf[side, pl.ds(kk * ROWS, ROWS), :] = state[b]
        pos = [None] * 4
        vel = [None] * 4
        for side, pair in enumerate(((0, 3), (1, 2))):
            column = [corner_buf[side, pl.ds(x, ROWS, stride=ROWS), :] for x in range(6)]
            for c in pair:
                ids = slot_ref[pl.ds(part * ROWS * 4 + c, ROWS, stride=4), :]
                picked = [gather_lanes(value, ids) for value in column]
                pos[c] = picked[:3]
                vel[c] = picked[3:]
        old = [stress_ref[x, here, :] for x in range(3)]
        forces, new = shell_forces(pos, vel, old)
        for x in range(3):
            stress_out[x, here, :] = new[x]
            for side, pair in enumerate(((0, 3), (1, 2))):
                spread[side, x, here, :] = sum(
                    gather_lanes(forces[c][x], inverse[pl.ds(part * ROWS * 4 + c, ROWS, stride=4), :]) for c in pair
                )
        return carry

    lax.fori_loop(0, blocks // ROWS, elements, 0)

    block_iota = lax.broadcasted_iota(jnp.int32, (blocks + ROWS, blocks), 0)
    hits = jnp.concatenate(
        [(block_iota == cb_ref[side : side + 1, :]).astype(jnp.float32) for side in range(2)], 1
    )
    both = jnp.concatenate(
        [
            jnp.concatenate([spread[side, c] for c in range(3)], 1)
            for side in range(2)
        ],
        0,
    )
    internal = pick_rows(hits, both, 2)
    for c in range(3):
        push_out[pl.ds(c, 1), :] = internal[blocks : blocks + 1, c * LANES : (c + 1) * LANES]
    push_copy = pltpu.make_async_remote_copy(
        src_ref=push_out,
        dst_ref=push_in,
        send_sem=push_sems.at[0],
        recv_sem=push_sems.at[1],
        device_id=(g, right),
        device_id_type=MESH,
    )
    push_copy.start()

    for copy in backward:
        copy.wait_recv()
    answers = jnp.concatenate(
        [ret[:, :, c, :, :].reshape(places, LANES) for c in range(3)], 1
    )
    answers = jnp.concatenate([answers, jnp.zeros((LANES - places, 3 * LANES), jnp.float32)], 0)
    contact = pick_rows(goers, answers, 2)
    push_copy.wait_recv()
    is_rim = lax.broadcasted_iota(jnp.int32, (blocks, LANES), 0) == halo
    factor = DT / mass_ref[...]
    for c in range(3):
        extra = jnp.where(is_rim, push_in[pl.ds(c, 1), :], 0.0)
        cols = slice(c * LANES, (c + 1) * LANES)
        force = contact[:, cols] - internal[0:blocks, cols] - extra
        vel_out[c] = vel_ref[c] + factor * force
    rim_copy.wait_send()
    push_copy.wait_send()
    for copy in forward:
        copy.wait_send()
    for copy in backward:
        copy.wait_send()


def local(
    positions,
    velocity,
    mass,
    stress,
    corner_block,
    corner_slot,
    halo_block,
    contact_owner,
    contact_slot,
    tile_pairs,
    tile_active,
):
    groups = lax.axis_size("group")
    doms = lax.axis_size("dom")
    blocks = corner_block.shape[2]
    nodes = positions.shape[2]
    tiles = tile_pairs.shape[2]
    slots = groups * ROWS
    vmem = pl.BlockSpec(memory_space=pltpu.VMEM)
    i32 = jnp.int32
    f32 = jnp.float32
    out = pl.pallas_call(
        functools.partial(kernel, groups, doms),
        out_shape=[jax.ShapeDtypeStruct((3, blocks, LANES), f32)] * 2,
        in_specs=[pl.BlockSpec(memory_space=pltpu.HBM)] * 11,
        out_specs=[vmem] * 2,
        scratch_shapes=[
            pltpu.VMEM((3, blocks, LANES), f32),
            pltpu.VMEM((3, blocks, LANES), f32),
            pltpu.VMEM((blocks, LANES), f32),
            pltpu.VMEM((3, blocks, LANES), f32),
            pltpu.VMEM((4 * blocks, LANES), i32),
            pltpu.VMEM((4, blocks), i32),
            pltpu.VMEM((1, blocks), i32),
            pltpu.VMEM((1, blocks), i32),
            pltpu.VMEM((2, tiles), i32),
            pltpu.VMEM((1, tiles), i32),
            pltpu.SMEM((4, blocks), i32),
            pltpu.SMEM((2, tiles), i32),
            pltpu.SMEM((1, 1), i32),
            pltpu.SemaphoreType.DMA((13,)),
            pltpu.VMEM((blocks + 1, ROWS, LANES), f32),
            pltpu.VMEM((ROWS, LANES), f32),
            pltpu.VMEM((ROWS, LANES), f32),
            pltpu.VMEM((groups, 3, 3, ROWS, LANES), f32),
            pltpu.VMEM((3, groups, 3, ROWS, LANES), f32),
            pltpu.VMEM((groups, 3, ROWS, LANES), f32),
            pltpu.VMEM((groups, 3, 3, ROWS, LANES), f32),
            pltpu.VMEM((slots, ROWS, LANES), f32),
            pltpu.VMEM((tiles + UNROLL, LANES, LANES), jnp.bfloat16),
            pltpu.VMEM((UNROLL, 3 * LANES, LANES), f32),
            pltpu.VMEM((UNROLL, 3 * LANES, LANES), f32),
            pltpu.VMEM((UNROLL, 3 * LANES, LANES), f32),
            pltpu.VMEM((UNROLL, 3 * LANES, LANES), f32),
            pltpu.VMEM((3 * LANES, LANES), f32),
            pltpu.VMEM((tiles * ROWS, 3 * LANES), f32),
            pltpu.VMEM((4 * blocks, LANES), jnp.int32),
            pltpu.VMEM((4 * blocks // LANES, LANES, LANES), f32),
            pltpu.VMEM((2, ROWS * ROWS, LANES), f32),
            pltpu.VMEM((2, 3, blocks, LANES), f32),
            pltpu.VMEM((ROWS, LANES), f32),
            pltpu.VMEM((ROWS, LANES), f32),
            pltpu.SemaphoreType.DMA((groups, 3)),
            pltpu.SemaphoreType.DMA((groups, 3)),
            pltpu.SemaphoreType.DMA((groups, 3)),
            pltpu.SemaphoreType.DMA((groups, 3)),
            pltpu.SemaphoreType.DMA((2,)),
            pltpu.SemaphoreType.DMA((2,)),
        ],
        compiler_params=pltpu.CompilerParams(
            collective_id=0, has_side_effects=True, vmem_limit_bytes=60 * 1024 * 1024
        ),
        name="shell_step",
    )(
        positions.reshape(3, blocks, LANES),
        velocity.reshape(3, blocks, LANES),
        mass.reshape(blocks, LANES),
        stress.reshape(3, blocks, LANES),
        corner_slot.reshape(4, blocks, LANES).transpose(1, 0, 2).reshape(4 * blocks, LANES),
        corner_block.reshape(4, blocks),
        contact_owner,
        contact_slot,
        tile_pairs.reshape(2, tiles),
        tile_active,
        halo_block,
    )
    return out[0].reshape(1, 3, nodes), out[1].reshape(1, 3, nodes)


def solution(mesh):
    in_specs = (
        P("group", None, "dom"),
        P("group", None, "dom"),
        P("group", "dom"),
        P("group", None, "dom"),
        P("group", None, "dom"),
        P("group", None, "dom"),
        P("group", "dom"),
        P("group", "dom"),
        P("group", "dom"),
        P("group", None, "dom"),
        P("group", "dom"),
    )
    out_specs = (P("group", None, "dom"), P("group", None, "dom"))
    return jax.shard_map(local, mesh=mesh, in_specs=in_specs, out_specs=out_specs, check_vma=False)
```

```python
import functools

import jax
import jax.numpy as jnp
from jax import lax
from jax.experimental import pallas as pl
from jax.experimental.pallas import tpu as pltpu
from jax.sharding import PartitionSpec as P

LANES = 128
ROWS = 8
DT = 0.5
STIFF = 2.0
POISSON = 0.3
HOURGLASS = 0.1
PENALTY = 4.0
REACH = 1.0
MESH = pl.DeviceIdType.MESH
HIGHEST = lax.Precision.HIGHEST
BF16 = jnp.bfloat16
UNROLL = 2


def inner_rows(a, b):
    return a[0] * b[0] + a[1] * b[1] + a[2] * b[2]


def cross_rows(a, b):
    return (
        a[1] * b[2] - a[2] * b[1],
        a[2] * b[0] - a[0] * b[2],
        a[0] * b[1] - a[1] * b[0],
    )


def minus(a, b):
    return tuple(x - y for x, y in zip(a, b))


def scaled(a, s):
    return tuple(x * s for x in a)


def gather_lanes(value, index):
    return jnp.take_along_axis(value, index, axis=1, mode="promise_in_bounds")


def pieces(value, count):
    parts = []
    for _ in range(count - 1):
        top = value.astype(BF16).astype(jnp.float32)
        parts.append(top)
        value = value - top
    parts.append(value)
    return jnp.concatenate(parts, 0).astype(BF16)


def pick_rows(chosen, value, count):
    lhs = jnp.concatenate([chosen] * count, 1).astype(BF16)
    return jnp.dot(lhs, pieces(value, count), preferred_element_type=jnp.float32)


def sort_rows(rows, sub):
    rows = list(rows)
    for k in range(1, 8):
        up = None if k < 4 or k == 7 else (sub & (1 << (k - 4))) == 0
        for j in range(k - 1, -1, -1):
            if j >= 4:
                gap = 1 << (j - 4)
                keep = (sub & gap) == 0
                if up is not None:
                    keep = keep == up
                for r in range(16):
                    other = jnp.take_along_axis(
                        rows[r], sub ^ gap, axis=0, mode="promise_in_bounds"
                    )
                    rows[r] = jnp.where(
                        keep, jnp.minimum(rows[r], other), jnp.maximum(rows[r], other)
                    )
                continue
            for r in range(16):
                far = r | (1 << j)
                if far == r:
                    continue
                low = jnp.minimum(rows[r], rows[far])
                high = jnp.maximum(rows[r], rows[far])
                if up is not None:
                    low, high = jnp.where(up, low, high), jnp.where(up, high, low)
                elif k < 4 and r & (1 << k):
                    low, high = high, low
                rows[r], rows[far] = low, high
    return rows


def shell_forces(pos, vel, stress_old):
    diag_a = minus(pos[2], pos[0])
    diag_b = minus(pos[3], pos[1])
    normal = cross_rows(diag_a, diag_b)
    inv_j = lax.rsqrt(inner_rows(normal, normal))
    axis_three = scaled(normal, inv_j)
    tangent = minus(diag_a, diag_b)
    tangent = minus(tangent, scaled(axis_three, inner_rows(tangent, axis_three)))
    axis_one = scaled(tangent, lax.rsqrt(inner_rows(tangent, tangent)))
    axis_two = cross_rows(axis_three, axis_one)
    along_a = inner_rows(diag_a, axis_one)
    across_a = inner_rows(diag_a, axis_two)
    along_b = inner_rows(diag_b, axis_one)
    across_b = inner_rows(diag_b, axis_two)
    speed_a = minus(vel[2], vel[0])
    speed_b = minus(vel[3], vel[1])
    slide_a = inner_rows(speed_a, axis_one)
    lift_a = inner_rows(speed_a, axis_two)
    slide_b = inner_rows(speed_b, axis_one)
    lift_b = inner_rows(speed_b, axis_two)
    rate_xx = (across_b * slide_a - across_a * slide_b) * inv_j
    rate_yy = (along_a * lift_b - along_b * lift_a) * inv_j
    rate_xy = (
        across_b * lift_a - across_a * lift_b + along_a * slide_b - along_b * slide_a
    ) * inv_j
    s_xx = stress_old[0] + (DT * STIFF) * (rate_xx + POISSON * rate_yy)
    s_yy = stress_old[1] + (DT * STIFF) * (POISSON * rate_xx + rate_yy)
    s_xy = stress_old[2] + (DT * STIFF * 0.5 * (1.0 - POISSON)) * rate_xy
    half_xx, half_yy, half_xy = 0.5 * s_xx, 0.5 * s_yy, 0.5 * s_xy
    fx0 = along_b * half_xy - across_b * half_xx
    fy0 = along_b * half_yy - across_b * half_xy
    fx1 = across_a * half_xx - along_a * half_xy
    fy1 = across_a * half_xy - along_a * half_yy
    forces = [[], [], [], []]
    for c in range(3):
        mode = HOURGLASS * (vel[0][c] - vel[1][c] + vel[2][c] - vel[3][c])
        first = fx0 * axis_one[c] + fy0 * axis_two[c]
        second = fx1 * axis_one[c] + fy1 * axis_two[c]
        forces[0].append(mode + first)
        forces[1].append(second - mode)
        forces[2].append(mode - first)
        forces[3].append(-mode - second)
    return forces, (s_xx, s_yy, s_xy)


def kernel(
    groups,
    doms,
    pos_hbm,
    vel_hbm,
    mass_hbm,
    stress_hbm,
    slot_hbm,
    cb_hbm,
    owner_hbm,
    spot_hbm,
    pair_hbm,
    active_hbm,
    halo_hbm,
    vel_out,
    stress_out,
    pos_ref,
    vel_ref,
    mass_ref,
    stress_ref,
    slot_ref,
    cb_ref,
    owner_ref,
    spot_ref,
    pair_ref,
    active_ref,
    cb_smem,
    pair_smem,
    halo_smem,
    in_sems,
    state,
    rim,
    ghost_in,
    out_buf,
    in_buf,
    ans,
    ret,
    canon,
    near_pick,
    cols_even,
    cols_odd,
    held_even,
    held_odd,
    near_sums,
    far_sums,
    inverse,
    sort_buf,
    corner_buf,
    spread,
    push_out,
    push_in,
    fwd_send,
    fwd_recv,
    back_send,
    back_recv,
    rim_sems,
    push_sems,
):
    g = lax.axis_index("group")
    d = lax.axis_index("dom")
    blocks = mass_ref.shape[0]
    tiles = pair_ref.shape[1]
    slots = groups * ROWS
    left = lax.rem(d + doms - 1, doms)
    right = lax.rem(d + 1, doms)
    partners = []
    for turn in (2, 1, 3, 0):
        k = lax.rem(g + turn, groups)
        for step, dd in ((0, left), (1, d), (2, right)):
            if turn == 0 and step == 1:
                continue
            partners.append((turn, k, step, dd))

    barrier = pltpu.get_barrier_semaphore()
    for turn, k, step, dd in partners:
        pl.semaphore_signal(barrier, inc=1, device_id=(k, dd), device_id_type=MESH)

    sources = (
        (pos_hbm, pos_ref),
        (owner_hbm, owner_ref),
        (spot_hbm, spot_ref),
        (vel_hbm, vel_ref),
        (halo_hbm, halo_smem),
        (slot_hbm, slot_ref),
        (pair_hbm, pair_ref),
        (pair_hbm, pair_smem),
        (active_hbm, active_ref),
        (cb_hbm, cb_ref),
        (cb_hbm, cb_smem),
        (stress_hbm, stress_ref),
        (mass_hbm, mass_ref),
    )
    loads = []
    for n, (source, target) in enumerate(sources):
        copy = pltpu.make_async_copy(source, target, in_sems.at[n])
        copy.start()
        loads.append(copy)
    for copy in loads[:3]:
        copy.wait()
    sub_iota = lax.broadcasted_iota(jnp.int32, (ROWS, LANES), 0)
    lane_iota = lax.broadcasted_iota(jnp.int32, (ROWS, LANES), 1)
    owner = owner_ref[...]
    step_of = lax.rem(lax.rem(owner, doms) - d + 1 + doms, doms)
    goal = (lax.div(owner, doms) * 3 + step_of) * ROWS + lax.rem(spot_ref[...], ROWS)
    goal = jnp.where(owner >= 0, goal, -1)
    places = groups * 3 * ROWS
    chosen = (
        lax.broadcasted_iota(jnp.int32, (places, blocks), 0) == goal
    ).astype(jnp.float32)
    everywhere = jnp.concatenate([pos_ref[c] for c in range(3)], 1)
    packed = pick_rows(chosen, everywhere, 3)
    for c in range(3):
        out_buf[:, :, c, :, :] = packed[:, c * LANES : (c + 1) * LANES].reshape(
            groups, 3, ROWS, LANES
        )
    pl.semaphore_wait(barrier, len(partners))

    forward = []
    for turn, k, step, dd in partners:
        copy = pltpu.make_async_remote_copy(
            src_ref=out_buf.at[k, step],
            dst_ref=in_buf.at[step, g],
            send_sem=fwd_send.at[turn, step],
            recv_sem=fwd_recv.at[turn, step],
            device_id=(k, dd),
            device_id_type=MESH,
        )
        copy.start()
        forward.append(copy)
    in_buf[1, g] = out_buf[g, 1]

    for copy in loads[3:5]:
        copy.wait()
    halo = halo_smem[0, 0]
    state_rows = state.reshape((blocks + 1) * ROWS, LANES)
    for c in range(3):
        state_rows[pl.ds(c, blocks, stride=ROWS), :] = pos_ref[c]
        state_rows[pl.ds(3 + c, blocks, stride=ROWS), :] = vel_ref[c]
    rim[...] = state[halo]
    rim_copy = pltpu.make_async_remote_copy(
        src_ref=rim,
        dst_ref=ghost_in,
        send_sem=rim_sems.at[0],
        recv_sem=rim_sems.at[1],
        device_id=(g, left),
        device_id_type=MESH,
    )
    rim_copy.start()
    for copy in loads[5:]:
        copy.wait()
    goers = jnp.transpose(jnp.concatenate([chosen, jnp.zeros((LANES - places, blocks), jnp.float32)], 0))

    wide_iota = lax.broadcasted_iota(jnp.int32, (LANES, LANES), 1)
    for half in range(4 * blocks // LANES):
        rows = pl.ds(half * LANES, LANES)
        keys = jnp.transpose((slot_ref[rows, :] * LANES + wide_iota).astype(jnp.float32))
        keys = sort_rows([keys[r * ROWS : (r + 1) * ROWS, :] for r in range(16)], sub_iota)
        for r in range(16):
            sort_buf[half, pl.ds(r, ROWS, stride=16), :] = keys[r]
        inverse[rows, :] = jnp.transpose(sort_buf[half]).astype(jnp.int32) - wide_iota * LANES

    slot_iota = lax.broadcasted_iota(jnp.int32, (slots, tiles), 0)
    gain = PENALTY * active_ref[...].astype(jnp.float32)
    take_near = jnp.where(slot_iota == pair_ref[0:1, :], gain, 0.0).astype(BF16)
    take_far = jnp.where(slot_iota == pair_ref[1:2, :], -gain, 0.0).astype(BF16)
    tile_iota = lax.broadcasted_iota(jnp.int32, (tiles, 2 * LANES), 0)
    column = lax.broadcasted_iota(jnp.int32, (tiles, 2 * LANES), 1)
    same = ((column & (LANES - 1)) == tile_iota).astype(BF16)
    take_near = jnp.dot(take_near, same, preferred_element_type=jnp.float32).astype(BF16)
    tile_iota = lax.broadcasted_iota(jnp.int32, (tiles, tiles * ROWS), 0)
    column = lax.broadcasted_iota(jnp.int32, (tiles, tiles * ROWS), 1)
    same = (lax.div(column, ROWS) == tile_iota).astype(BF16)
    take_far = jnp.dot(take_far, same, preferred_element_type=jnp.float32)
    near_sums[...] = jnp.zeros_like(near_sums)
    depth = lax.broadcasted_iota(jnp.int32, (LANES, LANES), 0)
    depth = jnp.where(depth < 3 * slots, lax.rem(depth, slots), -1)

    def pick(t, carry):
        near_pick[t] = (depth == pair_smem[0, t]).astype(jnp.float32).astype(BF16)
        return carry

    lax.fori_loop(0, tiles, pick, 0)

    for copy in forward:
        copy.wait_recv()
    cols = (cols_even, cols_odd)
    held = (held_even, held_odd)
    canon_rows = canon.reshape(slots * ROWS, LANES)
    split = []
    for c in range(3):
        layers = []
        for layer in range(groups):
            rows = in_buf[0, layer, c] + in_buf[1, layer, c] + in_buf[2, layer, c]
            canon_rows[pl.ds(layer * ROWS * ROWS + c, ROWS, stride=ROWS), :] = rows
            layers.append(rows)
        value = jnp.concatenate(layers, 0)
        top = value.astype(BF16).astype(jnp.float32)
        rest = value - top
        middle = rest.astype(BF16).astype(jnp.float32)
        stack = jnp.concatenate([top, middle, rest - middle, jnp.zeros_like(value)], 0)
        split.append(jnp.transpose(stack).astype(BF16))
    split = jnp.concatenate(split, 0)

    def broadcasts(step, cols):
        for u in range(UNROLL):
            cols[u] = jnp.dot(
                split, near_pick[step * UNROLL + u], preferred_element_type=jnp.float32
            )

    def lane_sums(step, held):
        for c in range(3):
            for r in range(LANES // ROWS):
                rows = pl.ds(c * LANES + r * ROWS, ROWS)
                value = near_sums[rows, :]
                for u in range(UNROLL):
                    total = jnp.sum(held[u, rows, :], 1, keepdims=True)
                    value = jnp.where(lane_iota == step * UNROLL + u, total, value)
                near_sums[rows, :] = value

    def pushes(step, cols, held):
        for u in range(UNROLL):
            t = step * UNROLL + u
            far_block = canon[pair_smem[1, t]]
            far = [jnp.broadcast_to(far_block[c : c + 1, :], (ROWS, LANES)) for c in range(3)]
            far_sum = [None] * 3
            for r in range(LANES // ROWS):
                rows = [pl.ds(c * LANES + r * ROWS, ROWS) for c in range(3)]
                diff = [cols[u, rows[c], :] - far[c] for c in range(3)]
                weight = jnp.maximum(REACH - inner_rows(diff, diff), 0.0)
                for c in range(3):
                    push = weight * diff[c]
                    held[u, rows[c], :] = push
                    far_sum[c] = far_sum[c] + push if r else push
            place = pl.ds(pl.multiple_of(t * ROWS, ROWS), ROWS)
            for c in range(3):
                far_sums[place, c * LANES : (c + 1) * LANES] = far_sum[c]

    def tile_steps(half, carry):
        for phase in range(2):
            step = half * 2 + phase
            lane_sums(step - 1, held[1 - phase])
            pushes(step, cols[phase], held[phase])
            broadcasts(step + 1, cols[1 - phase])
        return carry

    steps = tiles // UNROLL
    broadcasts(0, cols[0])
    lax.fori_loop(0, steps // 2, tile_steps, 0)
    lane_sums(steps - 1, held[1])
    total = pick_rows(take_far, far_sums[...], 2)
    near_total = []
    for c in range(3):
        value = near_sums[pl.ds(c * LANES, LANES), :]
        top = value.astype(BF16)
        low = (value - top.astype(jnp.float32)).astype(BF16)
        near_total.append(
            lax.dot_general(
                take_near,
                jnp.concatenate([top, low], 1),
                (((1,), (1,)), ((), ())),
                preferred_element_type=jnp.float32,
            )
        )
    total = total + jnp.concatenate(near_total, 1)
    for c in range(3):
        ans[:, c, :, :] = total[:, c * LANES : (c + 1) * LANES].reshape(groups, ROWS, LANES)
    backward = []
    for turn, k, step, dd in partners:
        copy = pltpu.make_async_remote_copy(
            src_ref=ans.at[k],
            dst_ref=ret.at[g, 2 - step],
            send_sem=back_send.at[turn, step],
            recv_sem=back_recv.at[turn, step],
            device_id=(k, dd),
            device_id_type=MESH,
        )
        copy.start()
        backward.append(copy)
    ret[g, 1] = ans[g]

    rim_copy.wait_recv()
    state[blocks] = ghost_in[...]

    def elements(part, carry):
        here = pl.ds(pl.multiple_of(part * ROWS, ROWS), ROWS)
        for side in range(2):
            for kk in range(ROWS):
                b = cb_smem[side, part * ROWS + kk]
                corner_buf[side, pl.ds(kk * ROWS, ROWS), :] = state[b]
        pos = [None] * 4
        vel = [None] * 4
        for side, pair in enumerate(((0, 3), (1, 2))):
            column = [corner_buf[side, pl.ds(x, ROWS, stride=ROWS), :] for x in range(6)]
            for c in pair:
                ids = slot_ref[pl.ds(part * ROWS * 4 + c, ROWS, stride=4), :]
                picked = [gather_lanes(value, ids) for value in column]
                pos[c] = picked[:3]
                vel[c] = picked[3:]
        old = [stress_ref[x, here, :] for x in range(3)]
        forces, new = shell_forces(pos, vel, old)
        for x in range(3):
            stress_out[x, here, :] = new[x]
            for side, pair in enumerate(((0, 3), (1, 2))):
                spread[side, x, here, :] = sum(
                    gather_lanes(forces[c][x], inverse[pl.ds(part * ROWS * 4 + c, ROWS, stride=4), :]) for c in pair
                )
        return carry

    lax.fori_loop(0, blocks // ROWS, elements, 0)

    block_iota = lax.broadcasted_iota(jnp.int32, (blocks + ROWS, blocks), 0)
    hits = jnp.concatenate(
        [(block_iota == cb_ref[side : side + 1, :]).astype(jnp.float32) for side in range(2)], 1
    )
    both = jnp.concatenate(
        [
            jnp.concatenate([spread[side, c] for c in range(3)], 1)
            for side in range(2)
        ],
        0,
    )
    internal = pick_rows(hits, both, 2)
    for c in range(3):
        push_out[pl.ds(c, 1), :] = internal[blocks : blocks + 1, c * LANES : (c + 1) * LANES]
    push_copy = pltpu.make_async_remote_copy(
        src_ref=push_out,
        dst_ref=push_in,
        send_sem=push_sems.at[0],
        recv_sem=push_sems.at[1],
        device_id=(g, right),
        device_id_type=MESH,
    )
    push_copy.start()

    for copy in backward:
        copy.wait_recv()
    answers = jnp.concatenate(
        [ret[:, :, c, :, :].reshape(places, LANES) for c in range(3)], 1
    )
    answers = jnp.concatenate([answers, jnp.zeros((LANES - places, 3 * LANES), jnp.float32)], 0)
    contact = pick_rows(goers, answers, 2)
    push_copy.wait_recv()
    is_rim = lax.broadcasted_iota(jnp.int32, (blocks, LANES), 0) == halo
    factor = DT / mass_ref[...]
    for c in range(3):
        extra = jnp.where(is_rim, push_in[pl.ds(c, 1), :], 0.0)
        cols = slice(c * LANES, (c + 1) * LANES)
        force = contact[:, cols] - internal[0:blocks, cols] - extra
        vel_out[c] = vel_ref[c] + factor * force
    rim_copy.wait_send()
    push_copy.wait_send()
    for copy in forward:
        copy.wait_send()
    for copy in backward:
        copy.wait_send()


def local(
    positions,
    velocity,
    mass,
    stress,
    corner_block,
    corner_slot,
    halo_block,
    contact_owner,
    contact_slot,
    tile_pairs,
    tile_active,
):
    groups = lax.axis_size("group")
    doms = lax.axis_size("dom")
    blocks = corner_block.shape[2]
    nodes = positions.shape[2]
    tiles = tile_pairs.shape[2]
    slots = groups * ROWS
    vmem = pl.BlockSpec(memory_space=pltpu.VMEM)
    i32 = jnp.int32
    f32 = jnp.float32
    out = pl.pallas_call(
        functools.partial(kernel, groups, doms),
        out_shape=[jax.ShapeDtypeStruct((3, blocks, LANES), f32)] * 2,
        in_specs=[pl.BlockSpec(memory_space=pltpu.HBM)] * 11,
        out_specs=[vmem] * 2,
        scratch_shapes=[
            pltpu.VMEM((3, blocks, LANES), f32),
            pltpu.VMEM((3, blocks, LANES), f32),
            pltpu.VMEM((blocks, LANES), f32),
            pltpu.VMEM((3, blocks, LANES), f32),
            pltpu.VMEM((4 * blocks, LANES), i32),
            pltpu.VMEM((4, blocks), i32),
            pltpu.VMEM((1, blocks), i32),
            pltpu.VMEM((1, blocks), i32),
            pltpu.VMEM((2, tiles), i32),
            pltpu.VMEM((1, tiles), i32),
            pltpu.SMEM((4, blocks), i32),
            pltpu.SMEM((2, tiles), i32),
            pltpu.SMEM((1, 1), i32),
            pltpu.SemaphoreType.DMA((13,)),
            pltpu.VMEM((blocks + 1, ROWS, LANES), f32),
            pltpu.VMEM((ROWS, LANES), f32),
            pltpu.VMEM((ROWS, LANES), f32),
            pltpu.VMEM((groups, 3, 3, ROWS, LANES), f32),
            pltpu.VMEM((3, groups, 3, ROWS, LANES), f32),
            pltpu.VMEM((groups, 3, ROWS, LANES), f32),
            pltpu.VMEM((groups, 3, 3, ROWS, LANES), f32),
            pltpu.VMEM((slots, ROWS, LANES), f32),
            pltpu.VMEM((tiles + UNROLL, LANES, LANES), jnp.bfloat16),
            pltpu.VMEM((UNROLL, 3 * LANES, LANES), f32),
            pltpu.VMEM((UNROLL, 3 * LANES, LANES), f32),
            pltpu.VMEM((UNROLL, 3 * LANES, LANES), f32),
            pltpu.VMEM((UNROLL, 3 * LANES, LANES), f32),
            pltpu.VMEM((3 * LANES, LANES), f32),
            pltpu.VMEM((tiles * ROWS, 3 * LANES), f32),
            pltpu.VMEM((4 * blocks, LANES), jnp.int32),
            pltpu.VMEM((4 * blocks // LANES, LANES, LANES), f32),
            pltpu.VMEM((2, ROWS * ROWS, LANES), f32),
            pltpu.VMEM((2, 3, blocks, LANES), f32),
            pltpu.VMEM((ROWS, LANES), f32),
            pltpu.VMEM((ROWS, LANES), f32),
            pltpu.SemaphoreType.DMA((groups, 3)),
            pltpu.SemaphoreType.DMA((groups, 3)),
            pltpu.SemaphoreType.DMA((groups, 3)),
            pltpu.SemaphoreType.DMA((groups, 3)),
            pltpu.SemaphoreType.DMA((2,)),
            pltpu.SemaphoreType.DMA((2,)),
        ],
        compiler_params=pltpu.CompilerParams(
            collective_id=0, has_side_effects=True, vmem_limit_bytes=32 * 1024 * 1024
        ),
        name="shell_step",
    )(
        pltpu.with_memory_space_constraint(positions.reshape(3, blocks, LANES), pltpu.HBM),
        pltpu.with_memory_space_constraint(velocity.reshape(3, blocks, LANES), pltpu.HBM),
        pltpu.with_memory_space_constraint(mass.reshape(blocks, LANES), pltpu.HBM),
        pltpu.with_memory_space_constraint(stress.reshape(3, blocks, LANES), pltpu.HBM),
        pltpu.with_memory_space_constraint(corner_slot.reshape(4, blocks, LANES).transpose(1, 0, 2).reshape(4 * blocks, LANES), pltpu.HBM),
        pltpu.with_memory_space_constraint(corner_block.reshape(4, blocks), pltpu.HBM),
        pltpu.with_memory_space_constraint(contact_owner, pltpu.HBM),
        pltpu.with_memory_space_constraint(contact_slot, pltpu.HBM),
        pltpu.with_memory_space_constraint(tile_pairs.reshape(2, tiles), pltpu.HBM),
        pltpu.with_memory_space_constraint(tile_active, pltpu.HBM),
        halo_block,
    )
    return out[0].reshape(1, 3, nodes), out[1].reshape(1, 3, nodes)


def solution(mesh):
    in_specs = (
        P("group", None, "dom"),
        P("group", None, "dom"),
        P("group", "dom"),
        P("group", None, "dom"),
        P("group", None, "dom"),
        P("group", None, "dom"),
        P("group", "dom"),
        P("group", "dom"),
        P("group", "dom"),
        P("group", None, "dom"),
        P("group", "dom"),
    )
    out_specs = (P("group", None, "dom"), P("group", None, "dom"))
    return jax.shard_map(local, mesh=mesh, in_specs=in_specs, out_specs=out_specs, check_vma=False)
```

```python
import functools

import jax
import jax.numpy as jnp
from jax import lax
from jax.experimental import pallas as pl
from jax.experimental.pallas import tpu as pltpu
from jax.sharding import PartitionSpec as P

LANES = 128
ROWS = 8
DT = 0.5
STIFF = 2.0
POISSON = 0.3
HOURGLASS = 0.1
PENALTY = 4.0
REACH = 1.0
MESH = pl.DeviceIdType.MESH
HIGHEST = lax.Precision.HIGHEST
BF16 = jnp.bfloat16
UNROLL = 3


def inner_rows(a, b):
    return a[0] * b[0] + a[1] * b[1] + a[2] * b[2]


def cross_rows(a, b):
    return (
        a[1] * b[2] - a[2] * b[1],
        a[2] * b[0] - a[0] * b[2],
        a[0] * b[1] - a[1] * b[0],
    )


def minus(a, b):
    return tuple(x - y for x, y in zip(a, b))


def scaled(a, s):
    return tuple(x * s for x in a)


def gather_lanes(value, index):
    return jnp.take_along_axis(value, index, axis=1, mode="promise_in_bounds")


def pieces(value, count):
    parts = []
    for _ in range(count - 1):
        top = value.astype(BF16).astype(jnp.float32)
        parts.append(top)
        value = value - top
    parts.append(value)
    return jnp.concatenate(parts, 0).astype(BF16)


def pick_rows(chosen, value, count):
    lhs = jnp.concatenate([chosen] * count, 1).astype(BF16)
    return jnp.dot(lhs, pieces(value, count), preferred_element_type=jnp.float32)


def sort_rows(rows, sub):
    rows = list(rows)
    for k in range(1, 8):
        up = None if k < 4 or k == 7 else (sub & (1 << (k - 4))) == 0
        for j in range(k - 1, -1, -1):
            if j >= 4:
                gap = 1 << (j - 4)
                keep = (sub & gap) == 0
                if up is not None:
                    keep = keep == up
                for r in range(16):
                    other = jnp.take_along_axis(
                        rows[r], sub ^ gap, axis=0, mode="promise_in_bounds"
                    )
                    rows[r] = jnp.where(
                        keep, jnp.minimum(rows[r], other), jnp.maximum(rows[r], other)
                    )
                continue
            for r in range(16):
                far = r | (1 << j)
                if far == r:
                    continue
                low = jnp.minimum(rows[r], rows[far])
                high = jnp.maximum(rows[r], rows[far])
                if up is not None:
                    low, high = jnp.where(up, low, high), jnp.where(up, high, low)
                elif k < 4 and r & (1 << k):
                    low, high = high, low
                rows[r], rows[far] = low, high
    return rows


def shell_forces(pos, vel, stress_old):
    diag_a = minus(pos[2], pos[0])
    diag_b = minus(pos[3], pos[1])
    normal = cross_rows(diag_a, diag_b)
    inv_j = lax.rsqrt(inner_rows(normal, normal))
    axis_three = scaled(normal, inv_j)
    tangent = minus(diag_a, diag_b)
    tangent = minus(tangent, scaled(axis_three, inner_rows(tangent, axis_three)))
    axis_one = scaled(tangent, lax.rsqrt(inner_rows(tangent, tangent)))
    axis_two = cross_rows(axis_three, axis_one)
    along_a = inner_rows(diag_a, axis_one)
    across_a = inner_rows(diag_a, axis_two)
    along_b = inner_rows(diag_b, axis_one)
    across_b = inner_rows(diag_b, axis_two)
    speed_a = minus(vel[2], vel[0])
    speed_b = minus(vel[3], vel[1])
    slide_a = inner_rows(speed_a, axis_one)
    lift_a = inner_rows(speed_a, axis_two)
    slide_b = inner_rows(speed_b, axis_one)
    lift_b = inner_rows(speed_b, axis_two)
    rate_xx = (across_b * slide_a - across_a * slide_b) * inv_j
    rate_yy = (along_a * lift_b - along_b * lift_a) * inv_j
    rate_xy = (
        across_b * lift_a - across_a * lift_b + along_a * slide_b - along_b * slide_a
    ) * inv_j
    s_xx = stress_old[0] + (DT * STIFF) * (rate_xx + POISSON * rate_yy)
    s_yy = stress_old[1] + (DT * STIFF) * (POISSON * rate_xx + rate_yy)
    s_xy = stress_old[2] + (DT * STIFF * 0.5 * (1.0 - POISSON)) * rate_xy
    half_xx, half_yy, half_xy = 0.5 * s_xx, 0.5 * s_yy, 0.5 * s_xy
    fx0 = along_b * half_xy - across_b * half_xx
    fy0 = along_b * half_yy - across_b * half_xy
    fx1 = across_a * half_xx - along_a * half_xy
    fy1 = across_a * half_xy - along_a * half_yy
    forces = [[], [], [], []]
    for c in range(3):
        mode = HOURGLASS * (vel[0][c] - vel[1][c] + vel[2][c] - vel[3][c])
        first = fx0 * axis_one[c] + fy0 * axis_two[c]
        second = fx1 * axis_one[c] + fy1 * axis_two[c]
        forces[0].append(mode + first)
        forces[1].append(second - mode)
        forces[2].append(mode - first)
        forces[3].append(-mode - second)
    return forces, (s_xx, s_yy, s_xy)


def kernel(
    groups,
    doms,
    pos_hbm,
    vel_hbm,
    mass_hbm,
    stress_hbm,
    slot_hbm,
    cb_hbm,
    owner_hbm,
    spot_hbm,
    pair_hbm,
    active_hbm,
    halo_hbm,
    vel_out,
    stress_out,
    pos_ref,
    vel_ref,
    mass_ref,
    stress_ref,
    slot_ref,
    cb_ref,
    owner_ref,
    spot_ref,
    pair_ref,
    active_ref,
    cb_smem,
    info_smem,
    info_out,
    info_in,
    info_sems,
    halo_smem,
    in_sems,
    state,
    rim,
    ghost_in,
    out_buf,
    in_buf,
    ans,
    ret,
    canon,
    near_pick,
    held_even,
    held_odd,
    near_sums,
    far_sums,
    inverse,
    sort_buf,
    corner_buf,
    spread,
    push_out,
    push_in,
    fwd_send,
    fwd_recv,
    back_send,
    back_recv,
    rim_sems,
    push_sems,
):
    g = lax.axis_index("group")
    d = lax.axis_index("dom")
    blocks = mass_ref.shape[0]
    tiles = pair_ref.shape[1]
    slots = groups * ROWS
    left = lax.rem(d + doms - 1, doms)
    right = lax.rem(d + 1, doms)
    partners = []
    for step in (2, 1, 0):
        for turn in (2, 3, 1, 0):
            if turn == 0 and step == 0:
                continue
            partners.append((turn, lax.rem(g + turn, groups), step))

    barrier = pltpu.get_barrier_semaphore()
    greeted = 0
    for ahead in (2, 1, 0, doms - 1, doms - 2):
        for turn in (2, 3, 1, 0):
            if turn == 0 and ahead == 0:
                continue
            pl.semaphore_signal(
                barrier,
                inc=1,
                device_id=(lax.rem(g + turn, groups), lax.rem(d + ahead, doms)),
                device_id_type=MESH,
            )
            greeted += 1

    sources = (
        (pos_hbm, pos_ref),
        (owner_hbm, owner_ref),
        (spot_hbm, spot_ref),
        (pair_hbm, pair_ref),
        (active_hbm, active_ref),
        (vel_hbm, vel_ref),
        (halo_hbm, halo_smem),
        (slot_hbm, slot_ref),
        (cb_hbm, cb_ref),
        (cb_hbm, cb_smem),
        (stress_hbm, stress_ref),
        (mass_hbm, mass_ref),
    )
    loads = []
    for n, (source, target) in enumerate(sources):
        copy = pltpu.make_async_copy(source, target, in_sems.at[n])
        copy.start()
        loads.append(copy)
    for copy in loads[:3]:
        copy.wait()
    sub_iota = lax.broadcasted_iota(jnp.int32, (ROWS, LANES), 0)
    lane_iota = lax.broadcasted_iota(jnp.int32, (ROWS, LANES), 1)
    owner = owner_ref[...]
    step_of = lax.rem(lax.rem(owner, doms) - d + 1 + doms, doms)
    goal = (lax.div(owner, doms) * 3 + step_of) * ROWS + lax.rem(spot_ref[...], ROWS)
    goal = jnp.where(owner >= 0, goal, -1)
    places = groups * 3 * ROWS
    chosen = (
        lax.broadcasted_iota(jnp.int32, (places, blocks), 0) == goal
    ).astype(jnp.float32)
    everywhere = jnp.concatenate([pos_ref[c] for c in range(3)], 1)
    packed = pick_rows(chosen, everywhere, 3)
    for c in range(3):
        out_buf[:, :, c, :, :] = packed[:, c * LANES : (c + 1) * LANES].reshape(
            groups, 3, ROWS, LANES
        )
    for copy in loads[3:5]:
        copy.wait()
    info_out[0:2, 0:tiles] = pair_ref[...]
    info_out[2:3, 0:tiles] = active_ref[...]
    pl.semaphore_wait(barrier, greeted)

    info_copy = pltpu.make_async_remote_copy(
        src_ref=info_out,
        dst_ref=info_in,
        send_sem=info_sems.at[0],
        recv_sem=info_sems.at[1],
        device_id=(g, right),
        device_id_type=MESH,
    )
    info_copy.start()

    forward = []
    for turn, k, step in partners:
        copy = pltpu.make_async_remote_copy(
            src_ref=out_buf.at[k, step],
            dst_ref=in_buf.at[step, g],
            send_sem=fwd_send.at[turn, step],
            recv_sem=fwd_recv.at[turn, step],
            device_id=(k, lax.rem(d + step, doms)),
            device_id_type=MESH,
        )
        copy.start()
        forward.append(copy)
    in_buf[0, g] = out_buf[g, 0]

    for copy in loads[5:7]:
        copy.wait()
    halo = halo_smem[0, 0]
    state_rows = state.reshape((blocks + 1) * ROWS, LANES)
    for c in range(3):
        state_rows[pl.ds(c, blocks, stride=ROWS), :] = pos_ref[c]
        state_rows[pl.ds(3 + c, blocks, stride=ROWS), :] = vel_ref[c]
    rim[...] = state[halo]
    rim_copy = pltpu.make_async_remote_copy(
        src_ref=rim,
        dst_ref=ghost_in,
        send_sem=rim_sems.at[0],
        recv_sem=rim_sems.at[1],
        device_id=(g, left),
        device_id_type=MESH,
    )
    rim_copy.start()
    for copy in loads[7:]:
        copy.wait()
    goers = jnp.transpose(jnp.concatenate([chosen, jnp.zeros((LANES - places, blocks), jnp.float32)], 0))

    wide_iota = lax.broadcasted_iota(jnp.int32, (LANES, LANES), 1)
    for half in range(4 * blocks // LANES):
        rows = pl.ds(half * LANES, LANES)
        keys = jnp.transpose((slot_ref[rows, :] * LANES + wide_iota).astype(jnp.float32))
        keys = sort_rows([keys[r * ROWS : (r + 1) * ROWS, :] for r in range(16)], sub_iota)
        for r in range(16):
            sort_buf[half, pl.ds(r, ROWS, stride=16), :] = keys[r]
        inverse[rows, :] = jnp.transpose(sort_buf[half]).astype(jnp.int32) - wide_iota * LANES

    info_copy.wait_recv()
    to_smem = pltpu.make_async_copy(info_in, info_smem, info_sems.at[2])
    to_smem.start()
    to_smem.wait()
    slot_iota = lax.broadcasted_iota(jnp.int32, (slots, tiles), 0)
    gain = PENALTY * info_in[2:3, 0:tiles].astype(jnp.float32)
    take_near = jnp.where(slot_iota == info_in[0:1, 0:tiles], gain, 0.0).astype(BF16)
    take_far = jnp.where(slot_iota == info_in[1:2, 0:tiles], -gain, 0.0).astype(BF16)
    tile_iota = lax.broadcasted_iota(jnp.int32, (tiles, 2 * LANES), 0)
    column = lax.broadcasted_iota(jnp.int32, (tiles, 2 * LANES), 1)
    same = ((column & (LANES - 1)) == tile_iota).astype(BF16)
    take_near = jnp.dot(take_near, same, preferred_element_type=jnp.float32).astype(BF16)
    tile_iota = lax.broadcasted_iota(jnp.int32, (tiles, tiles * ROWS), 0)
    column = lax.broadcasted_iota(jnp.int32, (tiles, tiles * ROWS), 1)
    same = (lax.div(column, ROWS) == tile_iota).astype(BF16)
    take_far = jnp.dot(take_far, same, preferred_element_type=jnp.float32)
    near_sums[...] = jnp.zeros_like(near_sums)
    depth = lax.broadcasted_iota(jnp.int32, (LANES, LANES), 0)
    depth = jnp.where(depth < 3 * slots, lax.rem(depth, slots), -1)

    def pick(t, carry):
        near_pick[t] = (depth == info_smem[0, t]).astype(jnp.float32).astype(BF16)
        return carry

    lax.fori_loop(0, tiles, pick, 0)

    for copy in forward:
        copy.wait_recv()
    held = (held_even, held_odd)
    canon_rows = canon.reshape(slots * ROWS, LANES)
    split = []
    for c in range(3):
        layers = []
        for layer in range(groups):
            rows = in_buf[0, layer, c] + in_buf[1, layer, c] + in_buf[2, layer, c]
            canon_rows[pl.ds(layer * ROWS * ROWS + c, ROWS, stride=ROWS), :] = rows
            layers.append(rows)
        value = jnp.concatenate(layers, 0)
        top = value.astype(BF16).astype(jnp.float32)
        rest = value - top
        middle = rest.astype(BF16).astype(jnp.float32)
        stack = jnp.concatenate([top, middle, rest - middle, jnp.zeros_like(value)], 0)
        split.append(jnp.transpose(stack).astype(BF16))
    split = jnp.concatenate(
        [split[c][16 * r : 16 * r + 16] for r in range(LANES // 16) for c in range(3)], 0
    )

    def lane_sums(step, held):
        for c in range(3):
            for r in range(LANES // ROWS):
                rows = pl.ds(c * LANES + r * ROWS, ROWS)
                value = near_sums[rows, :]
                for u in range(UNROLL):
                    total = jnp.sum(held[u, rows, :], 1, keepdims=True)
                    value = jnp.where(lane_iota == step * UNROLL + u, total, value)
                near_sums[rows, :] = value

    def pushes(step, held):
        for u in range(UNROLL):
            t = step * UNROLL + u
            far_block = canon[info_smem[1, t]]
            far = [jnp.broadcast_to(far_block[c : c + 1, :], (ROWS, LANES)) for c in range(3)]
            near = jnp.dot(split, near_pick[t], preferred_element_type=jnp.float32)
            far_sum = [None] * 3
            for r in range(LANES // ROWS):
                rows = [pl.ds(c * LANES + r * ROWS, ROWS) for c in range(3)]
                spots = [(r // 2 * 3 + c) * 16 + r % 2 * ROWS for c in range(3)]
                diff = [near[spots[c] : spots[c] + ROWS, :] - far[c] for c in range(3)]
                weight = jnp.maximum(REACH - inner_rows(diff, diff), 0.0)
                for c in range(3):
                    push = weight * diff[c]
                    held[u, rows[c], :] = push
                    far_sum[c] = far_sum[c] + push if r else push
            place = pl.ds(pl.multiple_of(t * ROWS, ROWS), ROWS)
            for c in range(3):
                far_sums[place, c * LANES : (c + 1) * LANES] = far_sum[c]

    def tile_steps(half, carry):
        for phase in range(2):
            step = half * 2 + phase
            lane_sums(step - 1, held[1 - phase])
            pushes(step, held[phase])
        return carry

    steps = tiles // UNROLL
    lax.fori_loop(0, steps // 2, tile_steps, 0)
    lane_sums(steps - 1, held[1])
    total = pick_rows(take_far, far_sums[...], 2)
    near_total = []
    for c in range(3):
        value = near_sums[pl.ds(c * LANES, LANES), :]
        top = value.astype(BF16)
        low = (value - top.astype(jnp.float32)).astype(BF16)
        near_total.append(
            lax.dot_general(
                take_near,
                jnp.concatenate([top, low], 1),
                (((1,), (1,)), ((), ())),
                preferred_element_type=jnp.float32,
            )
        )
    total = total + jnp.concatenate(near_total, 1)
    for c in range(3):
        ans[:, c, :, :] = total[:, c * LANES : (c + 1) * LANES].reshape(groups, ROWS, LANES)
    backward = []
    for turn, k, step in partners:
        copy = pltpu.make_async_remote_copy(
            src_ref=ans.at[k],
            dst_ref=ret.at[g, step],
            send_sem=back_send.at[turn, step],
            recv_sem=back_recv.at[turn, step],
            device_id=(k, lax.rem(d + doms - step, doms)),
            device_id_type=MESH,
        )
        copy.start()
        backward.append(copy)
    ret[g, 0] = ans[g]

    rim_copy.wait_recv()
    state[blocks] = ghost_in[...]

    def elements(part, carry):
        here = pl.ds(pl.multiple_of(part * ROWS, ROWS), ROWS)
        for side in range(2):
            for kk in range(ROWS):
                b = cb_smem[side, part * ROWS + kk]
                corner_buf[side, pl.ds(kk * ROWS, ROWS), :] = state[b]
        pos = [None] * 4
        vel = [None] * 4
        for side, pair in enumerate(((0, 3), (1, 2))):
            column = [corner_buf[side, pl.ds(x, ROWS, stride=ROWS), :] for x in range(6)]
            for c in pair:
                ids = slot_ref[pl.ds(part * ROWS * 4 + c, ROWS, stride=4), :]
                picked = [gather_lanes(value, ids) for value in column]
                pos[c] = picked[:3]
                vel[c] = picked[3:]
        old = [stress_ref[x, here, :] for x in range(3)]
        forces, new = shell_forces(pos, vel, old)
        for x in range(3):
            stress_out[x, here, :] = new[x]
            for side, pair in enumerate(((0, 3), (1, 2))):
                spread[side, x, here, :] = sum(
                    gather_lanes(forces[c][x], inverse[pl.ds(part * ROWS * 4 + c, ROWS, stride=4), :]) for c in pair
                )
        return carry

    lax.fori_loop(0, blocks // ROWS, elements, 0)

    block_iota = lax.broadcasted_iota(jnp.int32, (blocks + ROWS, blocks), 0)
    hits = jnp.concatenate(
        [(block_iota == cb_ref[side : side + 1, :]).astype(jnp.float32) for side in range(2)], 1
    )
    both = jnp.concatenate(
        [
            jnp.concatenate([spread[side, c] for c in range(3)], 1)
            for side in range(2)
        ],
        0,
    )
    internal = pick_rows(hits, both, 2)
    for c in range(3):
        push_out[pl.ds(c, 1), :] = internal[blocks : blocks + 1, c * LANES : (c + 1) * LANES]
    push_copy = pltpu.make_async_remote_copy(
        src_ref=push_out,
        dst_ref=push_in,
        send_sem=push_sems.at[0],
        recv_sem=push_sems.at[1],
        device_id=(g, right),
        device_id_type=MESH,
    )
    push_copy.start()

    for copy in backward:
        copy.wait_recv()
    answers = jnp.concatenate(
        [ret[:, :, c, :, :].reshape(places, LANES) for c in range(3)], 1
    )
    answers = jnp.concatenate([answers, jnp.zeros((LANES - places, 3 * LANES), jnp.float32)], 0)
    contact = pick_rows(goers, answers, 2)
    push_copy.wait_recv()
    is_rim = lax.broadcasted_iota(jnp.int32, (blocks, LANES), 0) == halo
    factor = DT / mass_ref[...]
    for c in range(3):
        extra = jnp.where(is_rim, push_in[pl.ds(c, 1), :], 0.0)
        cols = slice(c * LANES, (c + 1) * LANES)
        force = contact[:, cols] - internal[0:blocks, cols] - extra
        vel_out[c] = vel_ref[c] + factor * force
    rim_copy.wait_send()
    info_copy.wait_send()
    push_copy.wait_send()
    for copy in forward:
        copy.wait_send()
    for copy in backward:
        copy.wait_send()


def local(
    positions,
    velocity,
    mass,
    stress,
    corner_block,
    corner_slot,
    halo_block,
    contact_owner,
    contact_slot,
    tile_pairs,
    tile_active,
):
    groups = lax.axis_size("group")
    doms = lax.axis_size("dom")
    blocks = corner_block.shape[2]
    nodes = positions.shape[2]
    tiles = tile_pairs.shape[2]
    slots = groups * ROWS
    vmem = pl.BlockSpec(memory_space=pltpu.VMEM)
    i32 = jnp.int32
    f32 = jnp.float32
    out = pl.pallas_call(
        functools.partial(kernel, groups, doms),
        out_shape=[jax.ShapeDtypeStruct((3, blocks, LANES), f32)] * 2,
        in_specs=[pl.BlockSpec(memory_space=pltpu.HBM)] * 11,
        out_specs=[vmem] * 2,
        scratch_shapes=[
            pltpu.VMEM((3, blocks, LANES), f32),
            pltpu.VMEM((3, blocks, LANES), f32),
            pltpu.VMEM((blocks, LANES), f32),
            pltpu.VMEM((3, blocks, LANES), f32),
            pltpu.VMEM((4 * blocks, LANES), i32),
            pltpu.VMEM((4, blocks), i32),
            pltpu.VMEM((1, blocks), i32),
            pltpu.VMEM((1, blocks), i32),
            pltpu.VMEM((2, tiles), i32),
            pltpu.VMEM((1, tiles), i32),
            pltpu.SMEM((4, blocks), i32),
            pltpu.SMEM((ROWS, LANES), i32),
            pltpu.VMEM((ROWS, LANES), i32),
            pltpu.VMEM((ROWS, LANES), i32),
            pltpu.SemaphoreType.DMA((3,)),
            pltpu.SMEM((1, 1), i32),
            pltpu.SemaphoreType.DMA((12,)),
            pltpu.VMEM((blocks + 1, ROWS, LANES), f32),
            pltpu.VMEM((ROWS, LANES), f32),
            pltpu.VMEM((ROWS, LANES), f32),
            pltpu.VMEM((groups, 3, 3, ROWS, LANES), f32),
            pltpu.VMEM((3, groups, 3, ROWS, LANES), f32),
            pltpu.VMEM((groups, 3, ROWS, LANES), f32),
            pltpu.VMEM((groups, 3, 3, ROWS, LANES), f32),
            pltpu.VMEM((slots, ROWS, LANES), f32),
            pltpu.VMEM((tiles + UNROLL, LANES, LANES), jnp.bfloat16),
            pltpu.VMEM((UNROLL, 3 * LANES, LANES), f32),
            pltpu.VMEM((UNROLL, 3 * LANES, LANES), f32),
            pltpu.VMEM((3 * LANES, LANES), f32),
            pltpu.VMEM((tiles * ROWS, 3 * LANES), f32),
            pltpu.VMEM((4 * blocks, LANES), jnp.int32),
            pltpu.VMEM((4 * blocks // LANES, LANES, LANES), f32),
            pltpu.VMEM((2, ROWS * ROWS, LANES), f32),
            pltpu.VMEM((2, 3, blocks, LANES), f32),
            pltpu.VMEM((ROWS, LANES), f32),
            pltpu.VMEM((ROWS, LANES), f32),
            pltpu.SemaphoreType.DMA((groups, 3)),
            pltpu.SemaphoreType.DMA((groups, 3)),
            pltpu.SemaphoreType.DMA((groups, 3)),
            pltpu.SemaphoreType.DMA((groups, 3)),
            pltpu.SemaphoreType.DMA((2,)),
            pltpu.SemaphoreType.DMA((2,)),
        ],
        compiler_params=pltpu.CompilerParams(
            collective_id=0, has_side_effects=True, vmem_limit_bytes=32 * 1024 * 1024
        ),
        name="shell_step",
    )(
        pltpu.with_memory_space_constraint(positions.reshape(3, blocks, LANES), pltpu.HBM),
        pltpu.with_memory_space_constraint(velocity.reshape(3, blocks, LANES), pltpu.HBM),
        pltpu.with_memory_space_constraint(mass.reshape(blocks, LANES), pltpu.HBM),
        pltpu.with_memory_space_constraint(stress.reshape(3, blocks, LANES), pltpu.HBM),
        pltpu.with_memory_space_constraint(corner_slot.reshape(4, blocks, LANES).transpose(1, 0, 2).reshape(4 * blocks, LANES), pltpu.HBM),
        pltpu.with_memory_space_constraint(corner_block.reshape(4, blocks), pltpu.HBM),
        pltpu.with_memory_space_constraint(contact_owner, pltpu.HBM),
        pltpu.with_memory_space_constraint(contact_slot, pltpu.HBM),
        pltpu.with_memory_space_constraint(tile_pairs.reshape(2, tiles), pltpu.HBM),
        pltpu.with_memory_space_constraint(tile_active, pltpu.HBM),
        halo_block,
    )
    return out[0].reshape(1, 3, nodes), out[1].reshape(1, 3, nodes)


def solution(mesh):
    in_specs = (
        P("group", None, "dom"),
        P("group", None, "dom"),
        P("group", "dom"),
        P("group", None, "dom"),
        P("group", None, "dom"),
        P("group", None, "dom"),
        P("group", "dom"),
        P("group", "dom"),
        P("group", "dom"),
        P("group", None, "dom"),
        P("group", "dom"),
    )
    out_specs = (P("group", None, "dom"), P("group", None, "dom"))
    return jax.shard_map(local, mesh=mesh, in_specs=in_specs, out_specs=out_specs, check_vma=False)
```

```python
import functools

import jax
import jax.numpy as jnp
from jax import lax
from jax.experimental import pallas as pl
from jax.experimental.pallas import tpu as pltpu
from jax.sharding import PartitionSpec as P

LANES = 128
ROWS = 8
DT = 0.5
STIFF = 2.0
POISSON = 0.3
HOURGLASS = 0.1
PENALTY = 4.0
REACH = 1.0
MESH = pl.DeviceIdType.MESH
HIGHEST = lax.Precision.HIGHEST
BF16 = jnp.bfloat16
UNROLL = 3


def inner_rows(a, b):
    return a[0] * b[0] + a[1] * b[1] + a[2] * b[2]


def cross_rows(a, b):
    return (
        a[1] * b[2] - a[2] * b[1],
        a[2] * b[0] - a[0] * b[2],
        a[0] * b[1] - a[1] * b[0],
    )


def minus(a, b):
    return tuple(x - y for x, y in zip(a, b))


def scaled(a, s):
    return tuple(x * s for x in a)


def gather_lanes(value, index):
    return jnp.take_along_axis(value, index, axis=1, mode="promise_in_bounds")


def pieces(value, count):
    parts = []
    for _ in range(count - 1):
        top = value.astype(BF16).astype(jnp.float32)
        parts.append(top)
        value = value - top
    parts.append(value)
    return jnp.concatenate(parts, 0).astype(BF16)


def pick_rows(chosen, value, count):
    lhs = jnp.concatenate([chosen] * count, 1).astype(BF16)
    return jnp.dot(lhs, pieces(value, count), preferred_element_type=jnp.float32)


def sort_rows(rows, sub):
    rows = list(rows)
    for k in range(1, 8):
        up = None if k < 4 or k == 7 else (sub & (1 << (k - 4))) == 0
        for j in range(k - 1, -1, -1):
            if j >= 4:
                gap = 1 << (j - 4)
                keep = (sub & gap) == 0
                if up is not None:
                    keep = keep == up
                for r in range(16):
                    other = jnp.take_along_axis(
                        rows[r], sub ^ gap, axis=0, mode="promise_in_bounds"
                    )
                    rows[r] = jnp.where(
                        keep, jnp.minimum(rows[r], other), jnp.maximum(rows[r], other)
                    )
                continue
            for r in range(16):
                far = r | (1 << j)
                if far == r:
                    continue
                low = jnp.minimum(rows[r], rows[far])
                high = jnp.maximum(rows[r], rows[far])
                if up is not None:
                    low, high = jnp.where(up, low, high), jnp.where(up, high, low)
                elif k < 4 and r & (1 << k):
                    low, high = high, low
                rows[r], rows[far] = low, high
    return rows


def shell_forces(pos, vel, stress_old):
    diag_a = minus(pos[2], pos[0])
    diag_b = minus(pos[3], pos[1])
    normal = cross_rows(diag_a, diag_b)
    inv_j = lax.rsqrt(inner_rows(normal, normal))
    axis_three = scaled(normal, inv_j)
    tangent = minus(diag_a, diag_b)
    tangent = minus(tangent, scaled(axis_three, inner_rows(tangent, axis_three)))
    axis_one = scaled(tangent, lax.rsqrt(inner_rows(tangent, tangent)))
    axis_two = cross_rows(axis_three, axis_one)
    along_a = inner_rows(diag_a, axis_one)
    across_a = inner_rows(diag_a, axis_two)
    along_b = inner_rows(diag_b, axis_one)
    across_b = inner_rows(diag_b, axis_two)
    speed_a = minus(vel[2], vel[0])
    speed_b = minus(vel[3], vel[1])
    slide_a = inner_rows(speed_a, axis_one)
    lift_a = inner_rows(speed_a, axis_two)
    slide_b = inner_rows(speed_b, axis_one)
    lift_b = inner_rows(speed_b, axis_two)
    rate_xx = (across_b * slide_a - across_a * slide_b) * inv_j
    rate_yy = (along_a * lift_b - along_b * lift_a) * inv_j
    rate_xy = (
        across_b * lift_a - across_a * lift_b + along_a * slide_b - along_b * slide_a
    ) * inv_j
    s_xx = stress_old[0] + (DT * STIFF) * (rate_xx + POISSON * rate_yy)
    s_yy = stress_old[1] + (DT * STIFF) * (POISSON * rate_xx + rate_yy)
    s_xy = stress_old[2] + (DT * STIFF * 0.5 * (1.0 - POISSON)) * rate_xy
    half_xx, half_yy, half_xy = 0.5 * s_xx, 0.5 * s_yy, 0.5 * s_xy
    fx0 = along_b * half_xy - across_b * half_xx
    fy0 = along_b * half_yy - across_b * half_xy
    fx1 = across_a * half_xx - along_a * half_xy
    fy1 = across_a * half_xy - along_a * half_yy
    forces = [[], [], [], []]
    for c in range(3):
        mode = HOURGLASS * (vel[0][c] - vel[1][c] + vel[2][c] - vel[3][c])
        first = fx0 * axis_one[c] + fy0 * axis_two[c]
        second = fx1 * axis_one[c] + fy1 * axis_two[c]
        forces[0].append(mode + first)
        forces[1].append(second - mode)
        forces[2].append(mode - first)
        forces[3].append(-mode - second)
    return forces, (s_xx, s_yy, s_xy)


def kernel(
    groups,
    doms,
    pos_hbm,
    vel_hbm,
    mass_hbm,
    stress_hbm,
    slot_hbm,
    cb_hbm,
    owner_hbm,
    spot_hbm,
    pair_hbm,
    active_hbm,
    halo_hbm,
    vel_out,
    stress_out,
    pos_ref,
    vel_ref,
    mass_ref,
    stress_ref,
    slot_ref,
    cb_ref,
    owner_ref,
    spot_ref,
    pair_ref,
    active_ref,
    cb_smem,
    info_smem,
    info_out,
    info_in,
    info_sems,
    rim_ready,
    halo_smem,
    in_sems,
    state,
    rim,
    ghost_in,
    out_buf,
    in_buf,
    ans,
    ret,
    canon,
    near_pick,
    held_even,
    held_odd,
    near_sums,
    far_sums,
    inverse,
    sort_buf,
    corner_buf,
    spread,
    push_out,
    push_in,
    fwd_send,
    fwd_recv,
    back_send,
    back_recv,
    rim_sems,
    push_sems,
):
    g = lax.axis_index("group")
    d = lax.axis_index("dom")
    blocks = mass_ref.shape[0]
    tiles = pair_ref.shape[1]
    slots = groups * ROWS
    left = lax.rem(d + doms - 1, doms)
    right = lax.rem(d + 1, doms)
    partners = []
    for step in (2, 1, 0):
        for turn in (2, 3, 1, 0):
            if turn == 0 and step == 0:
                continue
            partners.append((turn, lax.rem(g + turn, groups), step))

    barrier = pltpu.get_barrier_semaphore()
    for turn, k, step in partners:
        pl.semaphore_signal(
            barrier,
            inc=1,
            device_id=(k, lax.rem(d + doms - step, doms)),
            device_id_type=MESH,
        )

    sources = (
        (pos_hbm, pos_ref),
        (owner_hbm, owner_ref),
        (spot_hbm, spot_ref),
        (pair_hbm, pair_ref),
        (active_hbm, active_ref),
        (vel_hbm, vel_ref),
        (halo_hbm, halo_smem),
        (slot_hbm, slot_ref),
        (cb_hbm, cb_ref),
        (cb_hbm, cb_smem),
        (stress_hbm, stress_ref),
        (mass_hbm, mass_ref),
    )
    loads = []
    for n, (source, target) in enumerate(sources):
        copy = pltpu.make_async_copy(source, target, in_sems.at[n])
        copy.start()
        loads.append(copy)
    for copy in loads[:3]:
        copy.wait()
    sub_iota = lax.broadcasted_iota(jnp.int32, (ROWS, LANES), 0)
    lane_iota = lax.broadcasted_iota(jnp.int32, (ROWS, LANES), 1)
    owner = owner_ref[...]
    step_of = lax.rem(lax.rem(owner, doms) - d + 1 + doms, doms)
    goal = (lax.div(owner, doms) * 3 + step_of) * ROWS + lax.rem(spot_ref[...], ROWS)
    goal = jnp.where(owner >= 0, goal, -1)
    places = groups * 3 * ROWS
    chosen = (
        lax.broadcasted_iota(jnp.int32, (places, blocks), 0) == goal
    ).astype(jnp.float32)
    everywhere = jnp.concatenate([pos_ref[c] for c in range(3)], 1)
    packed = pick_rows(chosen, everywhere, 3)
    for c in range(3):
        out_buf[:, :, c, :, :] = packed[:, c * LANES : (c + 1) * LANES].reshape(
            groups, 3, ROWS, LANES
        )
    for copy in loads[3:5]:
        copy.wait()
    info_out[0:2, 0:tiles] = pair_ref[...]
    info_out[2:3, 0:tiles] = active_ref[...]
    pl.semaphore_wait(barrier, len(partners))
    pl.semaphore_signal(rim_ready, inc=1, device_id=(g, right), device_id_type=MESH)

    info_copy = pltpu.make_async_remote_copy(
        src_ref=info_out,
        dst_ref=info_in,
        send_sem=info_sems.at[0],
        recv_sem=info_sems.at[1],
        device_id=(g, right),
        device_id_type=MESH,
    )
    info_copy.start()

    forward = []
    for turn, k, step in partners:
        copy = pltpu.make_async_remote_copy(
            src_ref=out_buf.at[k, step],
            dst_ref=in_buf.at[step, g],
            send_sem=fwd_send.at[turn, step],
            recv_sem=fwd_recv.at[turn, step],
            device_id=(k, lax.rem(d + step, doms)),
            device_id_type=MESH,
        )
        copy.start()
        forward.append(copy)
    in_buf[0, g] = out_buf[g, 0]

    for copy in loads[5:7]:
        copy.wait()
    halo = halo_smem[0, 0]
    state_rows = state.reshape((blocks + 1) * ROWS, LANES)
    for c in range(3):
        state_rows[pl.ds(c, blocks, stride=ROWS), :] = pos_ref[c]
        state_rows[pl.ds(3 + c, blocks, stride=ROWS), :] = vel_ref[c]
    rim[...] = state[halo]
    for copy in loads[7:]:
        copy.wait()
    goers = jnp.transpose(jnp.concatenate([chosen, jnp.zeros((LANES - places, blocks), jnp.float32)], 0))

    wide_iota = lax.broadcasted_iota(jnp.int32, (LANES, LANES), 1)
    for half in range(4 * blocks // LANES):
        rows = pl.ds(half * LANES, LANES)
        keys = jnp.transpose((slot_ref[rows, :] * LANES + wide_iota).astype(jnp.float32))
        keys = sort_rows([keys[r * ROWS : (r + 1) * ROWS, :] for r in range(16)], sub_iota)
        for r in range(16):
            sort_buf[half, pl.ds(r, ROWS, stride=16), :] = keys[r]
        inverse[rows, :] = jnp.transpose(sort_buf[half]).astype(jnp.int32) - wide_iota * LANES

    pl.semaphore_wait(rim_ready, 1)
    rim_copy = pltpu.make_async_remote_copy(
        src_ref=rim,
        dst_ref=ghost_in,
        send_sem=rim_sems.at[0],
        recv_sem=rim_sems.at[1],
        device_id=(g, left),
        device_id_type=MESH,
    )
    rim_copy.start()

    info_copy.wait_recv()
    to_smem = pltpu.make_async_copy(info_in, info_smem, info_sems.at[2])
    to_smem.start()
    to_smem.wait()
    slot_iota = lax.broadcasted_iota(jnp.int32, (slots, tiles), 0)
    gain = PENALTY * info_in[2:3, 0:tiles].astype(jnp.float32)
    take_near = jnp.where(slot_iota == info_in[0:1, 0:tiles], gain, 0.0).astype(BF16)
    take_far = jnp.where(slot_iota == info_in[1:2, 0:tiles], -gain, 0.0).astype(BF16)
    tile_iota = lax.broadcasted_iota(jnp.int32, (tiles, 2 * LANES), 0)
    column = lax.broadcasted_iota(jnp.int32, (tiles, 2 * LANES), 1)
    same = ((column & (LANES - 1)) == tile_iota).astype(BF16)
    take_near = jnp.dot(take_near, same, preferred_element_type=jnp.float32).astype(BF16)
    tile_iota = lax.broadcasted_iota(jnp.int32, (tiles, tiles * ROWS), 0)
    column = lax.broadcasted_iota(jnp.int32, (tiles, tiles * ROWS), 1)
    same = (lax.div(column, ROWS) == tile_iota).astype(BF16)
    take_far = jnp.dot(take_far, same, preferred_element_type=jnp.float32)
    near_sums[...] = jnp.zeros_like(near_sums)
    depth = lax.broadcasted_iota(jnp.int32, (LANES, LANES), 0)
    depth = jnp.where(depth < 3 * slots, lax.rem(depth, slots), -1)

    def pick(t, carry):
        near_pick[t] = (depth == info_smem[0, t]).astype(jnp.float32).astype(BF16)
        return carry

    lax.fori_loop(0, tiles, pick, 0)

    for copy in forward:
        copy.wait_recv()
    held = (held_even, held_odd)
    canon_rows = canon.reshape(slots * ROWS, LANES)
    split = []
    for c in range(3):
        layers = []
        for layer in range(groups):
            rows = in_buf[0, layer, c] + in_buf[1, layer, c] + in_buf[2, layer, c]
            canon_rows[pl.ds(layer * ROWS * ROWS + c, ROWS, stride=ROWS), :] = rows
            layers.append(rows)
        value = jnp.concatenate(layers, 0)
        top = value.astype(BF16).astype(jnp.float32)
        rest = value - top
        middle = rest.astype(BF16).astype(jnp.float32)
        stack = jnp.concatenate([top, middle, rest - middle, jnp.zeros_like(value)], 0)
        split.append(jnp.transpose(stack).astype(BF16))
    split = jnp.concatenate(
        [split[c][16 * r : 16 * r + 16] for r in range(LANES // 16) for c in range(3)], 0
    )

    def lane_sums(step, held):
        for c in range(3):
            for r in range(LANES // ROWS):
                rows = pl.ds(c * LANES + r * ROWS, ROWS)
                value = near_sums[rows, :]
                for u in range(UNROLL):
                    total = jnp.sum(held[u, rows, :], 1, keepdims=True)
                    value = jnp.where(lane_iota == step * UNROLL + u, total, value)
                near_sums[rows, :] = value

    def pushes(step, held):
        for u in range(UNROLL):
            t = step * UNROLL + u
            far_block = canon[info_smem[1, t]]
            far = [jnp.broadcast_to(far_block[c : c + 1, :], (ROWS, LANES)) for c in range(3)]
            near = jnp.dot(split, near_pick[t], preferred_element_type=jnp.float32)
            far_sum = [None] * 3
            for r in range(LANES // ROWS):
                rows = [pl.ds(c * LANES + r * ROWS, ROWS) for c in range(3)]
                spots = [(r // 2 * 3 + c) * 16 + r % 2 * ROWS for c in range(3)]
                diff = [near[spots[c] : spots[c] + ROWS, :] - far[c] for c in range(3)]
                weight = jnp.maximum(REACH - inner_rows(diff, diff), 0.0)
                for c in range(3):
                    push = weight * diff[c]
                    held[u, rows[c], :] = push
                    far_sum[c] = far_sum[c] + push if r else push
            place = pl.ds(pl.multiple_of(t * ROWS, ROWS), ROWS)
            for c in range(3):
                far_sums[place, c * LANES : (c + 1) * LANES] = far_sum[c]

    def tile_steps(half, carry):
        for phase in range(2):
            step = half * 2 + phase
            lane_sums(step - 1, held[1 - phase])
            pushes(step, held[phase])
        return carry

    steps = tiles // UNROLL
    lax.fori_loop(0, steps // 2, tile_steps, 0)
    lane_sums(steps - 1, held[1])
    total = pick_rows(take_far, far_sums[...], 2)
    near_total = []
    for c in range(3):
        value = near_sums[pl.ds(c * LANES, LANES), :]
        top = value.astype(BF16)
        low = (value - top.astype(jnp.float32)).astype(BF16)
        near_total.append(
            lax.dot_general(
                take_near,
                jnp.concatenate([top, low], 1),
                (((1,), (1,)), ((), ())),
                preferred_element_type=jnp.float32,
            )
        )
    total = total + jnp.concatenate(near_total, 1)
    for c in range(3):
        ans[:, c, :, :] = total[:, c * LANES : (c + 1) * LANES].reshape(groups, ROWS, LANES)
    backward = []
    for turn, k, step in partners:
        copy = pltpu.make_async_remote_copy(
            src_ref=ans.at[k],
            dst_ref=ret.at[g, step],
            send_sem=back_send.at[turn, step],
            recv_sem=back_recv.at[turn, step],
            device_id=(k, lax.rem(d + doms - step, doms)),
            device_id_type=MESH,
        )
        copy.start()
        backward.append(copy)
    ret[g, 0] = ans[g]

    rim_copy.wait_recv()
    state[blocks] = ghost_in[...]

    def elements(part, carry):
        here = pl.ds(pl.multiple_of(part * ROWS, ROWS), ROWS)
        for side in range(2):
            for kk in range(ROWS):
                b = cb_smem[side, part * ROWS + kk]
                corner_buf[side, pl.ds(kk * ROWS, ROWS), :] = state[b]
        pos = [None] * 4
        vel = [None] * 4
        for side, pair in enumerate(((0, 3), (1, 2))):
            column = [corner_buf[side, pl.ds(x, ROWS, stride=ROWS), :] for x in range(6)]
            for c in pair:
                ids = slot_ref[pl.ds(part * ROWS * 4 + c, ROWS, stride=4), :]
                picked = [gather_lanes(value, ids) for value in column]
                pos[c] = picked[:3]
                vel[c] = picked[3:]
        old = [stress_ref[x, here, :] for x in range(3)]
        forces, new = shell_forces(pos, vel, old)
        for x in range(3):
            stress_out[x, here, :] = new[x]
            for side, pair in enumerate(((0, 3), (1, 2))):
                spread[side, x, here, :] = sum(
                    gather_lanes(forces[c][x], inverse[pl.ds(part * ROWS * 4 + c, ROWS, stride=4), :]) for c in pair
                )
        return carry

    lax.fori_loop(0, blocks // ROWS, elements, 0)

    block_iota = lax.broadcasted_iota(jnp.int32, (blocks + ROWS, blocks), 0)
    hits = jnp.concatenate(
        [(block_iota == cb_ref[side : side + 1, :]).astype(jnp.float32) for side in range(2)], 1
    )
    both = jnp.concatenate(
        [
            jnp.concatenate([spread[side, c] for c in range(3)], 1)
            for side in range(2)
        ],
        0,
    )
    internal = pick_rows(hits, both, 2)
    for c in range(3):
        push_out[pl.ds(c, 1), :] = internal[blocks : blocks + 1, c * LANES : (c + 1) * LANES]
    push_copy = pltpu.make_async_remote_copy(
        src_ref=push_out,
        dst_ref=push_in,
        send_sem=push_sems.at[0],
        recv_sem=push_sems.at[1],
        device_id=(g, right),
        device_id_type=MESH,
    )
    push_copy.start()

    for copy in backward:
        copy.wait_recv()
    answers = jnp.concatenate(
        [ret[:, :, c, :, :].reshape(places, LANES) for c in range(3)], 1
    )
    answers = jnp.concatenate([answers, jnp.zeros((LANES - places, 3 * LANES), jnp.float32)], 0)
    contact = pick_rows(goers, answers, 2)
    push_copy.wait_recv()
    is_rim = lax.broadcasted_iota(jnp.int32, (blocks, LANES), 0) == halo
    factor = DT / mass_ref[...]
    for c in range(3):
        extra = jnp.where(is_rim, push_in[pl.ds(c, 1), :], 0.0)
        cols = slice(c * LANES, (c + 1) * LANES)
        force = contact[:, cols] - internal[0:blocks, cols] - extra
        vel_out[c] = vel_ref[c] + factor * force
    rim_copy.wait_send()
    info_copy.wait_send()
    push_copy.wait_send()
    for copy in forward:
        copy.wait_send()
    for copy in backward:
        copy.wait_send()


def local(
    positions,
    velocity,
    mass,
    stress,
    corner_block,
    corner_slot,
    halo_block,
    contact_owner,
    contact_slot,
    tile_pairs,
    tile_active,
):
    groups = lax.axis_size("group")
    doms = lax.axis_size("dom")
    blocks = corner_block.shape[2]
    nodes = positions.shape[2]
    tiles = tile_pairs.shape[2]
    slots = groups * ROWS
    vmem = pl.BlockSpec(memory_space=pltpu.VMEM)
    i32 = jnp.int32
    f32 = jnp.float32
    out = pl.pallas_call(
        functools.partial(kernel, groups, doms),
        out_shape=[jax.ShapeDtypeStruct((3, blocks, LANES), f32)] * 2,
        in_specs=[pl.BlockSpec(memory_space=pltpu.HBM)] * 11,
        out_specs=[vmem] * 2,
        scratch_shapes=[
            pltpu.VMEM((3, blocks, LANES), f32),
            pltpu.VMEM((3, blocks, LANES), f32),
            pltpu.VMEM((blocks, LANES), f32),
            pltpu.VMEM((3, blocks, LANES), f32),
            pltpu.VMEM((4 * blocks, LANES), i32),
            pltpu.VMEM((4, blocks), i32),
            pltpu.VMEM((1, blocks), i32),
            pltpu.VMEM((1, blocks), i32),
            pltpu.VMEM((2, tiles), i32),
            pltpu.VMEM((1, tiles), i32),
            pltpu.SMEM((4, blocks), i32),
            pltpu.SMEM((ROWS, LANES), i32),
            pltpu.VMEM((ROWS, LANES), i32),
            pltpu.VMEM((ROWS, LANES), i32),
            pltpu.SemaphoreType.DMA((3,)),
            pltpu.SemaphoreType.REGULAR,
            pltpu.SMEM((1, 1), i32),
            pltpu.SemaphoreType.DMA((12,)),
            pltpu.VMEM((blocks + 1, ROWS, LANES), f32),
            pltpu.VMEM((ROWS, LANES), f32),
            pltpu.VMEM((ROWS, LANES), f32),
            pltpu.VMEM((groups, 3, 3, ROWS, LANES), f32),
            pltpu.VMEM((3, groups, 3, ROWS, LANES), f32),
            pltpu.VMEM((groups, 3, ROWS, LANES), f32),
            pltpu.VMEM((groups, 3, 3, ROWS, LANES), f32),
            pltpu.VMEM((slots, ROWS, LANES), f32),
            pltpu.VMEM((tiles + UNROLL, LANES, LANES), jnp.bfloat16),
            pltpu.VMEM((UNROLL, 3 * LANES, LANES), f32),
            pltpu.VMEM((UNROLL, 3 * LANES, LANES), f32),
            pltpu.VMEM((3 * LANES, LANES), f32),
            pltpu.VMEM((tiles * ROWS, 3 * LANES), f32),
            pltpu.VMEM((4 * blocks, LANES), jnp.int32),
            pltpu.VMEM((4 * blocks // LANES, LANES, LANES), f32),
            pltpu.VMEM((2, ROWS * ROWS, LANES), f32),
            pltpu.VMEM((2, 3, blocks, LANES), f32),
            pltpu.VMEM((ROWS, LANES), f32),
            pltpu.VMEM((ROWS, LANES), f32),
            pltpu.SemaphoreType.DMA((groups, 3)),
            pltpu.SemaphoreType.DMA((groups, 3)),
            pltpu.SemaphoreType.DMA((groups, 3)),
            pltpu.SemaphoreType.DMA((groups, 3)),
            pltpu.SemaphoreType.DMA((2,)),
            pltpu.SemaphoreType.DMA((2,)),
        ],
        compiler_params=pltpu.CompilerParams(
            collective_id=0, has_side_effects=True, vmem_limit_bytes=32 * 1024 * 1024
        ),
        name="shell_step",
    )(
        pltpu.with_memory_space_constraint(positions.reshape(3, blocks, LANES), pltpu.HBM),
        pltpu.with_memory_space_constraint(velocity.reshape(3, blocks, LANES), pltpu.HBM),
        pltpu.with_memory_space_constraint(mass.reshape(blocks, LANES), pltpu.HBM),
        pltpu.with_memory_space_constraint(stress.reshape(3, blocks, LANES), pltpu.HBM),
        pltpu.with_memory_space_constraint(corner_slot.reshape(4, blocks, LANES).transpose(1, 0, 2).reshape(4 * blocks, LANES), pltpu.HBM),
        pltpu.with_memory_space_constraint(corner_block.reshape(4, blocks), pltpu.HBM),
        pltpu.with_memory_space_constraint(contact_owner, pltpu.HBM),
        pltpu.with_memory_space_constraint(contact_slot, pltpu.HBM),
        pltpu.with_memory_space_constraint(tile_pairs.reshape(2, tiles), pltpu.HBM),
        pltpu.with_memory_space_constraint(tile_active, pltpu.HBM),
        halo_block,
    )
    return out[0].reshape(1, 3, nodes), out[1].reshape(1, 3, nodes)


def solution(mesh):
    in_specs = (
        P("group", None, "dom"),
        P("group", None, "dom"),
        P("group", "dom"),
        P("group", None, "dom"),
        P("group", None, "dom"),
        P("group", None, "dom"),
        P("group", "dom"),
        P("group", "dom"),
        P("group", "dom"),
        P("group", None, "dom"),
        P("group", "dom"),
    )
    out_specs = (P("group", None, "dom"), P("group", None, "dom"))
    return jax.shard_map(local, mesh=mesh, in_specs=in_specs, out_specs=out_specs, check_vma=False)
```

```python
import functools

import jax
import jax.numpy as jnp
from jax import lax
from jax.experimental import pallas as pl
from jax.experimental.pallas import tpu as pltpu
from jax.sharding import PartitionSpec as P

LANES = 128
ROWS = 8
DT = 0.5
STIFF = 2.0
POISSON = 0.3
HOURGLASS = 0.1
PENALTY = 4.0
REACH = 1.0
MESH = pl.DeviceIdType.MESH
HIGHEST = lax.Precision.HIGHEST
BF16 = jnp.bfloat16
UNROLL = 3


def inner_rows(a, b):
    return a[0] * b[0] + a[1] * b[1] + a[2] * b[2]


def cross_rows(a, b):
    return (
        a[1] * b[2] - a[2] * b[1],
        a[2] * b[0] - a[0] * b[2],
        a[0] * b[1] - a[1] * b[0],
    )


def minus(a, b):
    return tuple(x - y for x, y in zip(a, b))


def scaled(a, s):
    return tuple(x * s for x in a)


def gather_lanes(value, index):
    return jnp.take_along_axis(value, index, axis=1, mode="promise_in_bounds")


def pieces(value, count):
    parts = []
    for _ in range(count - 1):
        top = value.astype(BF16).astype(jnp.float32)
        parts.append(top)
        value = value - top
    parts.append(value)
    return jnp.concatenate(parts, 0).astype(BF16)


def pick_rows(chosen, value, count):
    lhs = jnp.concatenate([chosen] * count, 1).astype(BF16)
    return jnp.dot(lhs, pieces(value, count), preferred_element_type=jnp.float32)


def sort_rows(rows, sub):
    rows = list(rows)
    for k in range(1, 8):
        up = None if k < 4 or k == 7 else (sub & (1 << (k - 4))) == 0
        for j in range(k - 1, -1, -1):
            if j >= 4:
                gap = 1 << (j - 4)
                keep = (sub & gap) == 0
                if up is not None:
                    keep = keep == up
                for r in range(16):
                    other = jnp.take_along_axis(
                        rows[r], sub ^ gap, axis=0, mode="promise_in_bounds"
                    )
                    rows[r] = jnp.where(
                        keep, jnp.minimum(rows[r], other), jnp.maximum(rows[r], other)
                    )
                continue
            for r in range(16):
                far = r | (1 << j)
                if far == r:
                    continue
                low = jnp.minimum(rows[r], rows[far])
                high = jnp.maximum(rows[r], rows[far])
                if up is not None:
                    low, high = jnp.where(up, low, high), jnp.where(up, high, low)
                elif k < 4 and r & (1 << k):
                    low, high = high, low
                rows[r], rows[far] = low, high
    return rows


def shell_forces(pos, vel, stress_old):
    diag_a = minus(pos[2], pos[0])
    diag_b = minus(pos[3], pos[1])
    normal = cross_rows(diag_a, diag_b)
    inv_j = lax.rsqrt(inner_rows(normal, normal))
    axis_three = scaled(normal, inv_j)
    tangent = minus(diag_a, diag_b)
    tangent = minus(tangent, scaled(axis_three, inner_rows(tangent, axis_three)))
    axis_one = scaled(tangent, lax.rsqrt(inner_rows(tangent, tangent)))
    axis_two = cross_rows(axis_three, axis_one)
    along_a = inner_rows(diag_a, axis_one)
    across_a = inner_rows(diag_a, axis_two)
    along_b = inner_rows(diag_b, axis_one)
    across_b = inner_rows(diag_b, axis_two)
    speed_a = minus(vel[2], vel[0])
    speed_b = minus(vel[3], vel[1])
    slide_a = inner_rows(speed_a, axis_one)
    lift_a = inner_rows(speed_a, axis_two)
    slide_b = inner_rows(speed_b, axis_one)
    lift_b = inner_rows(speed_b, axis_two)
    rate_xx = (across_b * slide_a - across_a * slide_b) * inv_j
    rate_yy = (along_a * lift_b - along_b * lift_a) * inv_j
    rate_xy = (
        across_b * lift_a - across_a * lift_b + along_a * slide_b - along_b * slide_a
    ) * inv_j
    s_xx = stress_old[0] + (DT * STIFF) * (rate_xx + POISSON * rate_yy)
    s_yy = stress_old[1] + (DT * STIFF) * (POISSON * rate_xx + rate_yy)
    s_xy = stress_old[2] + (DT * STIFF * 0.5 * (1.0 - POISSON)) * rate_xy
    half_xx, half_yy, half_xy = 0.5 * s_xx, 0.5 * s_yy, 0.5 * s_xy
    fx0 = along_b * half_xy - across_b * half_xx
    fy0 = along_b * half_yy - across_b * half_xy
    fx1 = across_a * half_xx - along_a * half_xy
    fy1 = across_a * half_xy - along_a * half_yy
    forces = [[], [], [], []]
    for c in range(3):
        mode = HOURGLASS * (vel[0][c] - vel[1][c] + vel[2][c] - vel[3][c])
        first = fx0 * axis_one[c] + fy0 * axis_two[c]
        second = fx1 * axis_one[c] + fy1 * axis_two[c]
        forces[0].append(mode + first)
        forces[1].append(second - mode)
        forces[2].append(mode - first)
        forces[3].append(-mode - second)
    return forces, (s_xx, s_yy, s_xy)


def kernel(
    groups,
    doms,
    pos_hbm,
    vel_hbm,
    mass_hbm,
    stress_hbm,
    slot_hbm,
    cb_hbm,
    owner_hbm,
    spot_hbm,
    pair_hbm,
    active_hbm,
    halo_hbm,
    vel_out,
    stress_out,
    pos_ref,
    vel_ref,
    mass_ref,
    stress_ref,
    slot_ref,
    cb_ref,
    owner_ref,
    spot_ref,
    pair_ref,
    active_ref,
    cb_smem,
    info_smem,
    info_out,
    info_in,
    info_sems,
    rim_ready,
    halo_smem,
    in_sems,
    state,
    rim,
    ghost_in,
    out_buf,
    in_buf,
    ans,
    ret,
    canon,
    near_pick,
    held_even,
    held_odd,
    near_sums,
    far_sums,
    inverse,
    sort_buf,
    corner_buf,
    spread,
    push_out,
    push_in,
    fwd_send,
    fwd_recv,
    back_send,
    back_recv,
    rim_sems,
    push_sems,
):
    g = lax.axis_index("group")
    d = lax.axis_index("dom")
    blocks = mass_ref.shape[0]
    tiles = pair_ref.shape[1]
    slots = groups * ROWS
    left = lax.rem(d + doms - 1, doms)
    right = lax.rem(d + 1, doms)
    partners = []
    for step in (2, 1, 0):
        for turn in (2, 3, 1, 0):
            if turn == 0 and step == 0:
                continue
            partners.append((turn, lax.rem(g + turn, groups), step))

    barrier = pltpu.get_barrier_semaphore()
    for turn, k, step in partners:
        pl.semaphore_signal(
            barrier,
            inc=1,
            device_id=(k, lax.rem(d + doms - step, doms)),
            device_id_type=MESH,
        )

    sources = (
        (pos_hbm, pos_ref),
        (owner_hbm, owner_ref),
        (spot_hbm, spot_ref),
        (pair_hbm, pair_ref),
        (active_hbm, active_ref),
        (vel_hbm, vel_ref),
        (halo_hbm, halo_smem),
        (slot_hbm, slot_ref),
        (cb_hbm, cb_ref),
        (cb_hbm, cb_smem),
        (stress_hbm, stress_ref),
        (mass_hbm, mass_ref),
    )
    loads = []
    for n, (source, target) in enumerate(sources):
        copy = pltpu.make_async_copy(source, target, in_sems.at[n])
        copy.start()
        loads.append(copy)
    for copy in loads[:3]:
        copy.wait()
    sub_iota = lax.broadcasted_iota(jnp.int32, (ROWS, LANES), 0)
    lane_iota = lax.broadcasted_iota(jnp.int32, (ROWS, LANES), 1)
    owner = owner_ref[...]
    step_of = lax.rem(lax.rem(owner, doms) - d + 1 + doms, doms)
    goal = (lax.div(owner, doms) * 3 + step_of) * ROWS + lax.rem(spot_ref[...], ROWS)
    goal = jnp.where(owner >= 0, goal, -1)
    places = groups * 3 * ROWS
    chosen = (
        lax.broadcasted_iota(jnp.int32, (places, blocks), 0) == goal
    ).astype(jnp.float32)
    everywhere = jnp.concatenate([pos_ref[c] for c in range(3)], 1)
    packed = pick_rows(chosen, everywhere, 3)
    for c in range(3):
        out_buf[:, :, c, :, :] = packed[:, c * LANES : (c + 1) * LANES].reshape(
            groups, 3, ROWS, LANES
        )
    for copy in loads[3:5]:
        copy.wait()
    info_out[0:2, 0:tiles] = pair_ref[...]
    info_out[2:3, 0:tiles] = active_ref[...]
    pl.semaphore_wait(barrier, len(partners))
    pl.semaphore_signal(rim_ready, inc=1, device_id=(g, right), device_id_type=MESH)

    info_copy = pltpu.make_async_remote_copy(
        src_ref=info_out,
        dst_ref=info_in,
        send_sem=info_sems.at[0],
        recv_sem=info_sems.at[1],
        device_id=(g, right),
        device_id_type=MESH,
    )
    info_copy.start()

    forward = []
    for turn, k, step in partners:
        copy = pltpu.make_async_remote_copy(
            src_ref=out_buf.at[k, step],
            dst_ref=in_buf.at[step, g],
            send_sem=fwd_send.at[turn, step],
            recv_sem=fwd_recv.at[turn, step],
            device_id=(k, lax.rem(d + step, doms)),
            device_id_type=MESH,
        )
        copy.start()
        forward.append(copy)
    in_buf[0, g] = out_buf[g, 0]

    for copy in loads[5:7]:
        copy.wait()
    halo = halo_smem[0, 0]
    state_rows = state.reshape((blocks + 1) * ROWS, LANES)
    for c in range(3):
        state_rows[pl.ds(c, blocks, stride=ROWS), :] = pos_ref[c]
        state_rows[pl.ds(3 + c, blocks, stride=ROWS), :] = vel_ref[c]
    rim[...] = state[halo]
    for copy in loads[7:]:
        copy.wait()
    goers = jnp.transpose(jnp.concatenate([chosen, jnp.zeros((LANES - places, blocks), jnp.float32)], 0))

    wide_iota = lax.broadcasted_iota(jnp.int32, (LANES, LANES), 1)
    for half in range(4 * blocks // LANES):
        rows = pl.ds(half * LANES, LANES)
        keys = jnp.transpose((slot_ref[rows, :] * LANES + wide_iota).astype(jnp.float32))
        keys = sort_rows([keys[r * ROWS : (r + 1) * ROWS, :] for r in range(16)], sub_iota)
        for r in range(16):
            sort_buf[half, pl.ds(r, ROWS, stride=16), :] = keys[r]
        inverse[rows, :] = jnp.transpose(sort_buf[half]).astype(jnp.int32) - wide_iota * LANES

    pl.semaphore_wait(rim_ready, 1)
    rim_copy = pltpu.make_async_remote_copy(
        src_ref=rim,
        dst_ref=ghost_in,
        send_sem=rim_sems.at[0],
        recv_sem=rim_sems.at[1],
        device_id=(g, left),
        device_id_type=MESH,
    )
    rim_copy.start()

    info_copy.wait_recv()
    to_smem = pltpu.make_async_copy(info_in, info_smem, info_sems.at[2])
    to_smem.start()
    to_smem.wait()
    slot_iota = lax.broadcasted_iota(jnp.int32, (slots, tiles), 0)
    gain = PENALTY * info_in[2:3, 0:tiles].astype(jnp.float32)
    take_near = jnp.where(slot_iota == info_in[0:1, 0:tiles], gain, 0.0).astype(BF16)
    take_far = jnp.where(slot_iota == info_in[1:2, 0:tiles], -gain, 0.0).astype(BF16)
    tile_iota = lax.broadcasted_iota(jnp.int32, (tiles, 2 * LANES), 0)
    column = lax.broadcasted_iota(jnp.int32, (tiles, 2 * LANES), 1)
    same = ((column & (LANES - 1)) == tile_iota).astype(BF16)
    take_near = jnp.dot(take_near, same, preferred_element_type=jnp.float32).astype(BF16)
    tile_iota = lax.broadcasted_iota(jnp.int32, (tiles, tiles * ROWS), 0)
    column = lax.broadcasted_iota(jnp.int32, (tiles, tiles * ROWS), 1)
    same = (lax.div(column, ROWS) == tile_iota).astype(BF16)
    take_far = jnp.dot(take_far, same, preferred_element_type=jnp.float32)
    near_sums[...] = jnp.zeros_like(near_sums)
    depth = lax.broadcasted_iota(jnp.int32, (LANES, LANES), 0)
    depth = jnp.where(depth < 3 * slots, lax.rem(depth, slots), -1)

    def pick(t, carry):
        near_pick[t] = (depth == info_smem[0, t]).astype(jnp.float32).astype(BF16)
        return carry

    lax.fori_loop(0, tiles, pick, 0)

    for copy in forward:
        copy.wait_recv()
    held = (held_even, held_odd)
    canon_rows = canon.reshape(slots * ROWS, LANES)
    split = []
    for c in range(3):
        layers = []
        for layer in range(groups):
            rows = in_buf[0, layer, c] + in_buf[1, layer, c] + in_buf[2, layer, c]
            canon_rows[pl.ds(layer * ROWS * ROWS + c, ROWS, stride=ROWS), :] = rows
            layers.append(rows)
        value = jnp.concatenate(layers, 0)
        top = value.astype(BF16).astype(jnp.float32)
        rest = value - top
        middle = rest.astype(BF16).astype(jnp.float32)
        stack = jnp.concatenate([top, middle, rest - middle, jnp.zeros_like(value)], 0)
        split.append(jnp.transpose(stack).astype(BF16))
    split = jnp.concatenate(
        [split[c][16 * r : 16 * r + 16] for r in range(LANES // 16) for c in range(3)], 0
    )

    def lane_sums(step, held):
        for c in range(3):
            for r in range(LANES // ROWS):
                rows = pl.ds(c * LANES + r * ROWS, ROWS)
                value = near_sums[rows, :]
                for u in range(UNROLL):
                    total = jnp.sum(held[u, rows, :], 1, keepdims=True)
                    value = jnp.where(lane_iota == step * UNROLL + u, total, value)
                near_sums[rows, :] = value

    def pushes(step, held):
        for u in range(UNROLL):
            t = step * UNROLL + u
            far_block = canon[info_smem[1, t]]
            far = [jnp.broadcast_to(far_block[c : c + 1, :], (ROWS, LANES)) for c in range(3)]
            near = jnp.dot(split, near_pick[t], preferred_element_type=jnp.float32)
            far_sum = [None] * 3
            for r in range(LANES // ROWS):
                rows = [pl.ds(c * LANES + r * ROWS, ROWS) for c in range(3)]
                spots = [(r // 2 * 3 + c) * 16 + r % 2 * ROWS for c in range(3)]
                diff = [near[spots[c] : spots[c] + ROWS, :] - far[c] for c in range(3)]
                weight = jnp.maximum(REACH - inner_rows(diff, diff), 0.0)
                for c in range(3):
                    push = weight * diff[c]
                    held[u, rows[c], :] = push
                    far_sum[c] = far_sum[c] + push if r else push
            place = pl.ds(pl.multiple_of(t * ROWS, ROWS), ROWS)
            for c in range(3):
                far_sums[place, c * LANES : (c + 1) * LANES] = far_sum[c]

    def tile_steps(half, carry):
        for phase in range(2):
            step = half * 2 + phase
            lane_sums(step - 1, held[1 - phase])
            pushes(step, held[phase])
        return carry

    steps = tiles // UNROLL
    lax.fori_loop(0, steps // 2, tile_steps, 0)
    lane_sums(steps - 1, held[1])
    total = pick_rows(take_far, far_sums[...], 2)
    near_total = []
    for c in range(3):
        value = near_sums[pl.ds(c * LANES, LANES), :]
        top = value.astype(BF16)
        low = (value - top.astype(jnp.float32)).astype(BF16)
        near_total.append(
            lax.dot_general(
                take_near,
                jnp.concatenate([top, low], 1),
                (((1,), (1,)), ((), ())),
                preferred_element_type=jnp.float32,
            )
        )
    total = total + jnp.concatenate(near_total, 1)
    for c in range(3):
        ans[:, c, :, :] = total[:, c * LANES : (c + 1) * LANES].reshape(groups, ROWS, LANES)
    backward = []
    for turn, k, step in partners:
        copy = pltpu.make_async_remote_copy(
            src_ref=ans.at[k],
            dst_ref=ret.at[g, step],
            send_sem=back_send.at[turn, step],
            recv_sem=back_recv.at[turn, step],
            device_id=(k, lax.rem(d + doms - step, doms)),
            device_id_type=MESH,
        )
        copy.start()
        backward.append(copy)
    ret[g, 0] = ans[g]

    rim_copy.wait_recv()
    state[blocks] = ghost_in[...]

    def elements(part, carry):
        here = pl.ds(pl.multiple_of(part * ROWS, ROWS), ROWS)
        for side in range(2):
            for kk in range(ROWS):
                b = cb_smem[side, part * ROWS + kk]
                corner_buf[side, pl.ds(kk * ROWS, ROWS), :] = state[b]
        pos = [None] * 4
        vel = [None] * 4
        for side, pair in enumerate(((0, 3), (1, 2))):
            column = [corner_buf[side, pl.ds(x, ROWS, stride=ROWS), :] for x in range(6)]
            for c in pair:
                ids = slot_ref[pl.ds(part * ROWS * 4 + c, ROWS, stride=4), :]
                picked = [gather_lanes(value, ids) for value in column]
                pos[c] = picked[:3]
                vel[c] = picked[3:]
        old = [stress_ref[x, here, :] for x in range(3)]
        forces, new = shell_forces(pos, vel, old)
        for x in range(3):
            stress_out[x, here, :] = new[x]
            for side, pair in enumerate(((0, 3), (1, 2))):
                spread[side, x, here, :] = sum(
                    gather_lanes(forces[c][x], inverse[pl.ds(part * ROWS * 4 + c, ROWS, stride=4), :]) for c in pair
                )
        return carry

    lax.fori_loop(0, blocks // ROWS, elements, 0, unroll=2)

    block_iota = lax.broadcasted_iota(jnp.int32, (blocks + ROWS, blocks), 0)
    hits = jnp.concatenate(
        [(block_iota == cb_ref[side : side + 1, :]).astype(jnp.float32) for side in range(2)], 1
    )
    both = jnp.concatenate(
        [
            jnp.concatenate([spread[side, c] for c in range(3)], 1)
            for side in range(2)
        ],
        0,
    )
    internal = pick_rows(hits, both, 2)
    for c in range(3):
        push_out[pl.ds(c, 1), :] = internal[blocks : blocks + 1, c * LANES : (c + 1) * LANES]
    push_copy = pltpu.make_async_remote_copy(
        src_ref=push_out,
        dst_ref=push_in,
        send_sem=push_sems.at[0],
        recv_sem=push_sems.at[1],
        device_id=(g, right),
        device_id_type=MESH,
    )
    push_copy.start()

    for copy in backward:
        copy.wait_recv()
    answers = jnp.concatenate(
        [ret[:, :, c, :, :].reshape(places, LANES) for c in range(3)], 1
    )
    answers = jnp.concatenate([answers, jnp.zeros((LANES - places, 3 * LANES), jnp.float32)], 0)
    contact = pick_rows(goers, answers, 2)
    push_copy.wait_recv()
    is_rim = lax.broadcasted_iota(jnp.int32, (blocks, LANES), 0) == halo
    factor = DT / mass_ref[...]
    for c in range(3):
        extra = jnp.where(is_rim, push_in[pl.ds(c, 1), :], 0.0)
        cols = slice(c * LANES, (c + 1) * LANES)
        force = contact[:, cols] - internal[0:blocks, cols] - extra
        vel_out[c] = vel_ref[c] + factor * force
    rim_copy.wait_send()
    info_copy.wait_send()
    push_copy.wait_send()
    for copy in forward:
        copy.wait_send()
    for copy in backward:
        copy.wait_send()


def local(
    positions,
    velocity,
    mass,
    stress,
    corner_block,
    corner_slot,
    halo_block,
    contact_owner,
    contact_slot,
    tile_pairs,
    tile_active,
):
    groups = lax.axis_size("group")
    doms = lax.axis_size("dom")
    blocks = corner_block.shape[2]
    nodes = positions.shape[2]
    tiles = tile_pairs.shape[2]
    slots = groups * ROWS
    vmem = pl.BlockSpec(memory_space=pltpu.VMEM)
    i32 = jnp.int32
    f32 = jnp.float32
    out = pl.pallas_call(
        functools.partial(kernel, groups, doms),
        out_shape=[jax.ShapeDtypeStruct((3, blocks, LANES), f32)] * 2,
        in_specs=[pl.BlockSpec(memory_space=pltpu.HBM)] * 11,
        out_specs=[vmem] * 2,
        scratch_shapes=[
            pltpu.VMEM((3, blocks, LANES), f32),
            pltpu.VMEM((3, blocks, LANES), f32),
            pltpu.VMEM((blocks, LANES), f32),
            pltpu.VMEM((3, blocks, LANES), f32),
            pltpu.VMEM((4 * blocks, LANES), i32),
            pltpu.VMEM((4, blocks), i32),
            pltpu.VMEM((1, blocks), i32),
            pltpu.VMEM((1, blocks), i32),
            pltpu.VMEM((2, tiles), i32),
            pltpu.VMEM((1, tiles), i32),
            pltpu.SMEM((4, blocks), i32),
            pltpu.SMEM((ROWS, LANES), i32),
            pltpu.VMEM((ROWS, LANES), i32),
            pltpu.VMEM((ROWS, LANES), i32),
            pltpu.SemaphoreType.DMA((3,)),
            pltpu.SemaphoreType.REGULAR,
            pltpu.SMEM((1, 1), i32),
            pltpu.SemaphoreType.DMA((12,)),
            pltpu.VMEM((blocks + 1, ROWS, LANES), f32),
            pltpu.VMEM((ROWS, LANES), f32),
            pltpu.VMEM((ROWS, LANES), f32),
            pltpu.VMEM((groups, 3, 3, ROWS, LANES), f32),
            pltpu.VMEM((3, groups, 3, ROWS, LANES), f32),
            pltpu.VMEM((groups, 3, ROWS, LANES), f32),
            pltpu.VMEM((groups, 3, 3, ROWS, LANES), f32),
            pltpu.VMEM((slots, ROWS, LANES), f32),
            pltpu.VMEM((tiles + UNROLL, LANES, LANES), jnp.bfloat16),
            pltpu.VMEM((UNROLL, 3 * LANES, LANES), f32),
            pltpu.VMEM((UNROLL, 3 * LANES, LANES), f32),
            pltpu.VMEM((3 * LANES, LANES), f32),
            pltpu.VMEM((tiles * ROWS, 3 * LANES), f32),
            pltpu.VMEM((4 * blocks, LANES), jnp.int32),
            pltpu.VMEM((4 * blocks // LANES, LANES, LANES), f32),
            pltpu.VMEM((2, ROWS * ROWS, LANES), f32),
            pltpu.VMEM((2, 3, blocks, LANES), f32),
            pltpu.VMEM((ROWS, LANES), f32),
            pltpu.VMEM((ROWS, LANES), f32),
            pltpu.SemaphoreType.DMA((groups, 3)),
            pltpu.SemaphoreType.DMA((groups, 3)),
            pltpu.SemaphoreType.DMA((groups, 3)),
            pltpu.SemaphoreType.DMA((groups, 3)),
            pltpu.SemaphoreType.DMA((2,)),
            pltpu.SemaphoreType.DMA((2,)),
        ],
        compiler_params=pltpu.CompilerParams(
            collective_id=0, has_side_effects=True, vmem_limit_bytes=32 * 1024 * 1024
        ),
        name="shell_step",
    )(
        pltpu.with_memory_space_constraint(positions.reshape(3, blocks, LANES), pltpu.HBM),
        pltpu.with_memory_space_constraint(velocity.reshape(3, blocks, LANES), pltpu.HBM),
        pltpu.with_memory_space_constraint(mass.reshape(blocks, LANES), pltpu.HBM),
        pltpu.with_memory_space_constraint(stress.reshape(3, blocks, LANES), pltpu.HBM),
        pltpu.with_memory_space_constraint(corner_slot.reshape(4, blocks, LANES).transpose(1, 0, 2).reshape(4 * blocks, LANES), pltpu.HBM),
        pltpu.with_memory_space_constraint(corner_block.reshape(4, blocks), pltpu.HBM),
        pltpu.with_memory_space_constraint(contact_owner, pltpu.HBM),
        pltpu.with_memory_space_constraint(contact_slot, pltpu.HBM),
        pltpu.with_memory_space_constraint(tile_pairs.reshape(2, tiles), pltpu.HBM),
        pltpu.with_memory_space_constraint(tile_active, pltpu.HBM),
        halo_block,
    )
    return out[0].reshape(1, 3, nodes), out[1].reshape(1, 3, nodes)


def solution(mesh):
    in_specs = (
        P("group", None, "dom"),
        P("group", None, "dom"),
        P("group", "dom"),
        P("group", None, "dom"),
        P("group", None, "dom"),
        P("group", None, "dom"),
        P("group", "dom"),
        P("group", "dom"),
        P("group", "dom"),
        P("group", None, "dom"),
        P("group", "dom"),
    )
    out_specs = (P("group", None, "dom"), P("group", None, "dom"))
    return jax.shard_map(local, mesh=mesh, in_specs=in_specs, out_specs=out_specs, check_vma=False)
```

```python
import functools

import jax
import jax.numpy as jnp
from jax import lax
from jax.experimental import pallas as pl
from jax.experimental.pallas import tpu as pltpu
from jax.sharding import PartitionSpec as P

LANES = 128
ROWS = 8
DT = 0.5
STIFF = 2.0
POISSON = 0.3
HOURGLASS = 0.1
PENALTY = 4.0
REACH = 1.0
MESH = pl.DeviceIdType.MESH
HIGHEST = lax.Precision.HIGHEST
BF16 = jnp.bfloat16
UNROLL = 3


def inner_rows(a, b):
    return a[0] * b[0] + a[1] * b[1] + a[2] * b[2]


def cross_rows(a, b):
    return (
        a[1] * b[2] - a[2] * b[1],
        a[2] * b[0] - a[0] * b[2],
        a[0] * b[1] - a[1] * b[0],
    )


def minus(a, b):
    return tuple(x - y for x, y in zip(a, b))


def scaled(a, s):
    return tuple(x * s for x in a)


def gather_lanes(value, index):
    return jnp.take_along_axis(value, index, axis=1, mode="promise_in_bounds")


def pieces(value, count):
    parts = []
    for _ in range(count - 1):
        top = value.astype(BF16).astype(jnp.float32)
        parts.append(top)
        value = value - top
    parts.append(value)
    return jnp.concatenate(parts, 0).astype(BF16)


def pick_rows(chosen, value, count):
    lhs = jnp.concatenate([chosen] * count, 1).astype(BF16)
    return jnp.dot(lhs, pieces(value, count), preferred_element_type=jnp.float32)


def sort_rows(rows, sub):
    rows = list(rows)
    for k in range(1, 8):
        up = None if k < 4 or k == 7 else (sub & (1 << (k - 4))) == 0
        for j in range(k - 1, -1, -1):
            if j >= 4:
                gap = 1 << (j - 4)
                keep = (sub & gap) == 0
                if up is not None:
                    keep = keep == up
                for r in range(16):
                    other = jnp.take_along_axis(
                        rows[r], sub ^ gap, axis=0, mode="promise_in_bounds"
                    )
                    rows[r] = jnp.where(
                        keep, jnp.minimum(rows[r], other), jnp.maximum(rows[r], other)
                    )
                continue
            for r in range(16):
                far = r | (1 << j)
                if far == r:
                    continue
                low = jnp.minimum(rows[r], rows[far])
                high = jnp.maximum(rows[r], rows[far])
                if up is not None:
                    low, high = jnp.where(up, low, high), jnp.where(up, high, low)
                elif k < 4 and r & (1 << k):
                    low, high = high, low
                rows[r], rows[far] = low, high
    return rows


def shell_forces(pos, vel, stress_old):
    diag_a = minus(pos[2], pos[0])
    diag_b = minus(pos[3], pos[1])
    normal = cross_rows(diag_a, diag_b)
    inv_j = lax.rsqrt(inner_rows(normal, normal))
    axis_three = scaled(normal, inv_j)
    tangent = minus(diag_a, diag_b)
    tangent = minus(tangent, scaled(axis_three, inner_rows(tangent, axis_three)))
    axis_one = scaled(tangent, lax.rsqrt(inner_rows(tangent, tangent)))
    axis_two = cross_rows(axis_three, axis_one)
    along_a = inner_rows(diag_a, axis_one)
    across_a = inner_rows(diag_a, axis_two)
    along_b = inner_rows(diag_b, axis_one)
    across_b = inner_rows(diag_b, axis_two)
    speed_a = minus(vel[2], vel[0])
    speed_b = minus(vel[3], vel[1])
    slide_a = inner_rows(speed_a, axis_one)
    lift_a = inner_rows(speed_a, axis_two)
    slide_b = inner_rows(speed_b, axis_one)
    lift_b = inner_rows(speed_b, axis_two)
    rate_xx = (across_b * slide_a - across_a * slide_b) * inv_j
    rate_yy = (along_a * lift_b - along_b * lift_a) * inv_j
    rate_xy = (
        across_b * lift_a - across_a * lift_b + along_a * slide_b - along_b * slide_a
    ) * inv_j
    s_xx = stress_old[0] + (DT * STIFF) * (rate_xx + POISSON * rate_yy)
    s_yy = stress_old[1] + (DT * STIFF) * (POISSON * rate_xx + rate_yy)
    s_xy = stress_old[2] + (DT * STIFF * 0.5 * (1.0 - POISSON)) * rate_xy
    half_xx, half_yy, half_xy = 0.5 * s_xx, 0.5 * s_yy, 0.5 * s_xy
    fx0 = along_b * half_xy - across_b * half_xx
    fy0 = along_b * half_yy - across_b * half_xy
    fx1 = across_a * half_xx - along_a * half_xy
    fy1 = across_a * half_xy - along_a * half_yy
    forces = [[], [], [], []]
    for c in range(3):
        mode = HOURGLASS * (vel[0][c] - vel[1][c] + vel[2][c] - vel[3][c])
        first = fx0 * axis_one[c] + fy0 * axis_two[c]
        second = fx1 * axis_one[c] + fy1 * axis_two[c]
        forces[0].append(mode + first)
        forces[1].append(second - mode)
        forces[2].append(mode - first)
        forces[3].append(-mode - second)
    return forces, (s_xx, s_yy, s_xy)


def kernel(
    groups,
    doms,
    pos_hbm,
    vel_hbm,
    mass_hbm,
    stress_hbm,
    slot_hbm,
    cb_hbm,
    owner_hbm,
    spot_hbm,
    pair_hbm,
    active_hbm,
    halo_hbm,
    vel_out,
    stress_out,
    pos_ref,
    vel_ref,
    mass_ref,
    stress_ref,
    slot_ref,
    cb_ref,
    owner_ref,
    spot_ref,
    pair_ref,
    active_ref,
    cb_smem,
    info_smem,
    info_out,
    info_in,
    info_sems,
    rim_ready,
    halo_smem,
    in_sems,
    state,
    rim,
    ghost_in,
    out_buf,
    in_buf,
    ans,
    ret,
    canon,
    near_pick,
    held_even,
    held_odd,
    near_sums,
    far_sums,
    inverse,
    sort_buf,
    corner_buf,
    spread,
    push_out,
    push_in,
    fwd_send,
    fwd_recv,
    back_send,
    back_recv,
    rim_sems,
    push_sems,
):
    g = lax.axis_index("group")
    d = lax.axis_index("dom")
    blocks = mass_ref.shape[0]
    tiles = pair_ref.shape[1]
    slots = groups * ROWS
    left = lax.rem(d + doms - 1, doms)
    right = lax.rem(d + 1, doms)
    partners = []
    for step in (2, 1, 0):
        for turn in (2, 3, 1, 0):
            if turn == 0 and step == 0:
                continue
            partners.append((turn, lax.rem(g + turn, groups), step))

    barrier = pltpu.get_barrier_semaphore()
    for turn, k, step in partners:
        pl.semaphore_signal(
            barrier,
            inc=1,
            device_id=(k, lax.rem(d + doms - step, doms)),
            device_id_type=MESH,
        )

    sources = (
        (pos_hbm, pos_ref),
        (owner_hbm, owner_ref),
        (spot_hbm, spot_ref),
        (pair_hbm, pair_ref),
        (active_hbm, active_ref),
        (vel_hbm, vel_ref),
        (halo_hbm, halo_smem),
        (slot_hbm, slot_ref),
        (cb_hbm, cb_ref),
        (cb_hbm, cb_smem),
        (stress_hbm, stress_ref),
        (mass_hbm, mass_ref),
    )
    loads = []
    for n, (source, target) in enumerate(sources):
        copy = pltpu.make_async_copy(source, target, in_sems.at[n])
        copy.start()
        loads.append(copy)
    for copy in loads[:3]:
        copy.wait()
    sub_iota = lax.broadcasted_iota(jnp.int32, (ROWS, LANES), 0)
    lane_iota = lax.broadcasted_iota(jnp.int32, (ROWS, LANES), 1)
    owner = owner_ref[...]
    step_of = lax.rem(lax.rem(owner, doms) - d + 1 + doms, doms)
    goal = (lax.div(owner, doms) * 3 + step_of) * ROWS + lax.rem(spot_ref[...], ROWS)
    goal = jnp.where(owner >= 0, goal, -1)
    places = groups * 3 * ROWS
    chosen = (
        lax.broadcasted_iota(jnp.int32, (places, blocks), 0) == goal
    ).astype(jnp.float32)
    everywhere = jnp.concatenate([pos_ref[c] for c in range(3)], 1)
    packed = pick_rows(chosen, everywhere, 3)
    for c in range(3):
        out_buf[:, :, c, :, :] = packed[:, c * LANES : (c + 1) * LANES].reshape(
            groups, 3, ROWS, LANES
        )
    for copy in loads[3:5]:
        copy.wait()
    info_out[0:2, 0:tiles] = pair_ref[...]
    info_out[2:3, 0:tiles] = active_ref[...]
    pl.semaphore_wait(barrier, len(partners))
    pl.semaphore_signal(rim_ready, inc=1, device_id=(g, right), device_id_type=MESH)

    info_copy = pltpu.make_async_remote_copy(
        src_ref=info_out,
        dst_ref=info_in,
        send_sem=info_sems.at[0],
        recv_sem=info_sems.at[1],
        device_id=(g, right),
        device_id_type=MESH,
    )
    info_copy.start()

    forward = []
    for turn, k, step in partners:
        copy = pltpu.make_async_remote_copy(
            src_ref=out_buf.at[k, step],
            dst_ref=in_buf.at[step, g],
            send_sem=fwd_send.at[turn, step],
            recv_sem=fwd_recv.at[turn, step],
            device_id=(k, lax.rem(d + step, doms)),
            device_id_type=MESH,
        )
        copy.start()
        forward.append(copy)
    in_buf[0, g] = out_buf[g, 0]

    for copy in loads[5:7]:
        copy.wait()
    halo = halo_smem[0, 0]
    state_rows = state.reshape((blocks + 1) * ROWS, LANES)
    for c in range(3):
        state_rows[pl.ds(c, blocks, stride=ROWS), :] = pos_ref[c]
        state_rows[pl.ds(3 + c, blocks, stride=ROWS), :] = vel_ref[c]
    rim[...] = state[halo]
    for copy in loads[7:]:
        copy.wait()
    goers = jnp.transpose(jnp.concatenate([chosen, jnp.zeros((LANES - places, blocks), jnp.float32)], 0))

    wide_iota = lax.broadcasted_iota(jnp.int32, (LANES, LANES), 1)
    for half in range(4 * blocks // LANES):
        rows = pl.ds(half * LANES, LANES)
        keys = jnp.transpose((slot_ref[rows, :] * LANES + wide_iota).astype(jnp.float32))
        keys = sort_rows([keys[r * ROWS : (r + 1) * ROWS, :] for r in range(16)], sub_iota)
        for r in range(16):
            sort_buf[half, pl.ds(r, ROWS, stride=16), :] = keys[r]
        inverse[rows, :] = jnp.transpose(sort_buf[half]).astype(jnp.int32) - wide_iota * LANES

    block_iota = lax.broadcasted_iota(jnp.int32, (blocks + 2 * ROWS, blocks), 0)
    hits = jnp.concatenate(
        [(block_iota == cb_ref[side : side + 1, :]).astype(jnp.float32) for side in range(2)], 1
    )
    hits = jnp.concatenate([hits, hits], 1).astype(BF16)
    factor = DT / mass_ref[...]
    pl.semaphore_wait(rim_ready, 1)
    rim_copy = pltpu.make_async_remote_copy(
        src_ref=rim,
        dst_ref=ghost_in,
        send_sem=rim_sems.at[0],
        recv_sem=rim_sems.at[1],
        device_id=(g, left),
        device_id_type=MESH,
    )
    rim_copy.start()

    info_copy.wait_recv()
    to_smem = pltpu.make_async_copy(info_in, info_smem, info_sems.at[2])
    to_smem.start()
    to_smem.wait()
    slot_iota = lax.broadcasted_iota(jnp.int32, (slots, tiles), 0)
    gain = PENALTY * info_in[2:3, 0:tiles].astype(jnp.float32)
    take_near = jnp.where(slot_iota == info_in[0:1, 0:tiles], gain, 0.0).astype(BF16)
    take_far = jnp.where(slot_iota == info_in[1:2, 0:tiles], -gain, 0.0).astype(BF16)
    tile_iota = lax.broadcasted_iota(jnp.int32, (tiles, 2 * LANES), 0)
    column = lax.broadcasted_iota(jnp.int32, (tiles, 2 * LANES), 1)
    same = ((column & (LANES - 1)) == tile_iota).astype(BF16)
    take_near = jnp.dot(take_near, same, preferred_element_type=jnp.float32).astype(BF16)
    tile_iota = lax.broadcasted_iota(jnp.int32, (tiles, tiles * ROWS), 0)
    column = lax.broadcasted_iota(jnp.int32, (tiles, tiles * ROWS), 1)
    same = (lax.div(column, ROWS) == tile_iota).astype(BF16)
    take_far = jnp.dot(take_far, same, preferred_element_type=jnp.float32)
    near_sums[...] = jnp.zeros_like(near_sums)
    depth = lax.broadcasted_iota(jnp.int32, (LANES, LANES), 0)
    depth = jnp.where(depth < 3 * slots, lax.rem(depth, slots), -1)

    def pick(t, carry):
        near_pick[t] = (depth == info_smem[0, t]).astype(jnp.float32).astype(BF16)
        return carry

    lax.fori_loop(0, tiles, pick, 0)

    for copy in forward:
        copy.wait_recv()
    held = (held_even, held_odd)
    canon_rows = canon.reshape(slots * ROWS, LANES)
    split = []
    for c in range(3):
        layers = []
        for layer in range(groups):
            rows = in_buf[0, layer, c] + in_buf[1, layer, c] + in_buf[2, layer, c]
            canon_rows[pl.ds(layer * ROWS * ROWS + c, ROWS, stride=ROWS), :] = rows
            layers.append(rows)
        value = jnp.concatenate(layers, 0)
        top = value.astype(BF16).astype(jnp.float32)
        rest = value - top
        middle = rest.astype(BF16).astype(jnp.float32)
        stack = jnp.concatenate([top, middle, rest - middle, jnp.zeros_like(value)], 0)
        split.append(jnp.transpose(stack).astype(BF16))
    split = jnp.concatenate(
        [split[c][16 * r : 16 * r + 16] for r in range(LANES // 16) for c in range(3)], 0
    )

    def lane_sums(step, held):
        for c in range(3):
            for r in range(LANES // ROWS):
                rows = pl.ds(c * LANES + r * ROWS, ROWS)
                value = near_sums[rows, :]
                for u in range(UNROLL):
                    total = jnp.sum(held[u, rows, :], 1, keepdims=True)
                    value = jnp.where(lane_iota == step * UNROLL + u, total, value)
                near_sums[rows, :] = value

    def pushes(step, held):
        for u in range(UNROLL):
            t = step * UNROLL + u
            far_block = canon[info_smem[1, t]]
            far = [jnp.broadcast_to(far_block[c : c + 1, :], (ROWS, LANES)) for c in range(3)]
            near = jnp.dot(split, near_pick[t], preferred_element_type=jnp.float32)
            far_sum = [None] * 3
            for r in range(LANES // ROWS):
                rows = [pl.ds(c * LANES + r * ROWS, ROWS) for c in range(3)]
                spots = [(r // 2 * 3 + c) * 16 + r % 2 * ROWS for c in range(3)]
                diff = [near[spots[c] : spots[c] + ROWS, :] - far[c] for c in range(3)]
                weight = jnp.maximum(REACH - inner_rows(diff, diff), 0.0)
                for c in range(3):
                    push = weight * diff[c]
                    held[u, rows[c], :] = push
                    far_sum[c] = far_sum[c] + push if r else push
            place = pl.ds(pl.multiple_of(t * ROWS, ROWS), ROWS)
            for c in range(3):
                far_sums[place, c * LANES : (c + 1) * LANES] = far_sum[c]

    def tile_steps(half, carry):
        for phase in range(2):
            step = half * 2 + phase
            lane_sums(step - 1, held[1 - phase])
            pushes(step, held[phase])
        return carry

    steps = tiles // UNROLL
    lax.fori_loop(0, steps // 2, tile_steps, 0)
    lane_sums(steps - 1, held[1])
    total = pick_rows(take_far, far_sums[...], 2)
    near_total = []
    for c in range(3):
        value = near_sums[pl.ds(c * LANES, LANES), :]
        top = value.astype(BF16)
        low = (value - top.astype(jnp.float32)).astype(BF16)
        near_total.append(
            lax.dot_general(
                take_near,
                jnp.concatenate([top, low], 1),
                (((1,), (1,)), ((), ())),
                preferred_element_type=jnp.float32,
            )
        )
    total = total + jnp.concatenate(near_total, 1)
    for c in range(3):
        ans[:, c, :, :] = total[:, c * LANES : (c + 1) * LANES].reshape(groups, ROWS, LANES)
    backward = []
    for turn, k, step in partners:
        copy = pltpu.make_async_remote_copy(
            src_ref=ans.at[k],
            dst_ref=ret.at[g, step],
            send_sem=back_send.at[turn, step],
            recv_sem=back_recv.at[turn, step],
            device_id=(k, lax.rem(d + doms - step, doms)),
            device_id_type=MESH,
        )
        copy.start()
        backward.append(copy)
    ret[g, 0] = ans[g]

    rim_copy.wait_recv()
    state[blocks] = ghost_in[...]

    def elements(part, carry):
        here = pl.ds(pl.multiple_of(part * ROWS, ROWS), ROWS)
        for side in range(2):
            for kk in range(ROWS):
                b = cb_smem[side, part * ROWS + kk]
                corner_buf[side, pl.ds(kk * ROWS, ROWS), :] = state[b]
        pos = [None] * 4
        vel = [None] * 4
        for side, pair in enumerate(((0, 3), (1, 2))):
            column = [corner_buf[side, pl.ds(x, ROWS, stride=ROWS), :] for x in range(6)]
            for c in pair:
                ids = slot_ref[pl.ds(part * ROWS * 4 + c, ROWS, stride=4), :]
                picked = [gather_lanes(value, ids) for value in column]
                pos[c] = picked[:3]
                vel[c] = picked[3:]
        old = [stress_ref[x, here, :] for x in range(3)]
        forces, new = shell_forces(pos, vel, old)
        for x in range(3):
            stress_out[x, here, :] = new[x]
            for side, pair in enumerate(((0, 3), (1, 2))):
                spread[side, x, here, :] = sum(
                    gather_lanes(forces[c][x], inverse[pl.ds(part * ROWS * 4 + c, ROWS, stride=4), :]) for c in pair
                )
        return carry

    lax.fori_loop(0, blocks // ROWS, elements, 0, unroll=2)

    both = jnp.concatenate(
        [
            jnp.concatenate([spread[side, c] for c in range(3)], 1)
            for side in range(2)
        ],
        0,
    )
    both = pieces(both, 2)
    shared = jnp.dot(
        hits[blocks : blocks + 2 * ROWS], both, preferred_element_type=jnp.float32
    )
    for c in range(3):
        push_out[pl.ds(c, 1), :] = shared[0:1, c * LANES : (c + 1) * LANES]
    push_copy = pltpu.make_async_remote_copy(
        src_ref=push_out,
        dst_ref=push_in,
        send_sem=push_sems.at[0],
        recv_sem=push_sems.at[1],
        device_id=(g, right),
        device_id_type=MESH,
    )
    push_copy.start()
    internal = jnp.dot(hits[0:blocks], both, preferred_element_type=jnp.float32)

    for copy in backward:
        copy.wait_recv()
    answers = jnp.concatenate(
        [ret[:, :, c, :, :].reshape(places, LANES) for c in range(3)], 1
    )
    answers = jnp.concatenate([answers, jnp.zeros((LANES - places, 3 * LANES), jnp.float32)], 0)
    contact = pick_rows(goers, answers, 2)
    push_copy.wait_recv()
    is_rim = lax.broadcasted_iota(jnp.int32, (blocks, LANES), 0) == halo
    for c in range(3):
        extra = jnp.where(is_rim, push_in[pl.ds(c, 1), :], 0.0)
        cols = slice(c * LANES, (c + 1) * LANES)
        force = contact[:, cols] - internal[:, cols] - extra
        vel_out[c] = vel_ref[c] + factor * force
    rim_copy.wait_send()
    info_copy.wait_send()
    push_copy.wait_send()
    for copy in forward:
        copy.wait_send()
    for copy in backward:
        copy.wait_send()


def local(
    positions,
    velocity,
    mass,
    stress,
    corner_block,
    corner_slot,
    halo_block,
    contact_owner,
    contact_slot,
    tile_pairs,
    tile_active,
):
    groups = lax.axis_size("group")
    doms = lax.axis_size("dom")
    blocks = corner_block.shape[2]
    nodes = positions.shape[2]
    tiles = tile_pairs.shape[2]
    slots = groups * ROWS
    vmem = pl.BlockSpec(memory_space=pltpu.VMEM)
    i32 = jnp.int32
    f32 = jnp.float32
    out = pl.pallas_call(
        functools.partial(kernel, groups, doms),
        out_shape=[jax.ShapeDtypeStruct((3, blocks, LANES), f32)] * 2,
        in_specs=[pl.BlockSpec(memory_space=pltpu.HBM)] * 11,
        out_specs=[vmem] * 2,
        scratch_shapes=[
            pltpu.VMEM((3, blocks, LANES), f32),
            pltpu.VMEM((3, blocks, LANES), f32),
            pltpu.VMEM((blocks, LANES), f32),
            pltpu.VMEM((3, blocks, LANES), f32),
            pltpu.VMEM((4 * blocks, LANES), i32),
            pltpu.VMEM((4, blocks), i32),
            pltpu.VMEM((1, blocks), i32),
            pltpu.VMEM((1, blocks), i32),
            pltpu.VMEM((2, tiles), i32),
            pltpu.VMEM((1, tiles), i32),
            pltpu.SMEM((4, blocks), i32),
            pltpu.SMEM((ROWS, LANES), i32),
            pltpu.VMEM((ROWS, LANES), i32),
            pltpu.VMEM((ROWS, LANES), i32),
            pltpu.SemaphoreType.DMA((3,)),
            pltpu.SemaphoreType.REGULAR,
            pltpu.SMEM((1, 1), i32),
            pltpu.SemaphoreType.DMA((12,)),
            pltpu.VMEM((blocks + 1, ROWS, LANES), f32),
            pltpu.VMEM((ROWS, LANES), f32),
            pltpu.VMEM((ROWS, LANES), f32),
            pltpu.VMEM((groups, 3, 3, ROWS, LANES), f32),
            pltpu.VMEM((3, groups, 3, ROWS, LANES), f32),
            pltpu.VMEM((groups, 3, ROWS, LANES), f32),
            pltpu.VMEM((groups, 3, 3, ROWS, LANES), f32),
            pltpu.VMEM((slots, ROWS, LANES), f32),
            pltpu.VMEM((tiles + UNROLL, LANES, LANES), jnp.bfloat16),
            pltpu.VMEM((UNROLL, 3 * LANES, LANES), f32),
            pltpu.VMEM((UNROLL, 3 * LANES, LANES), f32),
            pltpu.VMEM((3 * LANES, LANES), f32),
            pltpu.VMEM((tiles * ROWS, 3 * LANES), f32),
            pltpu.VMEM((4 * blocks, LANES), jnp.int32),
            pltpu.VMEM((4 * blocks // LANES, LANES, LANES), f32),
            pltpu.VMEM((2, ROWS * ROWS, LANES), f32),
            pltpu.VMEM((2, 3, blocks, LANES), f32),
            pltpu.VMEM((ROWS, LANES), f32),
            pltpu.VMEM((ROWS, LANES), f32),
            pltpu.SemaphoreType.DMA((groups, 3)),
            pltpu.SemaphoreType.DMA((groups, 3)),
            pltpu.SemaphoreType.DMA((groups, 3)),
            pltpu.SemaphoreType.DMA((groups, 3)),
            pltpu.SemaphoreType.DMA((2,)),
            pltpu.SemaphoreType.DMA((2,)),
        ],
        compiler_params=pltpu.CompilerParams(
            collective_id=0, has_side_effects=True, vmem_limit_bytes=32 * 1024 * 1024
        ),
        name="shell_step",
    )(
        pltpu.with_memory_space_constraint(positions.reshape(3, blocks, LANES), pltpu.HBM),
        pltpu.with_memory_space_constraint(velocity.reshape(3, blocks, LANES), pltpu.HBM),
        pltpu.with_memory_space_constraint(mass.reshape(blocks, LANES), pltpu.HBM),
        pltpu.with_memory_space_constraint(stress.reshape(3, blocks, LANES), pltpu.HBM),
        pltpu.with_memory_space_constraint(corner_slot.reshape(4, blocks, LANES).transpose(1, 0, 2).reshape(4 * blocks, LANES), pltpu.HBM),
        pltpu.with_memory_space_constraint(corner_block.reshape(4, blocks), pltpu.HBM),
        pltpu.with_memory_space_constraint(contact_owner, pltpu.HBM),
        pltpu.with_memory_space_constraint(contact_slot, pltpu.HBM),
        pltpu.with_memory_space_constraint(tile_pairs.reshape(2, tiles), pltpu.HBM),
        pltpu.with_memory_space_constraint(tile_active, pltpu.HBM),
        halo_block,
    )
    return out[0].reshape(1, 3, nodes), out[1].reshape(1, 3, nodes)


def solution(mesh):
    in_specs = (
        P("group", None, "dom"),
        P("group", None, "dom"),
        P("group", "dom"),
        P("group", None, "dom"),
        P("group", None, "dom"),
        P("group", None, "dom"),
        P("group", "dom"),
        P("group", "dom"),
        P("group", "dom"),
        P("group", None, "dom"),
        P("group", "dom"),
    )
    out_specs = (P("group", None, "dom"), P("group", None, "dom"))
    return jax.shard_map(local, mesh=mesh, in_specs=in_specs, out_specs=out_specs, check_vma=False)
```

```python
import functools

import jax
import jax.numpy as jnp
from jax import lax
from jax.experimental import pallas as pl
from jax.experimental.pallas import tpu as pltpu
from jax.sharding import PartitionSpec as P

LANES = 128
ROWS = 8
DT = 0.5
STIFF = 2.0
POISSON = 0.3
HOURGLASS = 0.1
PENALTY = 4.0
REACH = 1.0
MESH = pl.DeviceIdType.MESH
HIGHEST = lax.Precision.HIGHEST
BF16 = jnp.bfloat16
UNROLL = 3


def inner_rows(a, b):
    return a[0] * b[0] + a[1] * b[1] + a[2] * b[2]


def cross_rows(a, b):
    return (
        a[1] * b[2] - a[2] * b[1],
        a[2] * b[0] - a[0] * b[2],
        a[0] * b[1] - a[1] * b[0],
    )


def minus(a, b):
    return tuple(x - y for x, y in zip(a, b))


def scaled(a, s):
    return tuple(x * s for x in a)


def gather_lanes(value, index):
    return jnp.take_along_axis(value, index, axis=1, mode="promise_in_bounds")


def pieces(value, count):
    parts = []
    for _ in range(count - 1):
        top = value.astype(BF16).astype(jnp.float32)
        parts.append(top)
        value = value - top
    parts.append(value)
    return jnp.concatenate(parts, 0).astype(BF16)


def pick_rows(chosen, value, count):
    lhs = jnp.concatenate([chosen] * count, 1).astype(BF16)
    return jnp.dot(lhs, pieces(value, count), preferred_element_type=jnp.float32)


def sort_rows(rows, sub):
    rows = list(rows)
    for k in range(1, 8):
        up = None if k < 4 or k == 7 else (sub & (1 << (k - 4))) == 0
        for j in range(k - 1, -1, -1):
            if j >= 4:
                gap = 1 << (j - 4)
                keep = (sub & gap) == 0
                if up is not None:
                    keep = keep == up
                for r in range(16):
                    other = jnp.take_along_axis(
                        rows[r], sub ^ gap, axis=0, mode="promise_in_bounds"
                    )
                    rows[r] = jnp.where(
                        keep, jnp.minimum(rows[r], other), jnp.maximum(rows[r], other)
                    )
                continue
            for r in range(16):
                far = r | (1 << j)
                if far == r:
                    continue
                low = jnp.minimum(rows[r], rows[far])
                high = jnp.maximum(rows[r], rows[far])
                if up is not None:
                    low, high = jnp.where(up, low, high), jnp.where(up, high, low)
                elif k < 4 and r & (1 << k):
                    low, high = high, low
                rows[r], rows[far] = low, high
    return rows


def shell_forces(pos, vel, stress_old):
    diag_a = minus(pos[2], pos[0])
    diag_b = minus(pos[3], pos[1])
    normal = cross_rows(diag_a, diag_b)
    inv_j = lax.rsqrt(inner_rows(normal, normal))
    axis_three = scaled(normal, inv_j)
    tangent = minus(diag_a, diag_b)
    tangent = minus(tangent, scaled(axis_three, inner_rows(tangent, axis_three)))
    axis_one = scaled(tangent, lax.rsqrt(inner_rows(tangent, tangent)))
    axis_two = cross_rows(axis_three, axis_one)
    along_a = inner_rows(diag_a, axis_one)
    across_a = inner_rows(diag_a, axis_two)
    along_b = inner_rows(diag_b, axis_one)
    across_b = inner_rows(diag_b, axis_two)
    speed_a = minus(vel[2], vel[0])
    speed_b = minus(vel[3], vel[1])
    slide_a = inner_rows(speed_a, axis_one)
    lift_a = inner_rows(speed_a, axis_two)
    slide_b = inner_rows(speed_b, axis_one)
    lift_b = inner_rows(speed_b, axis_two)
    rate_xx = (across_b * slide_a - across_a * slide_b) * inv_j
    rate_yy = (along_a * lift_b - along_b * lift_a) * inv_j
    rate_xy = (
        across_b * lift_a - across_a * lift_b + along_a * slide_b - along_b * slide_a
    ) * inv_j
    s_xx = stress_old[0] + (DT * STIFF) * (rate_xx + POISSON * rate_yy)
    s_yy = stress_old[1] + (DT * STIFF) * (POISSON * rate_xx + rate_yy)
    s_xy = stress_old[2] + (DT * STIFF * 0.5 * (1.0 - POISSON)) * rate_xy
    half_xx, half_yy, half_xy = 0.5 * s_xx, 0.5 * s_yy, 0.5 * s_xy
    fx0 = along_b * half_xy - across_b * half_xx
    fy0 = along_b * half_yy - across_b * half_xy
    fx1 = across_a * half_xx - along_a * half_xy
    fy1 = across_a * half_xy - along_a * half_yy
    forces = [[], [], [], []]
    for c in range(3):
        mode = HOURGLASS * (vel[0][c] - vel[1][c] + vel[2][c] - vel[3][c])
        first = fx0 * axis_one[c] + fy0 * axis_two[c]
        second = fx1 * axis_one[c] + fy1 * axis_two[c]
        forces[0].append(mode + first)
        forces[1].append(second - mode)
        forces[2].append(mode - first)
        forces[3].append(-mode - second)
    return forces, (s_xx, s_yy, s_xy)


def kernel(
    groups,
    doms,
    pos_hbm,
    vel_hbm,
    mass_hbm,
    stress_hbm,
    slot_hbm,
    cb_hbm,
    owner_hbm,
    spot_hbm,
    pair_hbm,
    active_hbm,
    halo_hbm,
    vel_out,
    stress_out,
    pos_ref,
    vel_ref,
    mass_ref,
    stress_ref,
    slot_ref,
    cb_ref,
    owner_ref,
    spot_ref,
    pair_ref,
    active_ref,
    cb_smem,
    info_smem,
    info_out,
    info_in,
    info_sems,
    rim_ready,
    halo_smem,
    in_sems,
    state,
    rim,
    ghost_in,
    out_buf,
    in_buf,
    ans,
    ret,
    canon,
    near_pick,
    held_even,
    held_odd,
    near_sums,
    far_sums,
    inverse,
    sort_buf,
    corner_buf,
    spread,
    push_out,
    push_in,
    fwd_send,
    fwd_recv,
    back_send,
    back_recv,
    rim_sems,
    push_sems,
):
    g = lax.axis_index("group")
    d = lax.axis_index("dom")
    blocks = mass_ref.shape[0]
    tiles = pair_ref.shape[1]
    slots = groups * ROWS
    left = lax.rem(d + doms - 1, doms)
    right = lax.rem(d + 1, doms)
    partners = []
    for step in (2, 1, 0):
        for turn in (2, 3, 1, 0):
            if turn == 0 and step == 0:
                continue
            partners.append((turn, lax.rem(g + turn, groups), step))

    barrier = pltpu.get_barrier_semaphore()
    for turn, k, step in partners:
        pl.semaphore_signal(
            barrier,
            inc=1,
            device_id=(k, lax.rem(d + doms - step, doms)),
            device_id_type=MESH,
        )

    sources = (
        (pos_hbm, pos_ref),
        (owner_hbm, owner_ref),
        (spot_hbm, spot_ref),
        (pair_hbm, pair_ref),
        (active_hbm, active_ref),
        (vel_hbm, vel_ref),
        (halo_hbm, halo_smem),
        (slot_hbm, slot_ref),
        (cb_hbm, cb_ref),
        (cb_hbm, cb_smem),
        (stress_hbm, stress_ref),
        (mass_hbm, mass_ref),
    )
    loads = []
    for n, (source, target) in enumerate(sources):
        copy = pltpu.make_async_copy(source, target, in_sems.at[n])
        copy.start()
        loads.append(copy)
    for copy in loads[:3]:
        copy.wait()
    sub_iota = lax.broadcasted_iota(jnp.int32, (ROWS, LANES), 0)
    lane_iota = lax.broadcasted_iota(jnp.int32, (ROWS, LANES), 1)
    owner = owner_ref[...]
    step_of = lax.rem(lax.rem(owner, doms) - d + 1 + doms, doms)
    goal = (lax.div(owner, doms) * 3 + step_of) * ROWS + lax.rem(spot_ref[...], ROWS)
    goal = jnp.where(owner >= 0, goal, -1)
    places = groups * 3 * ROWS
    chosen = (
        lax.broadcasted_iota(jnp.int32, (places, blocks), 0) == goal
    ).astype(jnp.float32)
    everywhere = jnp.concatenate([pos_ref[c] for c in range(3)], 1)
    packed = pick_rows(chosen, everywhere, 3)
    for c in range(3):
        out_buf[:, :, c, :, :] = packed[:, c * LANES : (c + 1) * LANES].reshape(
            groups, 3, ROWS, LANES
        )
    for copy in loads[3:5]:
        copy.wait()
    info_out[0:2, 0:tiles] = pair_ref[...]
    info_out[2:3, 0:tiles] = active_ref[...]
    pl.semaphore_wait(barrier, len(partners))
    pl.semaphore_signal(rim_ready, inc=1, device_id=(g, right), device_id_type=MESH)

    info_copy = pltpu.make_async_remote_copy(
        src_ref=info_out,
        dst_ref=info_in,
        send_sem=info_sems.at[0],
        recv_sem=info_sems.at[1],
        device_id=(g, right),
        device_id_type=MESH,
    )
    info_copy.start()

    forward = []
    for turn, k, step in partners:
        copy = pltpu.make_async_remote_copy(
            src_ref=out_buf.at[k, step],
            dst_ref=in_buf.at[step, g],
            send_sem=fwd_send.at[turn, step],
            recv_sem=fwd_recv.at[turn, step],
            device_id=(k, lax.rem(d + step, doms)),
            device_id_type=MESH,
        )
        copy.start()
        forward.append(copy)
    in_buf[0, g] = out_buf[g, 0]

    for copy in loads[5:7]:
        copy.wait()
    halo = halo_smem[0, 0]
    state_rows = state.reshape((blocks + 1) * ROWS, LANES)
    for c in range(3):
        state_rows[pl.ds(c, blocks, stride=ROWS), :] = pos_ref[c]
        state_rows[pl.ds(3 + c, blocks, stride=ROWS), :] = vel_ref[c]
    rim[...] = state[halo]
    for copy in loads[7:]:
        copy.wait()
    goers = jnp.transpose(jnp.concatenate([chosen, jnp.zeros((LANES - places, blocks), jnp.float32)], 0))

    wide_iota = lax.broadcasted_iota(jnp.int32, (LANES, LANES), 1)
    for half in range(4 * blocks // LANES):
        rows = pl.ds(half * LANES, LANES)
        keys = jnp.transpose((slot_ref[rows, :] * LANES + wide_iota).astype(jnp.float32))
        keys = sort_rows([keys[r * ROWS : (r + 1) * ROWS, :] for r in range(16)], sub_iota)
        for r in range(16):
            sort_buf[half, pl.ds(r, ROWS, stride=16), :] = keys[r]
        inverse[rows, :] = jnp.transpose(sort_buf[half]).astype(jnp.int32) - wide_iota * LANES

    block_iota = lax.broadcasted_iota(jnp.int32, (blocks + 2 * ROWS, blocks), 0)
    hits = jnp.concatenate(
        [(block_iota == cb_ref[side : side + 1, :]).astype(jnp.float32) for side in range(2)], 1
    )
    hits = jnp.concatenate([hits, hits], 1).astype(BF16)
    factor = DT / mass_ref[...]
    pl.semaphore_wait(rim_ready, 1)
    rim_copy = pltpu.make_async_remote_copy(
        src_ref=rim,
        dst_ref=ghost_in,
        send_sem=rim_sems.at[0],
        recv_sem=rim_sems.at[1],
        device_id=(g, left),
        device_id_type=MESH,
    )
    rim_copy.start()

    info_copy.wait_recv()
    to_smem = pltpu.make_async_copy(info_in, info_smem, info_sems.at[2])
    to_smem.start()
    to_smem.wait()
    slot_iota = lax.broadcasted_iota(jnp.int32, (slots, tiles), 0)
    gain = PENALTY * info_in[2:3, 0:tiles].astype(jnp.float32)
    take_near = jnp.where(slot_iota == info_in[0:1, 0:tiles], gain, 0.0).astype(BF16)
    take_far = jnp.where(slot_iota == info_in[1:2, 0:tiles], -gain, 0.0).astype(BF16)
    tile_iota = lax.broadcasted_iota(jnp.int32, (tiles, 2 * LANES), 0)
    column = lax.broadcasted_iota(jnp.int32, (tiles, 2 * LANES), 1)
    same = ((column & (LANES - 1)) == tile_iota).astype(BF16)
    take_near = jnp.dot(take_near, same, preferred_element_type=jnp.float32).astype(BF16)
    tile_iota = lax.broadcasted_iota(jnp.int32, (tiles, tiles * ROWS), 0)
    column = lax.broadcasted_iota(jnp.int32, (tiles, tiles * ROWS), 1)
    same = (lax.div(column, ROWS) == tile_iota).astype(BF16)
    take_far = jnp.dot(take_far, same, preferred_element_type=jnp.float32)
    near_sums[...] = jnp.zeros_like(near_sums)
    depth = lax.broadcasted_iota(jnp.int32, (LANES, LANES), 0)
    depth = jnp.where(depth < 3 * slots, lax.rem(depth, slots), -1)

    def pick(t, carry):
        near_pick[t] = (depth == info_smem[0, t]).astype(jnp.float32).astype(BF16)
        return carry

    lax.fori_loop(0, tiles, pick, 0)

    for copy in forward:
        copy.wait_recv()
    held = (held_even, held_odd)
    canon_rows = canon.reshape(slots * ROWS, LANES)
    split = []
    for c in range(3):
        layers = []
        for layer in range(groups):
            rows = in_buf[0, layer, c] + in_buf[1, layer, c] + in_buf[2, layer, c]
            canon_rows[pl.ds(layer * ROWS * ROWS + c, ROWS, stride=ROWS), :] = rows
            layers.append(rows)
        value = jnp.concatenate(layers, 0)
        top = value.astype(BF16).astype(jnp.float32)
        rest = value - top
        middle = rest.astype(BF16).astype(jnp.float32)
        stack = jnp.concatenate([top, middle, rest - middle, jnp.zeros_like(value)], 0)
        split.append(jnp.transpose(stack).astype(BF16))
    split = jnp.concatenate(
        [split[c][16 * r : 16 * r + 16] for r in range(LANES // 16) for c in range(3)], 0
    )

    def lane_sums(step, held):
        for c in range(3):
            for r in range(LANES // ROWS):
                rows = pl.ds(c * LANES + r * ROWS, ROWS)
                value = near_sums[rows, :]
                for u in range(UNROLL):
                    total = jnp.sum(held[u, rows, :], 1, keepdims=True)
                    value = jnp.where(lane_iota == step * UNROLL + u, total, value)
                near_sums[rows, :] = value

    def pushes(step, held):
        for u in range(UNROLL):
            t = step * UNROLL + u
            far_block = canon[info_smem[1, t]]
            far = [jnp.broadcast_to(far_block[c : c + 1, :], (ROWS, LANES)) for c in range(3)]
            near = jnp.dot(split, near_pick[t], preferred_element_type=jnp.float32)
            far_sum = [None] * 3
            for r in range(LANES // ROWS):
                rows = [pl.ds(c * LANES + r * ROWS, ROWS) for c in range(3)]
                spots = [(r // 2 * 3 + c) * 16 + r % 2 * ROWS for c in range(3)]
                diff = [near[spots[c] : spots[c] + ROWS, :] - far[c] for c in range(3)]
                weight = jnp.maximum(REACH - inner_rows(diff, diff), 0.0)
                for c in range(3):
                    push = weight * diff[c]
                    held[u, rows[c], :] = push
                    far_sum[c] = far_sum[c] + push if r else push
            place = pl.ds(pl.multiple_of(t * ROWS, ROWS), ROWS)
            for c in range(3):
                far_sums[place, c * LANES : (c + 1) * LANES] = far_sum[c]

    def tile_steps(half, carry):
        for phase in range(2):
            step = half * 2 + phase
            lane_sums(step - 1, held[1 - phase])
            pushes(step, held[phase])
        return carry

    steps = tiles // UNROLL
    lax.fori_loop(0, steps // 2, tile_steps, 0)
    lane_sums(steps - 1, held[1])
    total = pick_rows(take_far, far_sums[...], 2)
    near_total = []
    for c in range(3):
        value = near_sums[pl.ds(c * LANES, LANES), :]
        top = value.astype(BF16)
        low = (value - top.astype(jnp.float32)).astype(BF16)
        near_total.append(
            lax.dot_general(
                take_near,
                jnp.concatenate([top, low], 1),
                (((1,), (1,)), ((), ())),
                preferred_element_type=jnp.float32,
            )
        )
    total = total + jnp.concatenate(near_total, 1)
    for c in range(3):
        ans[:, c, :, :] = total[:, c * LANES : (c + 1) * LANES].reshape(groups, ROWS, LANES)
    backward = []
    for turn, k, step in partners:
        copy = pltpu.make_async_remote_copy(
            src_ref=ans.at[k],
            dst_ref=ret.at[g, step],
            send_sem=back_send.at[turn, step],
            recv_sem=back_recv.at[turn, step],
            device_id=(k, lax.rem(d + doms - step, doms)),
            device_id_type=MESH,
        )
        copy.start()
        backward.append(copy)
    ret[g, 0] = ans[g]

    rim_copy.wait_recv()
    state[blocks] = ghost_in[...]

    def elements(part, carry):
        here = pl.ds(pl.multiple_of(part * ROWS, ROWS), ROWS)
        for side in range(2):
            for kk in range(ROWS):
                b = cb_smem[side, part * ROWS + kk]
                corner_buf[side, pl.ds(kk * ROWS, ROWS), :] = state[b]
        pos = [None] * 4
        vel = [None] * 4
        for side, pair in enumerate(((0, 3), (1, 2))):
            column = [corner_buf[side, pl.ds(x, ROWS, stride=ROWS), :] for x in range(6)]
            for c in pair:
                ids = slot_ref[pl.ds(part * ROWS * 4 + c, ROWS, stride=4), :]
                picked = [gather_lanes(value, ids) for value in column]
                pos[c] = picked[:3]
                vel[c] = picked[3:]
        old = [stress_ref[x, here, :] for x in range(3)]
        forces, new = shell_forces(pos, vel, old)
        for x in range(3):
            stress_out[x, here, :] = new[x]
            for side, pair in enumerate(((0, 3), (1, 2))):
                spread[side, x, here, :] = sum(
                    gather_lanes(forces[c][x], inverse[pl.ds(part * ROWS * 4 + c, ROWS, stride=4), :]) for c in pair
                )
        return carry

    lax.fori_loop(0, blocks // ROWS, elements, 0, unroll=4)

    both = jnp.concatenate(
        [
            jnp.concatenate([spread[side, c] for c in range(3)], 1)
            for side in range(2)
        ],
        0,
    )
    both = pieces(both, 2)
    shared = jnp.dot(
        hits[blocks : blocks + 2 * ROWS], both, preferred_element_type=jnp.float32
    )
    for c in range(3):
        push_out[pl.ds(c, 1), :] = shared[0:1, c * LANES : (c + 1) * LANES]
    push_copy = pltpu.make_async_remote_copy(
        src_ref=push_out,
        dst_ref=push_in,
        send_sem=push_sems.at[0],
        recv_sem=push_sems.at[1],
        device_id=(g, right),
        device_id_type=MESH,
    )
    push_copy.start()
    internal = jnp.dot(hits[0:blocks], both, preferred_element_type=jnp.float32)

    for copy in backward:
        copy.wait_recv()
    answers = jnp.concatenate(
        [ret[:, :, c, :, :].reshape(places, LANES) for c in range(3)], 1
    )
    answers = jnp.concatenate([answers, jnp.zeros((LANES - places, 3 * LANES), jnp.float32)], 0)
    contact = pick_rows(goers, answers, 2)
    push_copy.wait_recv()
    is_rim = lax.broadcasted_iota(jnp.int32, (blocks, LANES), 0) == halo
    for c in range(3):
        extra = jnp.where(is_rim, push_in[pl.ds(c, 1), :], 0.0)
        cols = slice(c * LANES, (c + 1) * LANES)
        force = contact[:, cols] - internal[:, cols] - extra
        vel_out[c] = vel_ref[c] + factor * force
    rim_copy.wait_send()
    info_copy.wait_send()
    push_copy.wait_send()
    for copy in forward:
        copy.wait_send()
    for copy in backward:
        copy.wait_send()


def local(
    positions,
    velocity,
    mass,
    stress,
    corner_block,
    corner_slot,
    halo_block,
    contact_owner,
    contact_slot,
    tile_pairs,
    tile_active,
):
    groups = lax.axis_size("group")
    doms = lax.axis_size("dom")
    blocks = corner_block.shape[2]
    nodes = positions.shape[2]
    tiles = tile_pairs.shape[2]
    slots = groups * ROWS
    vmem = pl.BlockSpec(memory_space=pltpu.VMEM)
    i32 = jnp.int32
    f32 = jnp.float32
    out = pl.pallas_call(
        functools.partial(kernel, groups, doms),
        out_shape=[jax.ShapeDtypeStruct((3, blocks, LANES), f32)] * 2,
        in_specs=[pl.BlockSpec(memory_space=pltpu.HBM)] * 11,
        out_specs=[vmem] * 2,
        scratch_shapes=[
            pltpu.VMEM((3, blocks, LANES), f32),
            pltpu.VMEM((3, blocks, LANES), f32),
            pltpu.VMEM((blocks, LANES), f32),
            pltpu.VMEM((3, blocks, LANES), f32),
            pltpu.VMEM((4 * blocks, LANES), i32),
            pltpu.VMEM((4, blocks), i32),
            pltpu.VMEM((1, blocks), i32),
            pltpu.VMEM((1, blocks), i32),
            pltpu.VMEM((2, tiles), i32),
            pltpu.VMEM((1, tiles), i32),
            pltpu.SMEM((4, blocks), i32),
            pltpu.SMEM((ROWS, LANES), i32),
            pltpu.VMEM((ROWS, LANES), i32),
            pltpu.VMEM((ROWS, LANES), i32),
            pltpu.SemaphoreType.DMA((3,)),
            pltpu.SemaphoreType.REGULAR,
            pltpu.SMEM((1, 1), i32),
            pltpu.SemaphoreType.DMA((12,)),
            pltpu.VMEM((blocks + 1, ROWS, LANES), f32),
            pltpu.VMEM((ROWS, LANES), f32),
            pltpu.VMEM((ROWS, LANES), f32),
            pltpu.VMEM((groups, 3, 3, ROWS, LANES), f32),
            pltpu.VMEM((3, groups, 3, ROWS, LANES), f32),
            pltpu.VMEM((groups, 3, ROWS, LANES), f32),
            pltpu.VMEM((groups, 3, 3, ROWS, LANES), f32),
            pltpu.VMEM((slots, ROWS, LANES), f32),
            pltpu.VMEM((tiles + UNROLL, LANES, LANES), jnp.bfloat16),
            pltpu.VMEM((UNROLL, 3 * LANES, LANES), f32),
            pltpu.VMEM((UNROLL, 3 * LANES, LANES), f32),
            pltpu.VMEM((3 * LANES, LANES), f32),
            pltpu.VMEM((tiles * ROWS, 3 * LANES), f32),
            pltpu.VMEM((4 * blocks, LANES), jnp.int32),
            pltpu.VMEM((4 * blocks // LANES, LANES, LANES), f32),
            pltpu.VMEM((2, ROWS * ROWS, LANES), f32),
            pltpu.VMEM((2, 3, blocks, LANES), f32),
            pltpu.VMEM((ROWS, LANES), f32),
            pltpu.VMEM((ROWS, LANES), f32),
            pltpu.SemaphoreType.DMA((groups, 3)),
            pltpu.SemaphoreType.DMA((groups, 3)),
            pltpu.SemaphoreType.DMA((groups, 3)),
            pltpu.SemaphoreType.DMA((groups, 3)),
            pltpu.SemaphoreType.DMA((2,)),
            pltpu.SemaphoreType.DMA((2,)),
        ],
        compiler_params=pltpu.CompilerParams(
            collective_id=0, has_side_effects=True, vmem_limit_bytes=32 * 1024 * 1024
        ),
        name="shell_step",
    )(
        pltpu.with_memory_space_constraint(positions.reshape(3, blocks, LANES), pltpu.HBM),
        pltpu.with_memory_space_constraint(velocity.reshape(3, blocks, LANES), pltpu.HBM),
        pltpu.with_memory_space_constraint(mass.reshape(blocks, LANES), pltpu.HBM),
        pltpu.with_memory_space_constraint(stress.reshape(3, blocks, LANES), pltpu.HBM),
        pltpu.with_memory_space_constraint(corner_slot.reshape(4, blocks, LANES).transpose(1, 0, 2).reshape(4 * blocks, LANES), pltpu.HBM),
        pltpu.with_memory_space_constraint(corner_block.reshape(4, blocks), pltpu.HBM),
        pltpu.with_memory_space_constraint(contact_owner, pltpu.HBM),
        pltpu.with_memory_space_constraint(contact_slot, pltpu.HBM),
        pltpu.with_memory_space_constraint(tile_pairs.reshape(2, tiles), pltpu.HBM),
        pltpu.with_memory_space_constraint(tile_active, pltpu.HBM),
        halo_block,
    )
    return out[0].reshape(1, 3, nodes), out[1].reshape(1, 3, nodes)


def solution(mesh):
    in_specs = (
        P("group", None, "dom"),
        P("group", None, "dom"),
        P("group", "dom"),
        P("group", None, "dom"),
        P("group", None, "dom"),
        P("group", None, "dom"),
        P("group", "dom"),
        P("group", "dom"),
        P("group", "dom"),
        P("group", None, "dom"),
        P("group", "dom"),
    )
    out_specs = (P("group", None, "dom"), P("group", None, "dom"))
    return jax.shard_map(local, mesh=mesh, in_specs=in_specs, out_specs=out_specs, check_vma=False)
```
